128 devices in a mesh: ha: 8 (over z_lo, y), ta: 16 (over x, z_hi, core).
Axes of the slice: x: 4, y: 4, z: 4 (z_hi: 2, z_lo: 2; z = z_hi * 2 + z_lo), core: 2. Of those that a mesh axis runs over, the one named last changes fastest.
Arguments:
- latent: bfloat16 [32, 128, 48, 384], P(None, ('ha', 'ta')), may hold values from -54 to 54
- group_start: int32 [16], replicated, may hold values from 0 to 30, as said below
- norm_gain: float32 [384], replicated, may hold values from 0.1 to 1.9
- conv_weight: bfloat16 [3, 3, 3, 384, 384], replicated, may hold values from -0.0625 to 0.0625
- conv_bias: float32 [384], replicated, may hold values from -3 to 3
Outputs:
- tiles: bfloat16 [64, 128, 48, 384], P('ta', 'ha')
The draws below stay inside these ranges and needn't reach their ends.
Inputs may be any that keep to these rules, and one draw needn't show every extreme that they name: group_start rises from 0; every group holds 1 to 4 frames and the last ends at 32; the first and the last group hold 2 frames, the second and the second-to-last one frame each, and some group holds exactly 4.
All inputs are finite; a program needn't handle non-finite values.
Results may differ from the reference program's by a relative error of at most 0.0021.
Values may be sent and summed in bfloat16 or wider, within the bound.
No kernel may reach another device: no remote copies, remote signals or barrier semaphores. Data moves between devices by JAX's collectives and lax.ppermute only.
A program may use at most 192 MiB of HBM per device.

```python
import math
import jax
import jax.numpy as jnp
from jax import lax

C = 384
W = 48
FR_DEV = 2
FMAX = 4
FRAMES = 32
SLOTS = 64
H = 128
N_TA = 16


def draw_latent(key, part):
    key = jax.random.fold_in(key, 11)
    key_rows, key_chans, key_base = jax.random.split(key, 3)
    row_scale = jnp.exp(jax.random.uniform(key_rows, (FRAMES, H, W, 1), jnp.float32, math.log(0.3), math.log(3.0)))
    chan_scale = jnp.exp(jax.random.uniform(key_chans, (C,), jnp.float32, math.log(0.3), math.log(3.0)))
    base = jax.random.truncated_normal(key_base, -6.0, 6.0, (FRAMES, H, W, C), jnp.float32)
    return (base * row_scale * chan_scale).astype(jnp.bfloat16)


def draw_group_start(key, part):
    key = jax.random.fold_in(key, 7)
    key_perm, key_delta = jax.random.split(key)
    inner = (jax.random.permutation(key_perm, N_TA - 4) + 2).astype(jnp.int32)
    lengths = jnp.full((N_TA,), FR_DEV, jnp.int32)
    lengths = lengths.at[1].set(1)
    lengths = lengths.at[N_TA - 2].set(1)
    lengths = lengths.at[inner[0]].set(2 * FR_DEV)
    pair_count = (N_TA - 5) // 2
    deltas = jax.random.randint(key_delta, (pair_count,), -(FR_DEV - 1), FR_DEV).astype(jnp.int32)
    lengths = lengths.at[inner[1:1 + 2 * pair_count:2]].add(deltas)
    lengths = lengths.at[inner[2:2 + 2 * pair_count:2]].add(-deltas)
    return (jnp.cumsum(lengths) - lengths).astype(jnp.int32)


def bell_draw(stream_key, dims, scale, bound, kind=jnp.bfloat16):
    return jnp.clip(scale * jax.random.normal(stream_key, dims, jnp.float32), -bound, bound).astype(kind)


def setup_inputs(seed: int = 0) -> dict:
    seeds = jax.random.split(jax.random.key(seed), 6)
    return {
        "latent": draw_latent(jax.random.fold_in(seeds[5], 71), 0),
        "group_start": draw_group_start(jax.random.fold_in(seeds[5], 71), 0),
        "norm_gain": jnp.clip(1.0 + 0.18 * jax.random.normal(seeds[2], (C,), jnp.float32), 0.1, 1.9),
        "conv_weight": bell_draw(seeds[3], (3, 3, 3, C, C), (27 * C) ** -0.5, 0.0625),
        "conv_bias": bell_draw(seeds[4], (C,), 0.5, 3.0, jnp.float32),
    }


def activate(values, norm_gain):
    widened = values.astype(jnp.float32)
    scaled = widened * lax.rsqrt(lax.optimization_barrier(jnp.mean(widened * widened, axis=-1, keepdims=True)) + 1e-06) * norm_gain
    return jax.nn.silu(scaled).astype(jnp.bfloat16)

def reference(latent, group_start, norm_gain, conv_weight, conv_bias):
    activated = activate(latent, norm_gain)
    padded = jnp.pad(activated, ((2, 0), (1, 1), (1, 1), (0, 0)))

    def one_frame(frame_id):
        window = lax.dynamic_slice_in_dim(padded, frame_id, 3, 0)
        running = jnp.zeros((H * W, C), jnp.float32)
        for time_tap in range(3):
            for row_tap in range(3):
                for col_tap in range(3):
                    tapped = window[time_tap, row_tap:row_tap + H, col_tap:col_tap + W].reshape(H * W, C)
                    running = running + jnp.dot(tapped, conv_weight[time_tap, row_tap, col_tap], preferred_element_type=jnp.float32)
        return running.reshape(H, W, C)
    convolved = lax.map(one_frame, jnp.arange(FRAMES, dtype=jnp.int32))
    summed = (latent.astype(jnp.float32) + convolved + conv_bias).astype(jnp.bfloat16)
    lengths = jnp.concatenate([group_start[1:], jnp.array([FRAMES], jnp.int32)]) - group_start
    slot_ids = jnp.arange(SLOTS, dtype=jnp.int32)
    owners = slot_ids // FMAX
    offset = slot_ids % FMAX
    source = group_start[owners] + offset
    usable = offset < lengths[owners]
    picked = jnp.take(summed, jnp.minimum(source, FRAMES - 1).astype(jnp.int32), axis=0)
    return jnp.where(usable[:, None, None, None], picked, jnp.zeros_like(picked))
```

```python
import functools

import jax
import jax.numpy as jnp
from jax import lax
from jax.experimental import pallas as pl
from jax.experimental.pallas import tpu as pltpu
from jax.sharding import Mesh, PartitionSpec as P

FMAX = 4
HIST = 2
SPAN = FMAX + HIST


def activate(raw, gain):
    wide = raw.astype(jnp.float32)
    power = jnp.mean(wide * wide, axis=-1, keepdims=True)
    scaled = wide * lax.rsqrt(power + 1e-06) * gain
    return (scaled / (1.0 + jnp.exp(-scaled))).astype(jnp.bfloat16)


def pack_kernel(bases, frames, packed, sems):
    chips, window = packed.shape[:2]
    copies = [
        pltpu.make_async_copy(frames.at[pl.ds(bases[c], window)], packed.at[c], sems.at[c])
        for c in range(chips)
    ]
    for copy in copies:
        copy.start()
    for copy in copies:
        copy.wait()


def pack(frames, bases, window):
    chips = bases.shape[0]
    return pl.pallas_call(
        pack_kernel,
        out_shape=jax.ShapeDtypeStruct((chips, window) + frames.shape[1:], frames.dtype),
        in_specs=[
            pl.BlockSpec(memory_space=pltpu.SMEM),
            pl.BlockSpec(memory_space=pl.ANY),
        ],
        out_specs=pl.BlockSpec(memory_space=pl.ANY),
        scratch_shapes=[pltpu.SemaphoreType.DMA((chips,))],
    )(bases, frames)


def conv_kernel(
    plan, own, other, own_rim, other_rim, weight, gain, bias, out,
    taps, raw, act, sums, result, weight_sems, frame_sems, out_sems,
):
    pairs = own.shape[0]
    rows, cols, chans = 2 * pairs, own.shape[2], own.shape[3]
    length, skip, base, core, history = (plan[i] for i in range(5))

    def arrivals(i):
        index = jnp.clip(i + skip, 0, SPAN - 1)
        return [
            pltpu.make_async_copy(
                own.at[:, base + index], raw.at[i, pl.ds(core, pairs), 1 - core], frame_sems.at[i, 0]
            ),
            pltpu.make_async_copy(
                other.at[:, index], raw.at[i, pl.ds(1 - core, pairs), core], frame_sems.at[i, 1]
            ),
            pltpu.make_async_copy(
                own_rim.at[base + index], raw.at[i, pairs * (1 - core), 1 - core], frame_sems.at[i, 2]
            ),
            pltpu.make_async_copy(
                other_rim.at[index], raw.at[i, pairs * core, core], frame_sems.at[i, 3]
            ),
        ]

    incoming = [arrivals(i) for i in range(SPAN)]
    for copies in incoming:
        for copy in copies:
            copy.start()
    tap_copies = []
    for a in range(3):
        for b in range(3):
            for e in range(3):
                tap_copies.append(
                    pltpu.make_async_copy(
                        weight.at[a, b, e],
                        taps.at[pl.ds((3 * a + b) * chans, chans), pl.ds(e * chans, chans)],
                        weight_sems.at[9 * a + 3 * b + e],
                    )
                )
    for copy in tap_copies:
        copy.start()

    sums[0, :, 7:8, :] = jnp.zeros((rows, 1, chans), jnp.float32)
    sums[2, :, cols + 8 : cols + 9, :] = jnp.zeros((rows, 1, chans), jnp.float32)

    def activated(i):
        return activate(raw[i].reshape(rows + 2, cols, chans), gain[...])

    for i in range(3):
        for copy in incoming[i]:
            copy.wait()
    act[2] = activated(2)

    @pl.when(history > 0)
    def _():
        act[0] = activated(0)
        act[1] = activated(1)

    @pl.when(history == 0)
    def _():
        act[0] = jnp.zeros(act.shape[1:], act.dtype)
        act[1] = jnp.zeros(act.shape[1:], act.dtype)

    for i in range(3, SPAN):
        for copy in incoming[i]:
            copy.wait()
    for copy in tap_copies:
        copy.wait()

    def one_frame(k, carry):
        lhs = jnp.concatenate(
            [
                act[k + a, pl.ds(b, rows)].reshape(rows * cols, chans)
                for a in range(3)
                for b in range(3)
            ],
            axis=1,
        )
        for e in range(3):
            part = jnp.dot(
                lhs, taps[:, pl.ds(e * chans, chans)], preferred_element_type=jnp.float32
            )
            sums[e, :, 8 : cols + 8, :] = part.reshape(rows, cols, chans)
        later = jnp.minimum(k + 3, SPAN - 1)
        act[later] = activated(later)
        convolved = (
            sums[0, :, 7 : cols + 7, :] + sums[1, :, 8 : cols + 8, :] + sums[2, :, 9 : cols + 9, :]
        )
        latent = raw[k + 2].reshape(rows + 2, cols, chans)[1 : rows + 1].astype(jnp.float32)
        result[k] = (latent + convolved + bias[...]).astype(result.dtype)
        pltpu.make_async_copy(result.at[k], out.at[k], out_sems.at[k]).start()
        return carry

    lax.fori_loop(0, length, one_frame, 0)

    def blank_frame(k, carry):
        result[k] = jnp.zeros(result.shape[1:], result.dtype)
        pltpu.make_async_copy(result.at[k], out.at[k], out_sems.at[k]).start()
        return carry

    lax.fori_loop(length, FMAX, blank_frame, 0)
    for k in range(FMAX):
        pltpu.make_async_copy(result.at[k], out.at[k], out_sems.at[k]).wait()


def conv(plan, own, other, own_rim, other_rim, weight, gain, bias):
    pairs, _, cols, chans = own.shape
    rows = 2 * pairs
    hbm = pl.BlockSpec(memory_space=pl.ANY)
    vmem = pl.BlockSpec(memory_space=pltpu.VMEM)
    return pl.pallas_call(
        conv_kernel,
        out_shape=jax.ShapeDtypeStruct((FMAX, rows, cols, chans), own.dtype),
        in_specs=[pl.BlockSpec(memory_space=pltpu.SMEM)] + [hbm] * 5 + [vmem] * 2,
        out_specs=hbm,
        scratch_shapes=[
            pltpu.VMEM((9 * chans, 3 * chans), jnp.bfloat16),
            pltpu.VMEM((SPAN, pairs + 1, 2, cols, chans), jnp.bfloat16),
            pltpu.VMEM((SPAN, rows + 2, cols, chans), jnp.bfloat16),
            pltpu.VMEM((3, rows, cols + 16, chans), jnp.float32),
            pltpu.VMEM((FMAX, rows, cols, chans), jnp.bfloat16),
            pltpu.SemaphoreType.DMA((27,)),
            pltpu.SemaphoreType.DMA((SPAN, 4)),
            pltpu.SemaphoreType.DMA((FMAX,)),
        ],
        compiler_params=pltpu.CompilerParams(vmem_limit_bytes=56 * 2**20),
    )(plan, own, other, own_rim, other_rim, weight, gain.reshape(1, chans), bias.reshape(1, chans))


def on_device(window, latent, group_start, norm_gain, conv_weight, conv_bias):
    frame_total = latent.shape[0]
    ends = jnp.concatenate([group_start[1:], jnp.array([frame_total], jnp.int32)])
    lengths = ends - group_start
    cores = lax.axis_size("core")
    stripes = lax.axis_size("ha")
    core = lax.axis_index("core")
    chip = lax.axis_index("tc")
    bases = jnp.clip(group_start[::cores] - HIST, 0, frame_total - window)
    packed = pack(latent[:, 0], bases, window)
    arrived = lax.all_to_all(packed, "tc", split_axis=0, concat_axis=0, tiled=True)

    rim = jnp.where(core == 0, arrived[0], arrived[-1])
    pairs = [((h + 1) * cores, h * cores) for h in range(stripes - 1)]
    pairs += [(h * cores + 1, (h + 1) * cores + 1) for h in range(stripes - 1)]
    own_rim = lax.ppermute(rim, ("ha", "core"), pairs)

    offsets = lax.dynamic_slice_in_dim(group_start, chip * cores, cores) - HIST - bases[chip]
    firsts = jnp.clip(offsets, 0, window - SPAN)
    swap = [(0, 1), (1, 0)]
    other = lax.ppermute(
        lax.dynamic_slice_in_dim(arrived, firsts[1 - core], SPAN, 1), "core", swap
    )
    other_rim = lax.ppermute(
        lax.dynamic_slice_in_dim(own_rim, firsts[1 - core], SPAN, 0), "core", swap
    )
    group = chip * cores + core
    plan = jnp.stack(
        [
            lengths[group],
            offsets[core] - firsts[core],
            firsts[core],
            core,
            group,
        ]
    ).astype(jnp.int32)
    return conv(plan, arrived, other, own_rim, other_rim, conv_weight, norm_gain, conv_bias)


def solution(mesh):
    devices = mesh.devices
    fine = Mesh(
        devices.reshape(devices.shape[0], devices.shape[1] // 2, 2), ("ha", "tc", "core")
    )
    placed = (P(None, ("ha", "tc", "core"), None, None), P(), P(), P(), P())
    return jax.shard_map(
        functools.partial(on_device, 2 * FMAX + HIST),
        mesh=fine,
        in_specs=placed,
        out_specs=P(("tc", "core"), "ha", None, None),
        check_vma=False,
    )
```

```python
import functools

import jax
import jax.numpy as jnp
from jax import lax
from jax.experimental import pallas as pl
from jax.experimental.pallas import tpu as pltpu
from jax.sharding import Mesh, PartitionSpec as P

FMAX = 4
HIST = 2
SPAN = FMAX + HIST
VMEM_BYTES = 56 * 2**20


def activate(raw, gain):
    wide = raw.astype(jnp.float32)
    power = jnp.mean(wide * wide, axis=-1, keepdims=True)
    half = wide * lax.rsqrt(power + 1e-06) * (0.5 * gain)
    return (half + half * jnp.tanh(half)).astype(jnp.bfloat16)


def first_held(starts, group, odd, groups, total, slots):
    after = jnp.where(group + 1 < groups, starts[jnp.minimum(group + 1, groups - 1)], total)
    wanted = jnp.where(odd, after - slots, starts[group] - HIST)
    return jnp.clip(wanted, 0, total - slots)


def pack_kernel(starts, frames, packed, sems):
    groups, slots = packed.shape[:2]
    total = frames.shape[0]
    copies = []
    for group in range(groups):
        first = first_held(starts, group, group % 2 == 1, groups, total, slots)
        copies.append(
            pltpu.make_async_copy(frames.at[pl.ds(first, slots)], packed.at[group], sems.at[group])
        )
    for copy in copies:
        copy.start()
    for copy in copies:
        copy.wait()


def pack(starts, frames, slots):
    groups = starts.shape[0]
    return pl.pallas_call(
        pack_kernel,
        out_shape=jax.ShapeDtypeStruct((groups, slots) + frames.shape[1:], frames.dtype),
        in_specs=[
            pl.BlockSpec(memory_space=pltpu.SMEM),
            pl.BlockSpec(memory_space=pltpu.VMEM),
        ],
        out_specs=pl.BlockSpec(memory_space=pl.ANY),
        scratch_shapes=[pltpu.SemaphoreType.DMA((groups,))],
    )(starts, frames)


def tap_copies(weight, taps, sems):
    chans = weight.shape[-1]
    return [
        pltpu.make_async_copy(
            weight.at[a, b, e],
            taps.at[pl.ds((3 * a + b) * chans, chans), pl.ds(e * chans, chans)],
            sems.at[9 * a + 3 * b + e],
        )
        for a in range(3)
        for b in range(3)
        for e in range(3)
    ]


def place(starts, total, slots):
    groups = starts.shape[0]
    group = lax.axis_index("tc") * 2 + lax.axis_index("core")
    odd = lax.axis_index("core") == 1
    held = first_held(starts, group, odd, groups, total, slots)
    after = jnp.where(group + 1 < groups, starts[jnp.minimum(group + 1, groups - 1)], total)
    extra = jnp.where(odd, held - (SPAN - slots), held + slots)
    return group, starts[group], after - starts[group], held, extra


def locate(i, start, held, extra, slots):
    frame = start - HIST + i
    slot = frame - held
    inside = jnp.logical_and(slot >= 0, slot < slots)
    inside = jnp.logical_or(inside, frame < 0)
    return inside, jnp.clip(slot, 0, slots - 1), jnp.clip(frame - extra, 0, SPAN - slots - 1)


def column_sums(sums, cols):
    return (
        sums[0, :, 7 : cols + 7, :] + sums[1, :, 8 : cols + 8, :] + sums[2, :, 9 : cols + 9, :]
    )


def clear_sides(sums, cols):
    shape = (sums.shape[1], 1, sums.shape[3])
    sums[0, :, 7:8, :] = jnp.zeros(shape, jnp.float32)
    sums[2, :, cols + 8 : cols + 9, :] = jnp.zeros(shape, jnp.float32)


def inner_kernel(
    total, starts, own, other, weight, gain, bias, out,
    taps, raw, act, sums, result, weight_sems, frame_sems, out_sems,
):
    rows, slots, cols, chans = own.shape
    inner = rows - 2
    group, start, length, held, extra = place(starts, total, slots)
    weights = tap_copies(weight, taps, weight_sems)
    for i in range(SPAN):
        inside, slot, spare = locate(i, start, held, extra, slots)

        @pl.when(inside)
        def _():
            pltpu.make_async_copy(own.at[:, slot], raw.at[i], frame_sems.at[i]).start()

        @pl.when(jnp.logical_not(inside))
        def _():
            pltpu.make_async_copy(other.at[:, spare], raw.at[i], frame_sems.at[i]).start()

        if i == 2:
            for copy in weights:
                copy.start()

    def arrived(i):
        pltpu.make_async_copy(own.at[:, 0], raw.at[i], frame_sems.at[i]).wait()

    clear_sides(sums, cols)

    for i in range(3):
        arrived(i)
    act[2] = activate(raw[2], gain[...])

    @pl.when(group > 0)
    def _():
        act[0] = activate(raw[0], gain[...])
        act[1] = activate(raw[1], gain[...])

    @pl.when(group == 0)
    def _():
        act[0] = jnp.zeros(act.shape[1:], act.dtype)
        act[1] = jnp.zeros(act.shape[1:], act.dtype)

    for i in range(3, SPAN):
        arrived(i)
    for copy in weights:
        copy.wait()

    def one_frame(k, carry):
        lhs = jnp.concatenate(
            [
                act[k + a, pl.ds(b, inner)].reshape(inner * cols, chans)
                for a in range(3)
                for b in range(3)
            ],
            axis=1,
        )
        part = jnp.dot(lhs, taps[...], preferred_element_type=jnp.float32)
        for e in range(3):
            sums[e, :, 8 : cols + 8, :] = part[:, e * chans : (e + 1) * chans].reshape(
                inner, cols, chans
            )
        later = jnp.minimum(k + 3, SPAN - 1)
        act[later] = activate(raw[later], gain[...])
        latent = raw[k + HIST, pl.ds(1, inner)].astype(jnp.float32)
        result[k, pl.ds(1, inner)] = (latent + column_sums(sums, cols) + bias[...]).astype(
            result.dtype
        )
        pltpu.make_async_copy(result.at[k], out.at[k], out_sems.at[k]).start()
        return carry

    def blank_frame(k, carry):
        result[k] = jnp.zeros(result.shape[1:], result.dtype)
        pltpu.make_async_copy(result.at[k], out.at[k], out_sems.at[k]).start()
        return carry

    lax.fori_loop(length, FMAX, blank_frame, 0)
    lax.fori_loop(0, length, one_frame, 0)
    for k in range(FMAX):
        pltpu.make_async_copy(result.at[k], out.at[k], out_sems.at[k]).wait()


def edge_kernel(
    total, starts, own, other, above, below, weight, gain, bias, partial, out,
    taps, raw, act, sums, result, weight_sems, frame_sems, out_sems,
):
    del partial
    rows, slots, cols, chans = own.shape
    group, start, length, held, extra = place(starts, total, slots)
    weights = tap_copies(weight, taps, weight_sems)

    def copies(i, source, index, rim):
        return [
            pltpu.make_async_copy(above.at[rim], raw.at[i, 0, 0], frame_sems.at[i, 0]),
            pltpu.make_async_copy(
                source.at[pl.ds(0, 2), index], raw.at[i, 0, pl.ds(1, 2)], frame_sems.at[i, 1]
            ),
            pltpu.make_async_copy(
                source.at[pl.ds(rows - 2, 2), index], raw.at[i, 1, pl.ds(0, 2)], frame_sems.at[i, 2]
            ),
            pltpu.make_async_copy(below.at[rim], raw.at[i, 1, 2], frame_sems.at[i, 3]),
        ]

    for i in range(SPAN):
        inside, slot, spare = locate(i, start, held, extra, slots)

        @pl.when(inside)
        def _():
            for copy in copies(i, own, slot, slot):
                copy.start()

        @pl.when(jnp.logical_not(inside))
        def _():
            for copy in copies(i, other, spare, slots + spare):
                copy.start()

    for copy in weights:
        copy.start()
    clear_sides(sums, cols)
    for i in range(SPAN):
        for copy in copies(i, own, 0, 0):
            copy.wait()
        act[i] = activate(raw[i], gain[...])

    @pl.when(group == 0)
    def _():
        for i in range(HIST):
            act[i] = jnp.zeros(act.shape[1:], act.dtype)

    for copy in weights:
        copy.wait()
    lhs = jnp.concatenate(
        [
            act[a : a + FMAX, :, b].reshape(FMAX * 2 * cols, chans)
            for a in range(3)
            for b in range(3)
        ],
        axis=1,
    )
    part = jnp.dot(lhs, taps[...], preferred_element_type=jnp.float32)
    for e in range(3):
        sums[e, :, 8 : cols + 8, :] = part[:, e * chans : (e + 1) * chans].reshape(
            FMAX * 2, cols, chans
        )
    convolved = column_sums(sums, cols).reshape(FMAX, 2, cols, chans)
    for k in range(FMAX):
        for side in range(2):
            latent = raw[k + HIST, side, 1].astype(jnp.float32)
            total_sum = (latent + convolved[k, side] + bias[...]).astype(result.dtype)
            result[k, side] = jnp.where(k < length, total_sum, jnp.zeros_like(total_sum))
    finished = [
        pltpu.make_async_copy(
            result.at[k, side], out.at[k, side * (rows - 1)], out_sems.at[k, side]
        )
        for k in range(FMAX)
        for side in range(2)
    ]
    for copy in finished:
        copy.start()
    for copy in finished:
        copy.wait()


def inner_rows(total, starts, own, other, weight, gain, bias):
    rows, _, cols, chans = own.shape
    hbm = pl.BlockSpec(memory_space=pl.ANY)
    vmem = pl.BlockSpec(memory_space=pltpu.VMEM)
    return pl.pallas_call(
        functools.partial(inner_kernel, total),
        out_shape=jax.ShapeDtypeStruct((FMAX, rows, cols, chans), own.dtype),
        in_specs=[pl.BlockSpec(memory_space=pltpu.SMEM)] + [hbm] * 3 + [vmem] * 2,
        out_specs=hbm,
        scratch_shapes=[
            pltpu.VMEM((9 * chans, 3 * chans), jnp.bfloat16),
            pltpu.VMEM((SPAN, rows, cols, chans), jnp.bfloat16),
            pltpu.VMEM((SPAN, rows, cols, chans), jnp.bfloat16),
            pltpu.VMEM((3, rows - 2, cols + 16, chans), jnp.float32),
            pltpu.VMEM((FMAX, rows, cols, chans), jnp.bfloat16),
            pltpu.SemaphoreType.DMA((27,)),
            pltpu.SemaphoreType.DMA((SPAN,)),
            pltpu.SemaphoreType.DMA((FMAX,)),
        ],
        compiler_params=pltpu.CompilerParams(vmem_limit_bytes=VMEM_BYTES),
    )(starts, own, other, weight, gain, bias)


def edge_rows(total, starts, own, other, above, below, weight, gain, bias, partial):
    rows, _, cols, chans = own.shape
    hbm = pl.BlockSpec(memory_space=pl.ANY)
    vmem = pl.BlockSpec(memory_space=pltpu.VMEM)
    return pl.pallas_call(
        functools.partial(edge_kernel, total),
        out_shape=jax.ShapeDtypeStruct(partial.shape, partial.dtype),
        in_specs=[pl.BlockSpec(memory_space=pltpu.SMEM)] + [hbm] * 5 + [vmem] * 2 + [hbm],
        out_specs=hbm,
        scratch_shapes=[
            pltpu.VMEM((9 * chans, 3 * chans), jnp.bfloat16),
            pltpu.VMEM((SPAN, 2, 3, cols, chans), jnp.bfloat16),
            pltpu.VMEM((SPAN, 2, 3, cols, chans), jnp.bfloat16),
            pltpu.VMEM((3, 2 * FMAX, cols + 16, chans), jnp.float32),
            pltpu.VMEM((FMAX, 2, cols, chans), jnp.bfloat16),
            pltpu.SemaphoreType.DMA((27,)),
            pltpu.SemaphoreType.DMA((SPAN, 4)),
            pltpu.SemaphoreType.DMA((FMAX, 2)),
        ],
        input_output_aliases={8: 0},
        compiler_params=pltpu.CompilerParams(vmem_limit_bytes=VMEM_BYTES),
    )(starts, own, other, above, below, weight, gain, bias, partial)


def on_device(slots, latent, group_start, norm_gain, conv_weight, conv_bias):
    total = latent.shape[0]
    groups = group_start.shape[0]
    missing = SPAN - slots
    stripes = lax.axis_size("ha")
    core = lax.axis_index("core")
    chip = lax.axis_index("tc")
    gain = norm_gain.reshape(1, -1)
    bias = conv_bias.reshape(1, -1)
    packed = pack(group_start, latent[:, 0], slots)
    own = lax.all_to_all(packed, ("tc", "core"), split_axis=0, concat_axis=0, tiled=True)

    front = first_held(group_start, 2 * chip, False, groups, total, slots)
    back = first_held(group_start, 2 * chip + 1, True, groups, total, slots)
    wanted = jnp.where(core == 0, back - missing - front, front + slots - back)
    sent = lax.dynamic_slice_in_dim(own, jnp.clip(wanted, 0, slots - missing), missing, 1)
    other = lax.ppermute(sent, "core", [(0, 1), (1, 0)])

    up = [(h, h + 1) for h in range(stripes - 1)]
    down = [(h + 1, h) for h in range(stripes - 1)]
    above = lax.ppermute(jnp.concatenate([own[-1], other[-1]], axis=0), "ha", up)
    below = lax.ppermute(jnp.concatenate([own[0], other[0]], axis=0), "ha", down)
    partial = inner_rows(total, group_start, own, other, conv_weight, gain, bias)
    return edge_rows(
        total, group_start, own, other, above, below, conv_weight, gain, bias, partial
    )


def solution(mesh):
    devices = mesh.devices
    fine = Mesh(
        devices.reshape(devices.shape[0], devices.shape[1] // 2, 2), ("ha", "tc", "core")
    )
    placed = (P(None, ("ha", "tc", "core"), None, None), P(), P(), P(), P())
    return jax.shard_map(
        functools.partial(on_device, 5),
        mesh=fine,
        in_specs=placed,
        out_specs=P(("tc", "core"), "ha", None, None),
        check_vma=False,
    )
```

```python
import functools

import jax
import jax.numpy as jnp
from jax import lax
from jax.experimental import pallas as pl
from jax.experimental.pallas import tpu as pltpu
from jax.sharding import Mesh, PartitionSpec as P

FMAX = 4
HIST = 2
SPAN = FMAX + HIST
VMEM_BYTES = 30 * 2**20


def activate(raw, gain):
    wide = raw.astype(jnp.float32)
    power = jnp.mean(wide * wide, axis=-1, keepdims=True)
    half = wide * lax.rsqrt(power + 1e-06) * (0.5 * gain)
    return (half + half * jnp.tanh(half)).astype(jnp.bfloat16)


def first_held(starts, group, odd, groups, total, slots):
    after = jnp.where(group + 1 < groups, starts[jnp.minimum(group + 1, groups - 1)], total)
    wanted = jnp.where(odd, after - slots, starts[group] - HIST)
    return jnp.clip(wanted, 0, total - slots)


def pack_kernel(starts, frames, packed, sems):
    groups, slots = packed.shape[:2]
    total = frames.shape[0]
    copies = []
    for group in range(groups):
        first = first_held(starts, group, group % 2 == 1, groups, total, slots)
        copies.append(
            pltpu.make_async_copy(frames.at[pl.ds(first, slots)], packed.at[group], sems.at[group])
        )
    for copy in copies:
        copy.start()
    for copy in copies:
        copy.wait()


def pack(starts, frames, slots):
    groups = starts.shape[0]
    return pl.pallas_call(
        pack_kernel,
        out_shape=jax.ShapeDtypeStruct((groups, slots) + frames.shape[1:], frames.dtype),
        in_specs=[
            pl.BlockSpec(memory_space=pltpu.SMEM),
            pl.BlockSpec(memory_space=pltpu.VMEM),
        ],
        out_specs=pl.BlockSpec(memory_space=pl.ANY),
        scratch_shapes=[pltpu.SemaphoreType.DMA((groups,))],
    )(starts, frames)


def all_taps(weight):
    return jnp.concatenate(
        [
            jnp.concatenate([weight[a, b, e] for e in range(3)], axis=1)
            for a in range(3)
            for b in range(3)
        ],
        axis=0,
    )


def place(starts, total, slots):
    groups = starts.shape[0]
    group = lax.axis_index("tc") * 2 + lax.axis_index("core")
    odd = lax.axis_index("core") == 1
    held = first_held(starts, group, odd, groups, total, slots)
    after = jnp.where(group + 1 < groups, starts[jnp.minimum(group + 1, groups - 1)], total)
    extra = jnp.where(odd, held - (SPAN - slots), held + slots)
    return group, starts[group], after - starts[group], held, extra


def locate(i, start, held, extra, slots):
    frame = start - HIST + i
    slot = frame - held
    inside = jnp.logical_and(slot >= 0, slot < slots)
    inside = jnp.logical_or(inside, frame < 0)
    return inside, jnp.clip(slot, 0, slots - 1), jnp.clip(frame - extra, 0, SPAN - slots - 1)


def column_sums(sums, cols):
    return (
        sums[0, :, 7 : cols + 7, :] + sums[1, :, 8 : cols + 8, :] + sums[2, :, 9 : cols + 9, :]
    )


def clear_sides(sums, cols):
    shape = (sums.shape[1], 1, sums.shape[3])
    sums[0, :, 7:8, :] = jnp.zeros(shape, jnp.float32)
    sums[2, :, cols + 8 : cols + 9, :] = jnp.zeros(shape, jnp.float32)


def inner_kernel(
    total, starts, own, other, weight, gain, bias, out,
    raw, act, sums, result, frame_sems, out_sems,
):
    rows, slots, cols, chans = own.shape
    inner = rows - 2
    group, start, length, held, extra = place(starts, total, slots)
    for i in range(SPAN):
        inside, slot, spare = locate(i, start, held, extra, slots)

        @pl.when(inside)
        def _():
            pltpu.make_async_copy(own.at[:, slot], raw.at[i], frame_sems.at[i]).start()

        @pl.when(jnp.logical_not(inside))
        def _():
            pltpu.make_async_copy(other.at[:, spare], raw.at[i], frame_sems.at[i]).start()

    def arrived(i):
        pltpu.make_async_copy(own.at[:, 0], raw.at[i], frame_sems.at[i]).wait()

    clear_sides(sums, cols)

    for i in range(3):
        arrived(i)
    act[2] = activate(raw[2], gain[...])

    @pl.when(group > 0)
    def _():
        act[0] = activate(raw[0], gain[...])
        act[1] = activate(raw[1], gain[...])

    @pl.when(group == 0)
    def _():
        act[0] = jnp.zeros(act.shape[1:], act.dtype)
        act[1] = jnp.zeros(act.shape[1:], act.dtype)

    for i in range(3, SPAN):
        arrived(i)

    def one_frame(k, carry):
        lhs = jnp.concatenate(
            [
                act[k + a, pl.ds(b, inner)].reshape(inner * cols, chans)
                for a in range(3)
                for b in range(3)
            ],
            axis=1,
        )
        part = jnp.dot(lhs, all_taps(weight), preferred_element_type=jnp.float32)
        for e in range(3):
            sums[e, :, 8 : cols + 8, :] = part[:, e * chans : (e + 1) * chans].reshape(
                inner, cols, chans
            )
        later = jnp.minimum(k + 3, SPAN - 1)
        act[later] = activate(raw[later], gain[...])
        latent = raw[k + HIST, pl.ds(1, inner)].astype(jnp.float32)
        result[k, pl.ds(1, inner)] = (latent + column_sums(sums, cols) + bias[...]).astype(
            result.dtype
        )
        pltpu.make_async_copy(result.at[k], out.at[k], out_sems.at[k]).start()
        return carry

    def blank_frame(k, carry):
        result[k] = jnp.zeros(result.shape[1:], result.dtype)
        pltpu.make_async_copy(result.at[k], out.at[k], out_sems.at[k]).start()
        return carry

    lax.fori_loop(length, FMAX, blank_frame, 0)
    lax.fori_loop(0, length, one_frame, 0)
    for k in range(FMAX):
        pltpu.make_async_copy(result.at[k], out.at[k], out_sems.at[k]).wait()


def edge_kernel(
    total, starts, own, other, above, below, weight, gain, bias, partial, out,
    raw, act, sums, result, frame_sems, out_sems,
):
    del partial
    rows, slots, cols, chans = own.shape
    group, start, length, held, extra = place(starts, total, slots)

    def copies(i, source, index, rim):
        return [
            pltpu.make_async_copy(above.at[rim], raw.at[i, 0, 0], frame_sems.at[i, 0]),
            pltpu.make_async_copy(
                source.at[pl.ds(0, 2), index], raw.at[i, 0, pl.ds(1, 2)], frame_sems.at[i, 1]
            ),
            pltpu.make_async_copy(
                source.at[pl.ds(rows - 2, 2), index], raw.at[i, 1, pl.ds(0, 2)], frame_sems.at[i, 2]
            ),
            pltpu.make_async_copy(below.at[rim], raw.at[i, 1, 2], frame_sems.at[i, 3]),
        ]

    for i in range(SPAN):
        inside, slot, spare = locate(i, start, held, extra, slots)

        @pl.when(inside)
        def _():
            for copy in copies(i, own, slot, slot):
                copy.start()

        @pl.when(jnp.logical_not(inside))
        def _():
            for copy in copies(i, other, spare, slots + spare):
                copy.start()

    clear_sides(sums, cols)
    for i in range(SPAN):
        for copy in copies(i, own, 0, 0):
            copy.wait()
        act[i] = activate(raw[i], gain[...])

    @pl.when(group == 0)
    def _():
        for i in range(HIST):
            act[i] = jnp.zeros(act.shape[1:], act.dtype)

    lhs = jnp.concatenate(
        [
            act[a : a + FMAX, :, b].reshape(FMAX * 2 * cols, chans)
            for a in range(3)
            for b in range(3)
        ],
        axis=1,
    )
    part = jnp.dot(lhs, all_taps(weight), preferred_element_type=jnp.float32)
    for e in range(3):
        sums[e, :, 8 : cols + 8, :] = part[:, e * chans : (e + 1) * chans].reshape(
            FMAX * 2, cols, chans
        )
    convolved = column_sums(sums, cols).reshape(FMAX, 2, cols, chans)
    for k in range(FMAX):
        for side in range(2):
            latent = raw[k + HIST, side, 1].astype(jnp.float32)
            total_sum = (latent + convolved[k, side] + bias[...]).astype(result.dtype)
            result[k, side] = jnp.where(k < length, total_sum, jnp.zeros_like(total_sum))
    finished = [
        pltpu.make_async_copy(
            result.at[k, side], out.at[k, side * (rows - 1)], out_sems.at[k, side]
        )
        for k in range(FMAX)
        for side in range(2)
    ]
    for copy in finished:
        copy.start()
    for copy in finished:
        copy.wait()


def inner_rows(total, starts, own, other, weight, gain, bias):
    rows, _, cols, chans = own.shape
    hbm = pl.BlockSpec(memory_space=pltpu.HBM)
    vmem = pl.BlockSpec(memory_space=pltpu.VMEM)
    return pl.pallas_call(
        functools.partial(inner_kernel, total),
        out_shape=jax.ShapeDtypeStruct((FMAX, rows, cols, chans), own.dtype),
        in_specs=[pl.BlockSpec(memory_space=pltpu.SMEM)] + [hbm] * 2 + [vmem] * 3,
        out_specs=hbm,
        scratch_shapes=[
            pltpu.VMEM((SPAN, rows, cols, chans), jnp.bfloat16),
            pltpu.VMEM((SPAN, rows, cols, chans), jnp.bfloat16),
            pltpu.VMEM((3, rows - 2, cols + 16, chans), jnp.float32),
            pltpu.VMEM((FMAX, rows, cols, chans), jnp.bfloat16),
            pltpu.SemaphoreType.DMA((SPAN,)),
            pltpu.SemaphoreType.DMA((FMAX,)),
        ],
        compiler_params=pltpu.CompilerParams(vmem_limit_bytes=VMEM_BYTES),
    )(starts, own, other, weight, gain, bias)


def edge_rows(total, starts, own, other, above, below, weight, gain, bias, partial):
    rows, _, cols, chans = own.shape
    hbm = pl.BlockSpec(memory_space=pltpu.HBM)
    vmem = pl.BlockSpec(memory_space=pltpu.VMEM)
    return pl.pallas_call(
        functools.partial(edge_kernel, total),
        out_shape=jax.ShapeDtypeStruct(partial.shape, partial.dtype),
        in_specs=[pl.BlockSpec(memory_space=pltpu.SMEM)] + [hbm] * 4 + [vmem] * 3 + [hbm],
        out_specs=hbm,
        scratch_shapes=[
            pltpu.VMEM((SPAN, 2, 3, cols, chans), jnp.bfloat16),
            pltpu.VMEM((SPAN, 2, 3, cols, chans), jnp.bfloat16),
            pltpu.VMEM((3, 2 * FMAX, cols + 16, chans), jnp.float32),
            pltpu.VMEM((FMAX, 2, cols, chans), jnp.bfloat16),
            pltpu.SemaphoreType.DMA((SPAN, 4)),
            pltpu.SemaphoreType.DMA((FMAX, 2)),
        ],
        input_output_aliases={8: 0},
        compiler_params=pltpu.CompilerParams(vmem_limit_bytes=VMEM_BYTES),
    )(starts, own, other, above, below, weight, gain, bias, partial)


def with_slots(slots, latent, group_start, gain, conv_weight, bias):
    total = latent.shape[0]
    groups = group_start.shape[0]
    missing = SPAN - slots
    stripes = lax.axis_size("ha")
    core = lax.axis_index("core")
    chip = lax.axis_index("tc")
    packed = pack(group_start, latent[:, 0], slots)
    own = lax.all_to_all(packed, ("tc", "core"), split_axis=0, concat_axis=0, tiled=True)

    front = first_held(group_start, 2 * chip, False, groups, total, slots)
    back = first_held(group_start, 2 * chip + 1, True, groups, total, slots)
    wanted = jnp.where(core == 0, back - missing - front, front + slots - back)
    sent = lax.dynamic_slice_in_dim(own, jnp.clip(wanted, 0, slots - missing), missing, 1)
    other = lax.ppermute(sent, "core", [(0, 1), (1, 0)])

    up = [(h, h + 1) for h in range(stripes - 1)]
    down = [(h + 1, h) for h in range(stripes - 1)]
    above = lax.ppermute(jnp.concatenate([own[-1], other[-1]], axis=0), "ha", up)
    below = lax.ppermute(jnp.concatenate([own[0], other[0]], axis=0), "ha", down)
    partial = inner_rows(total, group_start, own, other, conv_weight, gain, bias)
    return edge_rows(
        total, group_start, own, other, above, below, conv_weight, gain, bias, partial
    )


def on_device(latent, group_start, norm_gain, conv_weight, conv_bias):
    cores = lax.axis_size("core")
    chip_starts = jnp.append(group_start[::cores], latent.shape[0])
    most = jnp.max(chip_starts[1:] - chip_starts[:-1])
    return lax.cond(
        most <= 2 * (FMAX - 1),
        functools.partial(with_slots, FMAX),
        functools.partial(with_slots, FMAX + 1),
        latent, group_start, norm_gain.reshape(1, -1), conv_weight, conv_bias.reshape(1, -1),
    )


def solution(mesh):
    devices = mesh.devices
    fine = Mesh(
        devices.reshape(devices.shape[0], devices.shape[1] // 2, 2), ("ha", "tc", "core")
    )
    placed = (P(None, ("ha", "tc", "core"), None, None), P(), P(), P(), P())
    return jax.shard_map(
        on_device,
        mesh=fine,
        in_specs=placed,
        out_specs=P(("tc", "core"), "ha", None, None),
        check_vma=False,
    )
```

```python
import functools

import jax
import jax.numpy as jnp
from jax import lax
from jax.experimental import pallas as pl
from jax.experimental.pallas import tpu as pltpu
from jax.sharding import Mesh, PartitionSpec as P

FMAX = 4
HIST = 2
SPAN = FMAX + HIST
VMEM_BYTES = 30 * 2**20
EDGE_VMEM_BYTES = 50 * 2**20


def activate(raw, gain):
    wide = raw.astype(jnp.float32)
    power = jnp.mean(wide * wide, axis=-1, keepdims=True)
    half = wide * lax.rsqrt(power + 1e-06) * (0.5 * gain)
    return (half + half * jnp.tanh(half)).astype(jnp.bfloat16)


def first_held(starts, group, odd, groups, total, slots):
    after = jnp.where(group + 1 < groups, starts[jnp.minimum(group + 1, groups - 1)], total)
    wanted = jnp.where(odd, after - slots, starts[group] - HIST)
    return jnp.clip(wanted, 0, total - slots)


def pack_kernel(starts, frames, packed, sems):
    groups, slots = packed.shape[:2]
    total = frames.shape[0]
    copies = []
    for group in range(groups):
        first = first_held(starts, group, group % 2 == 1, groups, total, slots)
        copies.append(
            pltpu.make_async_copy(frames.at[pl.ds(first, slots)], packed.at[group], sems.at[group])
        )
    for copy in copies:
        copy.start()
    for copy in copies:
        copy.wait()


def pack(starts, frames, slots):
    groups = starts.shape[0]
    return pl.pallas_call(
        pack_kernel,
        out_shape=jax.ShapeDtypeStruct((groups, slots) + frames.shape[1:], frames.dtype),
        in_specs=[
            pl.BlockSpec(memory_space=pltpu.SMEM),
            pl.BlockSpec(memory_space=pltpu.VMEM),
        ],
        out_specs=pl.BlockSpec(memory_space=pl.ANY),
        scratch_shapes=[pltpu.SemaphoreType.DMA((groups,))],
    )(starts, frames)


def all_taps(weight):
    return jnp.concatenate(
        [
            jnp.concatenate([weight[a, b, e] for e in range(3)], axis=1)
            for a in range(3)
            for b in range(3)
        ],
        axis=0,
    )


def place(starts, total, slots):
    groups = starts.shape[0]
    group = lax.axis_index("tc") * 2 + lax.axis_index("core")
    odd = lax.axis_index("core") == 1
    held = first_held(starts, group, odd, groups, total, slots)
    after = jnp.where(group + 1 < groups, starts[jnp.minimum(group + 1, groups - 1)], total)
    extra = jnp.where(odd, held - (SPAN - slots), held + slots)
    return group, starts[group], after - starts[group], held, extra


def locate(i, start, held, extra, slots):
    frame = start - HIST + i
    slot = frame - held
    inside = jnp.logical_and(slot >= 0, slot < slots)
    inside = jnp.logical_or(inside, frame < 0)
    return inside, jnp.clip(slot, 0, slots - 1), jnp.clip(frame - extra, 0, SPAN - slots - 1)


def column_sums(sums, cols):
    return (
        sums[0, :, 7 : cols + 7, :] + sums[1, :, 8 : cols + 8, :] + sums[2, :, 9 : cols + 9, :]
    )


def clear_sides(sums, cols):
    shape = (sums.shape[1], 1, sums.shape[3])
    sums[0, :, 7:8, :] = jnp.zeros(shape, jnp.float32)
    sums[2, :, cols + 8 : cols + 9, :] = jnp.zeros(shape, jnp.float32)


def inner_kernel(
    total, starts, own, other, weight, gain, bias, out,
    raw, act, sums, result, frame_sems, out_sems,
):
    rows, slots, cols, chans = own.shape
    inner = rows - 2
    group, start, length, held, extra = place(starts, total, slots)
    for i in range(SPAN):
        inside, slot, spare = locate(i, start, held, extra, slots)

        @pl.when(inside)
        def _():
            pltpu.make_async_copy(own.at[:, slot], raw.at[i], frame_sems.at[i]).start()

        @pl.when(jnp.logical_not(inside))
        def _():
            pltpu.make_async_copy(other.at[:, spare], raw.at[i], frame_sems.at[i]).start()

    def arrived(i):
        pltpu.make_async_copy(own.at[:, 0], raw.at[i], frame_sems.at[i]).wait()

    clear_sides(sums, cols)

    for i in range(3):
        arrived(i)
    act[2] = activate(raw[2], gain[...])

    @pl.when(group > 0)
    def _():
        act[0] = activate(raw[0], gain[...])
        act[1] = activate(raw[1], gain[...])

    @pl.when(group == 0)
    def _():
        act[0] = jnp.zeros(act.shape[1:], act.dtype)
        act[1] = jnp.zeros(act.shape[1:], act.dtype)

    for i in range(3, SPAN):
        arrived(i)

    def one_frame(k, carry):
        lhs = jnp.concatenate(
            [
                act[k + a, pl.ds(b, inner)].reshape(inner * cols, chans)
                for a in range(3)
                for b in range(3)
            ],
            axis=1,
        )
        part = jnp.dot(lhs, all_taps(weight), preferred_element_type=jnp.float32)
        for e in range(3):
            sums[e, :, 8 : cols + 8, :] = part[:, e * chans : (e + 1) * chans].reshape(
                inner, cols, chans
            )
        later = jnp.minimum(k + 3, SPAN - 1)
        act[later] = activate(raw[later], gain[...])
        latent = raw[k + HIST, pl.ds(1, inner)].astype(jnp.float32)
        result[k, pl.ds(1, inner)] = (latent + column_sums(sums, cols) + bias[...]).astype(
            result.dtype
        )
        pltpu.make_async_copy(result.at[k], out.at[k], out_sems.at[k]).start()
        return carry

    def blank_frame(k, carry):
        result[k] = jnp.zeros(result.shape[1:], result.dtype)
        pltpu.make_async_copy(result.at[k], out.at[k], out_sems.at[k]).start()
        return carry

    lax.fori_loop(length, FMAX, blank_frame, 0)
    lax.fori_loop(0, length, one_frame, 0)
    for k in range(FMAX):
        pltpu.make_async_copy(result.at[k], out.at[k], out_sems.at[k]).wait()


def edge_kernel(
    total, starts, own, other, rims, weight, gain, bias, partial, out,
    raw, act, sums, result, frame_sems, out_sems,
):
    del partial
    rows, slots, cols, chans = own.shape
    group, start, length, held, extra = place(starts, total, slots)

    stripes = rims.shape[0]
    stripe = lax.axis_index("ha")
    above = rims.at[jnp.maximum(stripe - 1, 0), 1]
    below = rims.at[jnp.minimum(stripe + 1, stripes - 1), 0]

    def copies(i, source, index, rim):
        return [
            pltpu.make_async_copy(above.at[rim], raw.at[i, 0, 0], frame_sems.at[i, 0]),
            pltpu.make_async_copy(
                source.at[pl.ds(0, 2), index], raw.at[i, 0, pl.ds(1, 2)], frame_sems.at[i, 1]
            ),
            pltpu.make_async_copy(
                source.at[pl.ds(rows - 2, 2), index], raw.at[i, 1, pl.ds(0, 2)], frame_sems.at[i, 2]
            ),
            pltpu.make_async_copy(below.at[rim], raw.at[i, 1, 2], frame_sems.at[i, 3]),
        ]

    for i in range(SPAN):
        inside, slot, spare = locate(i, start, held, extra, slots)

        @pl.when(inside)
        def _():
            for copy in copies(i, own, slot, slot):
                copy.start()

        @pl.when(jnp.logical_not(inside))
        def _():
            for copy in copies(i, other, spare, slots + spare):
                copy.start()

    clear_sides(sums, cols)
    for i in range(SPAN):
        for copy in copies(i, own, 0, 0):
            copy.wait()
        act[i] = activate(raw[i], gain[...])

    @pl.when(group == 0)
    def _():
        for i in range(HIST):
            act[i] = jnp.zeros(act.shape[1:], act.dtype)

    for side, last in ((0, 0), (1, stripes - 1)):

        @pl.when(stripe == last)
        def _():
            for i in range(SPAN):
                act[i, side, 2 * side] = jnp.zeros(act.shape[3:], act.dtype)

    lhs = jnp.concatenate(
        [
            act[a : a + FMAX, :, b].reshape(FMAX * 2 * cols, chans)
            for a in range(3)
            for b in range(3)
        ],
        axis=1,
    )
    part = jnp.dot(lhs, all_taps(weight), preferred_element_type=jnp.float32)
    for e in range(3):
        sums[e, :, 8 : cols + 8, :] = part[:, e * chans : (e + 1) * chans].reshape(
            FMAX * 2, cols, chans
        )
    convolved = column_sums(sums, cols).reshape(FMAX, 2, cols, chans)
    for k in range(FMAX):
        for side in range(2):
            latent = raw[k + HIST, side, 1].astype(jnp.float32)
            total_sum = (latent + convolved[k, side] + bias[...]).astype(result.dtype)
            result[k, side] = jnp.where(k < length, total_sum, jnp.zeros_like(total_sum))
    finished = [
        pltpu.make_async_copy(
            result.at[k, side], out.at[k, side * (rows - 1)], out_sems.at[k, side]
        )
        for k in range(FMAX)
        for side in range(2)
    ]
    for copy in finished:
        copy.start()
    for copy in finished:
        copy.wait()


def inner_rows(total, starts, own, other, weight, gain, bias):
    rows, _, cols, chans = own.shape
    hbm = pl.BlockSpec(memory_space=pltpu.HBM)
    vmem = pl.BlockSpec(memory_space=pltpu.VMEM)
    return pl.pallas_call(
        functools.partial(inner_kernel, total),
        out_shape=jax.ShapeDtypeStruct((FMAX, rows, cols, chans), own.dtype),
        in_specs=[pl.BlockSpec(memory_space=pltpu.SMEM)] + [hbm] * 2 + [vmem] * 3,
        out_specs=hbm,
        scratch_shapes=[
            pltpu.VMEM((SPAN, rows, cols, chans), jnp.bfloat16),
            pltpu.VMEM((SPAN, rows, cols, chans), jnp.bfloat16),
            pltpu.VMEM((3, rows - 2, cols + 16, chans), jnp.float32),
            pltpu.VMEM((FMAX, rows, cols, chans), jnp.bfloat16),
            pltpu.SemaphoreType.DMA((SPAN,)),
            pltpu.SemaphoreType.DMA((FMAX,)),
        ],
        compiler_params=pltpu.CompilerParams(vmem_limit_bytes=VMEM_BYTES),
    )(starts, own, other, weight, gain, bias)


def edge_rows(total, starts, own, other, rims, weight, gain, bias, partial):
    rows, _, cols, chans = own.shape
    hbm = pl.BlockSpec(memory_space=pltpu.HBM)
    vmem = pl.BlockSpec(memory_space=pltpu.VMEM)
    return pl.pallas_call(
        functools.partial(edge_kernel, total),
        out_shape=jax.ShapeDtypeStruct(partial.shape, partial.dtype),
        in_specs=[pl.BlockSpec(memory_space=pltpu.SMEM)] + [hbm] * 3 + [vmem] * 3 + [hbm],
        out_specs=hbm,
        scratch_shapes=[
            pltpu.VMEM((SPAN, 2, 3, cols, chans), jnp.bfloat16),
            pltpu.VMEM((SPAN, 2, 3, cols, chans), jnp.bfloat16),
            pltpu.VMEM((3, 2 * FMAX, cols + 16, chans), jnp.float32),
            pltpu.VMEM((FMAX, 2, cols, chans), jnp.bfloat16),
            pltpu.SemaphoreType.DMA((SPAN, 4)),
            pltpu.SemaphoreType.DMA((FMAX, 2)),
        ],
        input_output_aliases={7: 0},
        compiler_params=pltpu.CompilerParams(vmem_limit_bytes=EDGE_VMEM_BYTES),
    )(starts, own, other, rims, weight, gain, bias, partial)


def with_slots(slots, latent, group_start, gain, conv_weight, bias):
    total = latent.shape[0]
    groups = group_start.shape[0]
    missing = SPAN - slots
    core = lax.axis_index("core")
    chip = lax.axis_index("tc")
    packed = pack(group_start, latent[:, 0], slots)
    own = lax.all_to_all(packed, ("tc", "core"), split_axis=0, concat_axis=0, tiled=True)

    front = first_held(group_start, 2 * chip, False, groups, total, slots)
    back = first_held(group_start, 2 * chip + 1, True, groups, total, slots)
    wanted = jnp.where(core == 0, back - missing - front, front + slots - back)
    sent = lax.dynamic_slice_in_dim(own, jnp.clip(wanted, 0, slots - missing), missing, 1)
    other = lax.ppermute(sent, "core", [(0, 1), (1, 0)])

    rim = jnp.stack(
        [
            jnp.concatenate([own[0], other[0]], axis=0),
            jnp.concatenate([own[-1], other[-1]], axis=0),
        ]
    )
    rims = lax.all_gather(rim, "ha", axis=0)
    partial = inner_rows(total, group_start, own, other, conv_weight, gain, bias)
    return edge_rows(
        total, group_start, own, other, rims, conv_weight, gain, bias, partial
    )


def on_device(latent, group_start, norm_gain, conv_weight, conv_bias):
    cores = lax.axis_size("core")
    chip_starts = jnp.append(group_start[::cores], latent.shape[0])
    most = jnp.max(chip_starts[1:] - chip_starts[:-1])
    return lax.cond(
        most <= 2 * (FMAX - 1),
        functools.partial(with_slots, FMAX),
        functools.partial(with_slots, FMAX + 1),
        latent, group_start, norm_gain.reshape(1, -1), conv_weight, conv_bias.reshape(1, -1),
    )


def solution(mesh):
    devices = mesh.devices
    fine = Mesh(
        devices.reshape(devices.shape[0], devices.shape[1] // 2, 2), ("ha", "tc", "core")
    )
    placed = (P(None, ("ha", "tc", "core"), None, None), P(), P(), P(), P())
    return jax.shard_map(
        on_device,
        mesh=fine,
        in_specs=placed,
        out_specs=P(("tc", "core"), "ha", None, None),
        check_vma=False,
    )
```

```python
import functools
from typing import NamedTuple

import jax
import jax.numpy as jnp
from jax import lax
from jax.experimental import pallas as pl
from jax.experimental.pallas import tpu as pltpu
from jax.sharding import Mesh, PartitionSpec as P

FMAX = 4
HIST = 2
SPAN = FMAX + HIST
VMEM_BYTES = 30 * 2**20


def activate(raw, gain):
    wide = raw.astype(jnp.float32)
    power = jnp.mean(wide * wide, axis=-1, keepdims=True)
    half = wide * lax.rsqrt(power + 1e-06) * (0.5 * gain)
    return (half + half * jnp.tanh(half)).astype(jnp.bfloat16)


def first_held(starts, group, odd, groups, total, slots):
    after = jnp.where(group + 1 < groups, starts[jnp.minimum(group + 1, groups - 1)], total)
    wanted = jnp.where(odd, after - slots, starts[group] - HIST)
    return jnp.clip(wanted, 0, total - slots)


def pack_kernel(starts, frames, packed, sems):
    groups, slots = packed.shape[:2]
    total = frames.shape[0]
    copies = []
    for group in range(groups):
        first = first_held(starts, group, group % 2 == 1, groups, total, slots)
        copies.append(
            pltpu.make_async_copy(frames.at[pl.ds(first, slots)], packed.at[group], sems.at[group])
        )
    for copy in copies:
        copy.start()
    for copy in copies:
        copy.wait()


def pack(starts, frames, slots):
    groups = starts.shape[0]
    return pl.pallas_call(
        pack_kernel,
        out_shape=jax.ShapeDtypeStruct((groups, slots) + frames.shape[1:], frames.dtype),
        in_specs=[
            pl.BlockSpec(memory_space=pltpu.SMEM),
            pl.BlockSpec(memory_space=pltpu.VMEM),
        ],
        out_specs=pl.BlockSpec(memory_space=pl.ANY),
        scratch_shapes=[pltpu.SemaphoreType.DMA((groups,))],
    )(starts, frames)


def all_taps(weight):
    return jnp.concatenate(
        [
            jnp.concatenate([weight[a, b, e] for e in range(3)], axis=1)
            for a in range(3)
            for b in range(3)
        ],
        axis=0,
    )


class Plan(NamedTuple):
    start: jax.Array
    length: jax.Array
    held: jax.Array
    extra: jax.Array
    first: jax.Array
    count: jax.Array
    gives: jax.Array
    takes: jax.Array
    slot: jax.Array


def place(starts, total, slots):
    groups = starts.shape[0]
    core = lax.axis_index("core")
    group = lax.axis_index("tc") * 2 + core
    odd = core == 1

    def start_of(j):
        return jnp.where(j < groups, starts[jnp.minimum(j, groups - 1)], total)

    held = first_held(starts, group, odd, groups, total, slots)
    extra = jnp.where(odd, held - (SPAN - slots), held + slots)
    most = slots - 1
    begin, other_start, end = (start_of(group - core + j) for j in range(3))
    middle = jnp.clip(other_start, end - most, begin + most)
    lost = jnp.where(odd, other_start < middle, other_start > middle)
    gained = jnp.where(odd, other_start > middle, other_start < middle)
    return Plan(
        start=starts[group],
        length=start_of(group + 1) - starts[group],
        held=held,
        extra=extra,
        first=jnp.where(odd, middle, begin),
        count=jnp.where(odd, end - middle, middle - begin),
        gives=gained,
        takes=lost,
        slot=jnp.where(odd, 0, other_start - begin - 1),
    )


def locate(frame, held, extra, slots):
    slot = frame - held
    inside = jnp.logical_and(slot >= 0, slot < slots)
    inside = jnp.logical_or(inside, frame < 0)
    return inside, jnp.clip(slot, 0, slots - 1), jnp.clip(frame - extra, 0, SPAN - slots - 1)


def column_sums(sums, cols):
    return (
        sums[0, :, 7 : cols + 7, :] + sums[1, :, 8 : cols + 8, :] + sums[2, :, 9 : cols + 9, :]
    )


def clear_sides(sums, cols):
    shape = (sums.shape[1], 1, sums.shape[3])
    sums[0, :, 7:8, :] = jnp.zeros(shape, jnp.float32)
    sums[2, :, cols + 8 : cols + 9, :] = jnp.zeros(shape, jnp.float32)


def inner_kernel(
    total, starts, own, other, weight, gain, bias, out, moved,
    raw, act, sums, result, frame_sems, out_sems,
):
    rows, slots, cols, chans = own.shape
    inner = rows - 2
    span = raw.shape[0]
    plan = place(starts, total, slots)
    for i in range(span):
        inside, slot, spare = locate(plan.first - HIST + i, plan.held, plan.extra, slots)

        @pl.when(inside)
        def _():
            pltpu.make_async_copy(own.at[:, slot], raw.at[i], frame_sems.at[i]).start()

        @pl.when(jnp.logical_not(inside))
        def _():
            pltpu.make_async_copy(other.at[:, spare], raw.at[i], frame_sems.at[i]).start()

    def arrived(i):
        pltpu.make_async_copy(own.at[:, 0], raw.at[i], frame_sems.at[i]).wait()

    clear_sides(sums, cols)

    for i in range(3):
        arrived(i)
    act[2] = activate(raw[2], gain[...])

    @pl.when(plan.first > 0)
    def _():
        act[0] = activate(raw[0], gain[...])
        act[1] = activate(raw[1], gain[...])

    @pl.when(plan.first == 0)
    def _():
        act[0] = jnp.zeros(act.shape[1:], act.dtype)
        act[1] = jnp.zeros(act.shape[1:], act.dtype)

    for i in range(3, span):
        arrived(i)

    def one_frame(k, carry):
        lhs = jnp.concatenate(
            [
                act[k + a, pl.ds(b, inner)].reshape(inner * cols, chans)
                for a in range(3)
                for b in range(3)
            ],
            axis=1,
        )
        part = jnp.dot(lhs, all_taps(weight), preferred_element_type=jnp.float32)
        for e in range(3):
            sums[e, :, 8 : cols + 8, :] = part[:, e * chans : (e + 1) * chans].reshape(
                inner, cols, chans
            )
        later = jnp.minimum(k + 3, span - 1)
        act[later] = activate(raw[later], gain[...])
        latent = raw[k + HIST, pl.ds(1, inner)].astype(jnp.float32)
        target = plan.first + k - plan.start
        mine = jnp.logical_and(target >= 0, target < plan.length)
        place_in = jnp.where(mine, target, FMAX)
        result[place_in, pl.ds(1, inner)] = (latent + column_sums(sums, cols) + bias[...]).astype(
            result.dtype
        )

        @pl.when(mine)
        def _():
            pltpu.make_async_copy(
                result.at[place_in], out.at[jnp.clip(target, 0, FMAX - 1)], out_sems.at[place_in]
            ).start()

        @pl.when(jnp.logical_not(mine))
        def _():
            pltpu.make_async_copy(result.at[FMAX], moved, out_sems.at[FMAX]).start()

        return carry

    def blank_frame(k, carry):
        result[k] = jnp.zeros(result.shape[1:], result.dtype)
        pltpu.make_async_copy(result.at[k], out.at[k], out_sems.at[k]).start()
        return carry

    lax.fori_loop(plan.length, FMAX, blank_frame, 0)
    lax.fori_loop(0, plan.count, one_frame, 0)
    for k in range(FMAX):

        @pl.when(jnp.logical_not(jnp.logical_and(plan.takes, plan.slot == k)))
        def _():
            pltpu.make_async_copy(result.at[k], out.at[k], out_sems.at[k]).wait()

    @pl.when(plan.gives)
    def _():
        pltpu.make_async_copy(result.at[FMAX], moved, out_sems.at[FMAX]).wait()


def edge_kernel(
    total, starts, own, other, above, below, moved, weight, gain, bias, partial, out,
    raw, act, sums, result, frame_sems, out_sems, moved_sem,
):
    del partial
    rows, slots, cols, chans = own.shape
    plan = place(starts, total, slots)
    inner = pl.ds(1, rows - 2)
    landing = pltpu.make_async_copy(
        moved.at[inner], out.at[jnp.clip(plan.slot, 0, FMAX - 1), inner], moved_sem
    )
    pl.when(plan.takes)(landing.start)

    def copies(i, source, index, rim):
        return [
            pltpu.make_async_copy(above.at[rim], raw.at[i, 0, 0], frame_sems.at[i, 0]),
            pltpu.make_async_copy(
                source.at[pl.ds(0, 2), index], raw.at[i, 0, pl.ds(1, 2)], frame_sems.at[i, 1]
            ),
            pltpu.make_async_copy(
                source.at[pl.ds(rows - 2, 2), index], raw.at[i, 1, pl.ds(0, 2)], frame_sems.at[i, 2]
            ),
            pltpu.make_async_copy(below.at[rim], raw.at[i, 1, 2], frame_sems.at[i, 3]),
        ]

    for i in range(SPAN):
        inside, slot, spare = locate(plan.start - HIST + i, plan.held, plan.extra, slots)

        @pl.when(inside)
        def _():
            for copy in copies(i, own, slot, slot):
                copy.start()

        @pl.when(jnp.logical_not(inside))
        def _():
            for copy in copies(i, other, spare, slots + spare):
                copy.start()

    clear_sides(sums, cols)
    for i in range(SPAN):
        for copy in copies(i, own, 0, 0):
            copy.wait()
        act[i] = activate(raw[i], gain[...])

    @pl.when(plan.start == 0)
    def _():
        for i in range(HIST):
            act[i] = jnp.zeros(act.shape[1:], act.dtype)

    stripe = lax.axis_index("ha")
    for side, last in ((0, 0), (1, lax.axis_size("ha") - 1)):

        @pl.when(stripe == last)
        def _():
            for i in range(SPAN):
                act[i, side, 2 * side] = jnp.zeros(act.shape[3:], act.dtype)

    lhs = jnp.concatenate(
        [
            act[a : a + FMAX, :, b].reshape(FMAX * 2 * cols, chans)
            for a in range(3)
            for b in range(3)
        ],
        axis=1,
    )
    part = jnp.dot(lhs, all_taps(weight), preferred_element_type=jnp.float32)
    for e in range(3):
        sums[e, :, 8 : cols + 8, :] = part[:, e * chans : (e + 1) * chans].reshape(
            FMAX * 2, cols, chans
        )
    convolved = column_sums(sums, cols).reshape(FMAX, 2, cols, chans)
    for k in range(FMAX):
        for side in range(2):
            latent = raw[k + HIST, side, 1].astype(jnp.float32)
            total_sum = (latent + convolved[k, side] + bias[...]).astype(result.dtype)
            result[k, side] = jnp.where(k < plan.length, total_sum, jnp.zeros_like(total_sum))
    finished = [
        pltpu.make_async_copy(
            result.at[k, side], out.at[k, side * (rows - 1)], out_sems.at[k, side]
        )
        for k in range(FMAX)
        for side in range(2)
    ]
    for copy in finished:
        copy.start()
    for copy in finished:
        copy.wait()
    pl.when(plan.takes)(landing.wait)


def inner_rows(total, starts, own, other, weight, gain, bias):
    rows, slots, cols, chans = own.shape
    span = slots - 1 + HIST
    hbm = pl.BlockSpec(memory_space=pltpu.HBM)
    vmem = pl.BlockSpec(memory_space=pltpu.VMEM)
    return pl.pallas_call(
        functools.partial(inner_kernel, total),
        out_shape=[
            jax.ShapeDtypeStruct((FMAX, rows, cols, chans), own.dtype),
            jax.ShapeDtypeStruct((rows, cols, chans), own.dtype),
        ],
        in_specs=[pl.BlockSpec(memory_space=pltpu.SMEM)] + [hbm] * 2 + [vmem] * 3,
        out_specs=[hbm] * 2,
        scratch_shapes=[
            pltpu.VMEM((span, rows, cols, chans), jnp.bfloat16),
            pltpu.VMEM((span, rows, cols, chans), jnp.bfloat16),
            pltpu.VMEM((3, rows - 2, cols + 16, chans), jnp.float32),
            pltpu.VMEM((FMAX + 1, rows, cols, chans), jnp.bfloat16),
            pltpu.SemaphoreType.DMA((span,)),
            pltpu.SemaphoreType.DMA((FMAX + 1,)),
        ],
        compiler_params=pltpu.CompilerParams(vmem_limit_bytes=VMEM_BYTES),
    )(starts, own, other, weight, gain, bias)


def edge_rows(total, starts, own, other, above, below, moved, weight, gain, bias, partial):
    rows, _, cols, chans = own.shape
    hbm = pl.BlockSpec(memory_space=pltpu.HBM)
    vmem = pl.BlockSpec(memory_space=pltpu.VMEM)
    return pl.pallas_call(
        functools.partial(edge_kernel, total),
        out_shape=jax.ShapeDtypeStruct(partial.shape, partial.dtype),
        in_specs=[pl.BlockSpec(memory_space=pltpu.SMEM)] + [hbm] * 5 + [vmem] * 3 + [hbm],
        out_specs=hbm,
        scratch_shapes=[
            pltpu.VMEM((SPAN, 2, 3, cols, chans), jnp.bfloat16),
            pltpu.VMEM((SPAN, 2, 3, cols, chans), jnp.bfloat16),
            pltpu.VMEM((3, 2 * FMAX, cols + 16, chans), jnp.float32),
            pltpu.VMEM((FMAX, 2, cols, chans), jnp.bfloat16),
            pltpu.SemaphoreType.DMA((SPAN, 4)),
            pltpu.SemaphoreType.DMA((FMAX, 2)),
            pltpu.SemaphoreType.DMA,
        ],
        input_output_aliases={9: 0},
        compiler_params=pltpu.CompilerParams(vmem_limit_bytes=VMEM_BYTES),
    )(starts, own, other, above, below, moved, weight, gain, bias, partial)


def with_slots(slots, latent, group_start, gain, conv_weight, bias):
    total = latent.shape[0]
    groups = group_start.shape[0]
    missing = SPAN - slots
    stripes = lax.axis_size("ha")
    core = lax.axis_index("core")
    chip = lax.axis_index("tc")
    packed = pack(group_start, latent[:, 0], slots)
    own = lax.all_to_all(packed, ("tc", "core"), split_axis=0, concat_axis=0, tiled=True)

    front = first_held(group_start, 2 * chip, False, groups, total, slots)
    back = first_held(group_start, 2 * chip + 1, True, groups, total, slots)
    wanted = jnp.where(core == 0, back - missing - front, front + slots - back)
    sent = lax.dynamic_slice_in_dim(own, jnp.clip(wanted, 0, slots - missing), missing, 1)
    other = lax.ppermute(sent, "core", [(0, 1), (1, 0)])

    up = [(h, (h + 1) % stripes) for h in range(stripes)]
    down = [(after, before) for before, after in up]
    above = lax.ppermute(jnp.concatenate([own[-1], other[-1]], axis=0), "ha", up)
    below = lax.ppermute(jnp.concatenate([own[0], other[0]], axis=0), "ha", down)
    partial, moved = inner_rows(total, group_start, own, other, conv_weight, gain, bias)
    if slots == FMAX:
        moved = lax.ppermute(moved, "core", [(0, 1), (1, 0)])
    return edge_rows(
        total, group_start, own, other, above, below, moved, conv_weight, gain, bias, partial
    )


def on_device(latent, group_start, norm_gain, conv_weight, conv_bias):
    cores = lax.axis_size("core")
    chip_starts = jnp.append(group_start[::cores], latent.shape[0])
    most = jnp.max(chip_starts[1:] - chip_starts[:-1])
    return lax.cond(
        most <= 2 * (FMAX - 1),
        functools.partial(with_slots, FMAX),
        functools.partial(with_slots, FMAX + 1),
        latent, group_start, norm_gain.reshape(1, -1), conv_weight, conv_bias.reshape(1, -1),
    )


def solution(mesh):
    devices = mesh.devices
    fine = Mesh(
        devices.reshape(devices.shape[0], devices.shape[1] // 2, 2), ("ha", "tc", "core")
    )
    placed = (P(None, ("ha", "tc", "core"), None, None), P(), P(), P(), P())
    return jax.shard_map(
        on_device,
        mesh=fine,
        in_specs=placed,
        out_specs=P(("tc", "core"), "ha", None, None),
        check_vma=False,
    )
```

```python
import functools
from typing import NamedTuple

import jax
import jax.numpy as jnp
from jax import lax
from jax.experimental import pallas as pl
from jax.experimental.pallas import tpu as pltpu
from jax.sharding import Mesh, PartitionSpec as P

FMAX = 4
HIST = 2
SPAN = FMAX + HIST
VMEM_BYTES = 30 * 2**20


def activate(raw, gain):
    wide = raw.astype(jnp.float32)
    power = jnp.mean(wide * wide, axis=-1, keepdims=True)
    half = wide * lax.rsqrt(power + 1e-06) * (0.5 * gain)
    return (half + half * jnp.tanh(half)).astype(jnp.bfloat16)


def first_held(starts, group, odd, groups, total, slots):
    after = jnp.where(group + 1 < groups, starts[jnp.minimum(group + 1, groups - 1)], total)
    wanted = jnp.where(odd, after - slots, starts[group] - HIST)
    return jnp.clip(wanted, 0, total - slots)


def pack_kernel(starts, frames, few, many, fits, sems):
    groups = starts.shape[0]
    total = frames.shape[0]
    chip_starts = [starts[j] for j in range(0, groups, 2)] + [total]
    most = functools.reduce(
        jnp.maximum, [after - start for start, after in zip(chip_starts, chip_starts[1:])]
    )
    enough = most <= 2 * (few.shape[1] - 1)
    fits[0] = enough.astype(jnp.int32)
    for packed, chosen in ((few, enough), (many, jnp.logical_not(enough))):

        @pl.when(chosen)
        def _():
            slots = packed.shape[1]
            copies = []
            for group in range(groups):
                first = first_held(starts, group, group % 2 == 1, groups, total, slots)
                copies.append(
                    pltpu.make_async_copy(
                        frames.at[pl.ds(first, slots)], packed.at[group], sems.at[group]
                    )
                )
            for copy in copies:
                copy.start()
            for copy in copies:
                copy.wait()


def pack(starts, frames):
    groups = starts.shape[0]
    hbm = pl.BlockSpec(memory_space=pltpu.HBM)
    smem = pl.BlockSpec(memory_space=pltpu.SMEM)
    return pl.pallas_call(
        pack_kernel,
        out_shape=[
            jax.ShapeDtypeStruct((groups, slots) + frames.shape[1:], frames.dtype)
            for slots in (FMAX, FMAX + 1)
        ]
        + [jax.ShapeDtypeStruct((1,), jnp.int32)],
        in_specs=[smem, pl.BlockSpec(memory_space=pltpu.VMEM)],
        out_specs=[hbm, hbm, smem],
        scratch_shapes=[pltpu.SemaphoreType.DMA((groups,))],
    )(starts, frames)


def all_taps(weight):
    return jnp.concatenate(
        [
            jnp.concatenate([weight[a, b, e] for e in range(3)], axis=1)
            for a in range(3)
            for b in range(3)
        ],
        axis=0,
    )


class Plan(NamedTuple):
    start: jax.Array
    length: jax.Array
    held: jax.Array
    extra: jax.Array
    first: jax.Array
    count: jax.Array
    gives: jax.Array
    takes: jax.Array
    slot: jax.Array


def place(starts, total, slots):
    groups = starts.shape[0]
    core = lax.axis_index("core")
    group = lax.axis_index("tc") * 2 + core
    odd = core == 1

    def start_of(j):
        return jnp.where(j < groups, starts[jnp.minimum(j, groups - 1)], total)

    held = first_held(starts, group, odd, groups, total, slots)
    extra = jnp.where(odd, held - (SPAN - slots), held + slots)
    most = slots - 1
    begin, other_start, end = (start_of(group - core + j) for j in range(3))
    middle = jnp.clip(other_start, end - most, begin + most)
    lost = jnp.where(odd, other_start < middle, other_start > middle)
    gained = jnp.where(odd, other_start > middle, other_start < middle)
    return Plan(
        start=starts[group],
        length=start_of(group + 1) - starts[group],
        held=held,
        extra=extra,
        first=jnp.where(odd, middle, begin),
        count=jnp.where(odd, end - middle, middle - begin),
        gives=gained,
        takes=lost,
        slot=jnp.where(odd, 0, other_start - begin - 1),
    )


def locate(frame, held, extra, slots):
    slot = frame - held
    inside = jnp.logical_and(slot >= 0, slot < slots)
    inside = jnp.logical_or(inside, frame < 0)
    return inside, jnp.clip(slot, 0, slots - 1), jnp.clip(frame - extra, 0, SPAN - slots - 1)


def column_sums(sums, cols):
    return (
        sums[0, :, 7 : cols + 7, :] + sums[1, :, 8 : cols + 8, :] + sums[2, :, 9 : cols + 9, :]
    )


def clear_sides(sums, cols):
    shape = (sums.shape[1], 1, sums.shape[3])
    sums[0, :, 7:8, :] = jnp.zeros(shape, jnp.float32)
    sums[2, :, cols + 8 : cols + 9, :] = jnp.zeros(shape, jnp.float32)


def inner_kernel(
    total, starts, own, other, weight, gain, bias, out, moved,
    raw, act, sums, result, frame_sems, out_sems,
):
    rows, slots, cols, chans = own.shape
    inner = rows - 2
    span = raw.shape[0]
    plan = place(starts, total, slots)
    for i in range(span):
        inside, slot, spare = locate(plan.first - HIST + i, plan.held, plan.extra, slots)

        @pl.when(inside)
        def _():
            pltpu.make_async_copy(own.at[:, slot], raw.at[i], frame_sems.at[i]).start()

        @pl.when(jnp.logical_not(inside))
        def _():
            pltpu.make_async_copy(other.at[:, spare], raw.at[i], frame_sems.at[i]).start()

    def arrived(i):
        pltpu.make_async_copy(own.at[:, 0], raw.at[i], frame_sems.at[i]).wait()

    clear_sides(sums, cols)

    for i in range(3):
        arrived(i)
    act[2] = activate(raw[2], gain[...])

    @pl.when(plan.first > 0)
    def _():
        act[0] = activate(raw[0], gain[...])
        act[1] = activate(raw[1], gain[...])

    @pl.when(plan.first == 0)
    def _():
        act[0] = jnp.zeros(act.shape[1:], act.dtype)
        act[1] = jnp.zeros(act.shape[1:], act.dtype)

    for i in range(3, span):
        arrived(i)

    def one_frame(k, carry):
        lhs = jnp.concatenate(
            [
                act[k + a, pl.ds(b, inner)].reshape(inner * cols, chans)
                for a in range(3)
                for b in range(3)
            ],
            axis=1,
        )
        part = jnp.dot(lhs, all_taps(weight), preferred_element_type=jnp.float32)
        for e in range(3):
            sums[e, :, 8 : cols + 8, :] = part[:, e * chans : (e + 1) * chans].reshape(
                inner, cols, chans
            )
        later = jnp.minimum(k + 3, span - 1)
        act[later] = activate(raw[later], gain[...])
        latent = raw[k + HIST, pl.ds(1, inner)].astype(jnp.float32)
        target = plan.first + k - plan.start
        mine = jnp.logical_and(target >= 0, target < plan.length)
        place_in = jnp.where(mine, target, FMAX)
        result[place_in, pl.ds(1, inner)] = (latent + column_sums(sums, cols) + bias[...]).astype(
            result.dtype
        )

        @pl.when(mine)
        def _():
            pltpu.make_async_copy(
                result.at[place_in], out.at[jnp.clip(target, 0, FMAX - 1)], out_sems.at[place_in]
            ).start()

        @pl.when(jnp.logical_not(mine))
        def _():
            pltpu.make_async_copy(result.at[FMAX], moved, out_sems.at[FMAX]).start()

        return carry

    def blank_frame(k, carry):
        result[k] = jnp.zeros(result.shape[1:], result.dtype)
        pltpu.make_async_copy(result.at[k], out.at[k], out_sems.at[k]).start()
        return carry

    lax.fori_loop(plan.length, FMAX, blank_frame, 0)
    lax.fori_loop(0, plan.count, one_frame, 0)
    for k in range(FMAX):

        @pl.when(jnp.logical_not(jnp.logical_and(plan.takes, plan.slot == k)))
        def _():
            pltpu.make_async_copy(result.at[k], out.at[k], out_sems.at[k]).wait()

    @pl.when(plan.gives)
    def _():
        pltpu.make_async_copy(result.at[FMAX], moved, out_sems.at[FMAX]).wait()


def edge_kernel(
    total, starts, own, other, above, below, moved, weight, gain, bias, partial, out,
    raw, act, sums, result, frame_sems, out_sems, moved_sem,
):
    del partial
    rows, slots, cols, chans = own.shape
    plan = place(starts, total, slots)
    inner = pl.ds(1, rows - 2)
    landing = pltpu.make_async_copy(
        moved.at[inner], out.at[jnp.clip(plan.slot, 0, FMAX - 1), inner], moved_sem
    )
    pl.when(plan.takes)(landing.start)

    def copies(i, source, index, rim):
        return [
            pltpu.make_async_copy(above.at[rim], raw.at[i, 0, 0], frame_sems.at[i, 0]),
            pltpu.make_async_copy(
                source.at[pl.ds(0, 2), index], raw.at[i, 0, pl.ds(1, 2)], frame_sems.at[i, 1]
            ),
            pltpu.make_async_copy(
                source.at[pl.ds(rows - 2, 2), index], raw.at[i, 1, pl.ds(0, 2)], frame_sems.at[i, 2]
            ),
            pltpu.make_async_copy(below.at[rim], raw.at[i, 1, 2], frame_sems.at[i, 3]),
        ]

    for i in range(SPAN):
        inside, slot, spare = locate(plan.start - HIST + i, plan.held, plan.extra, slots)

        @pl.when(inside)
        def _():
            for copy in copies(i, own, slot, slot):
                copy.start()

        @pl.when(jnp.logical_not(inside))
        def _():
            for copy in copies(i, other, spare, slots + spare):
                copy.start()

    clear_sides(sums, cols)
    for i in range(SPAN):
        for copy in copies(i, own, 0, 0):
            copy.wait()
        act[i] = activate(raw[i], gain[...])

    @pl.when(plan.start == 0)
    def _():
        for i in range(HIST):
            act[i] = jnp.zeros(act.shape[1:], act.dtype)

    stripe = lax.axis_index("ha")
    for side, last in ((0, 0), (1, lax.axis_size("ha") - 1)):

        @pl.when(stripe == last)
        def _():
            for i in range(SPAN):
                act[i, side, 2 * side] = jnp.zeros(act.shape[3:], act.dtype)

    lhs = jnp.concatenate(
        [
            act[a : a + FMAX, :, b].reshape(FMAX * 2 * cols, chans)
            for a in range(3)
            for b in range(3)
        ],
        axis=1,
    )
    part = jnp.dot(lhs, all_taps(weight), preferred_element_type=jnp.float32)
    for e in range(3):
        sums[e, :, 8 : cols + 8, :] = part[:, e * chans : (e + 1) * chans].reshape(
            FMAX * 2, cols, chans
        )
    convolved = column_sums(sums, cols).reshape(FMAX, 2, cols, chans)
    for k in range(FMAX):
        for side in range(2):
            latent = raw[k + HIST, side, 1].astype(jnp.float32)
            total_sum = (latent + convolved[k, side] + bias[...]).astype(result.dtype)
            result[k, side] = jnp.where(k < plan.length, total_sum, jnp.zeros_like(total_sum))
    finished = [
        pltpu.make_async_copy(
            result.at[k, side], out.at[k, side * (rows - 1)], out_sems.at[k, side]
        )
        for k in range(FMAX)
        for side in range(2)
    ]
    for copy in finished:
        copy.start()
    for copy in finished:
        copy.wait()
    pl.when(plan.takes)(landing.wait)


def inner_rows(total, starts, own, other, weight, gain, bias):
    rows, slots, cols, chans = own.shape
    span = slots - 1 + HIST
    hbm = pl.BlockSpec(memory_space=pltpu.HBM)
    vmem = pl.BlockSpec(memory_space=pltpu.VMEM)
    return pl.pallas_call(
        functools.partial(inner_kernel, total),
        out_shape=[
            jax.ShapeDtypeStruct((FMAX, rows, cols, chans), own.dtype),
            jax.ShapeDtypeStruct((rows, cols, chans), own.dtype),
        ],
        in_specs=[pl.BlockSpec(memory_space=pltpu.SMEM)] + [hbm] * 2 + [vmem] * 3,
        out_specs=[hbm] * 2,
        scratch_shapes=[
            pltpu.VMEM((span, rows, cols, chans), jnp.bfloat16),
            pltpu.VMEM((span, rows, cols, chans), jnp.bfloat16),
            pltpu.VMEM((3, rows - 2, cols + 16, chans), jnp.float32),
            pltpu.VMEM((FMAX + 1, rows, cols, chans), jnp.bfloat16),
            pltpu.SemaphoreType.DMA((span,)),
            pltpu.SemaphoreType.DMA((FMAX + 1,)),
        ],
        compiler_params=pltpu.CompilerParams(vmem_limit_bytes=VMEM_BYTES),
    )(starts, own, other, weight, gain, bias)


def edge_rows(total, starts, own, other, above, below, moved, weight, gain, bias, partial):
    rows, _, cols, chans = own.shape
    hbm = pl.BlockSpec(memory_space=pltpu.HBM)
    vmem = pl.BlockSpec(memory_space=pltpu.VMEM)
    return pl.pallas_call(
        functools.partial(edge_kernel, total),
        out_shape=jax.ShapeDtypeStruct(partial.shape, partial.dtype),
        in_specs=[pl.BlockSpec(memory_space=pltpu.SMEM)] + [hbm] * 5 + [vmem] * 3 + [hbm],
        out_specs=hbm,
        scratch_shapes=[
            pltpu.VMEM((SPAN, 2, 3, cols, chans), jnp.bfloat16),
            pltpu.VMEM((SPAN, 2, 3, cols, chans), jnp.bfloat16),
            pltpu.VMEM((3, 2 * FMAX, cols + 16, chans), jnp.float32),
            pltpu.VMEM((FMAX, 2, cols, chans), jnp.bfloat16),
            pltpu.SemaphoreType.DMA((SPAN, 4)),
            pltpu.SemaphoreType.DMA((FMAX, 2)),
            pltpu.SemaphoreType.DMA,
        ],
        input_output_aliases={9: 0},
        compiler_params=pltpu.CompilerParams(vmem_limit_bytes=VMEM_BYTES),
    )(starts, own, other, above, below, moved, weight, gain, bias, partial)


def with_slots(slots, total, few, many, group_start, gain, conv_weight, bias):
    packed = few if slots == FMAX else many
    groups = group_start.shape[0]
    missing = SPAN - slots
    stripes = lax.axis_size("ha")
    core = lax.axis_index("core")
    chip = lax.axis_index("tc")
    own = lax.all_to_all(packed, ("tc", "core"), split_axis=0, concat_axis=0, tiled=True)

    front = first_held(group_start, 2 * chip, False, groups, total, slots)
    back = first_held(group_start, 2 * chip + 1, True, groups, total, slots)
    wanted = jnp.where(core == 0, back - missing - front, front + slots - back)
    sent = lax.dynamic_slice_in_dim(own, jnp.clip(wanted, 0, slots - missing), missing, 1)
    other = lax.ppermute(sent, "core", [(0, 1), (1, 0)])

    up = [(h, (h + 1) % stripes) for h in range(stripes)]
    down = [(after, before) for before, after in up]
    above = lax.ppermute(jnp.concatenate([own[-1], other[-1]], axis=0), "ha", up)
    below = lax.ppermute(jnp.concatenate([own[0], other[0]], axis=0), "ha", down)
    partial, moved = inner_rows(total, group_start, own, other, conv_weight, gain, bias)
    if slots == FMAX:
        moved, above, below = lax.optimization_barrier((moved, above, below))
        moved = lax.ppermute(moved, "core", [(0, 1), (1, 0)])
    return edge_rows(
        total, group_start, own, other, above, below, moved, conv_weight, gain, bias, partial
    )


def on_device(latent, group_start, norm_gain, conv_weight, conv_bias):
    total = latent.shape[0]
    few, many, fits = pack(group_start, latent[:, 0])
    return lax.switch(
        fits[0],
        [
            functools.partial(with_slots, FMAX + 1, total),
            functools.partial(with_slots, FMAX, total),
        ],
        few, many, group_start, norm_gain.reshape(1, -1), conv_weight, conv_bias.reshape(1, -1),
    )


def solution(mesh):
    devices = mesh.devices
    fine = Mesh(
        devices.reshape(devices.shape[0], devices.shape[1] // 2, 2), ("ha", "tc", "core")
    )
    placed = (P(None, ("ha", "tc", "core"), None, None), P(), P(), P(), P())
    return jax.shard_map(
        on_device,
        mesh=fine,
        in_specs=placed,
        out_specs=P(("tc", "core"), "ha", None, None),
        check_vma=False,
    )
```

```python
import functools

import jax
import jax.numpy as jnp
from jax import lax
from jax.experimental import pallas as pl
from jax.experimental.pallas import tpu as pltpu
from jax.sharding import Mesh, PartitionSpec as P

FMAX = 4
HIST = 2
STEP = 8
VMEM_BYTES = 30 * 2**20
SMEM_SPEC = pl.BlockSpec(memory_space=pltpu.SMEM)
VMEM_SPEC = pl.BlockSpec(memory_space=pltpu.VMEM)
HBM_SPEC = pl.BlockSpec(memory_space=pltpu.HBM)


def activate(raw, gain):
    wide = raw.astype(jnp.float32)
    power = jnp.mean(wide * wide, axis=-1, keepdims=True)
    half = wide * lax.rsqrt(power + 1e-06) * (0.5 * gain)
    return (half + half * jnp.tanh(half)).astype(jnp.bfloat16)


def taps_of(weight, row_taps):
    return jnp.concatenate(
        [
            jnp.concatenate([weight[a, b, e] for e in range(3)], axis=1)
            for b in row_taps
            for a in range(3)
        ],
        axis=0,
    )


def convolve(acts, first, count, weight, row_taps, sums):
    cols, chans = acts[0].shape[1:]
    lhs = jnp.concatenate(
        [
            act[pl.ds(first + a, count)].reshape(count * cols, chans)
            for act in acts
            for a in range(3)
        ],
        axis=1,
    )
    part = jnp.dot(lhs, taps_of(weight, row_taps), preferred_element_type=jnp.float32)
    for e in range(3):
        sums[e, pl.ds(0, count), 8 : cols + 8, :] = part[:, e * chans : (e + 1) * chans].reshape(
            count, cols, chans
        )
    return (
        sums[0, pl.ds(0, count), 7 : cols + 7, :]
        + sums[1, pl.ds(0, count), 8 : cols + 8, :]
        + sums[2, pl.ds(0, count), 9 : cols + 9, :]
    )


def clear_sides(sums, cols):
    shape = (sums.shape[1], 1, sums.shape[3])
    sums[0, :, 7:8, :] = jnp.zeros(shape, jnp.float32)
    sums[2, :, cols + 8 : cols + 9, :] = jnp.zeros(shape, jnp.float32)


def near_kernel(own, twin, weight, gain, bias, partial, own_act, twin_act, sums):
    total, cols, _ = own.shape
    core = lax.axis_index("core")
    clear_sides(sums, cols)
    for act in (own_act, twin_act):
        act[pl.ds(0, HIST)] = jnp.zeros((HIST,) + act.shape[1:], act.dtype)

    def prepare(i, carry):
        frames = pl.ds(i * STEP, STEP)
        later = pl.ds(i * STEP + HIST, STEP)
        own_act[later] = activate(own[frames], gain[...])
        twin_act[later] = activate(twin[frames], gain[...])
        return carry

    lax.fori_loop(0, total // STEP, prepare, 0)

    def step(i, carry):
        frames = pl.ds(i * STEP, STEP)
        convolved = convolve(
            (own_act, twin_act), i * STEP, STEP, weight, (1, 2 * (1 - core)), sums
        )
        partial[frames] = own[frames].astype(jnp.float32) + convolved + bias[...]
        return carry

    lax.fori_loop(0, total // STEP, step, 0)


def near_rows(own, twin, weight, gain, bias):
    total, cols, chans = own.shape
    return pl.pallas_call(
        near_kernel,
        out_shape=jax.ShapeDtypeStruct(own.shape, jnp.float32),
        in_specs=[VMEM_SPEC] * 5,
        out_specs=VMEM_SPEC,
        scratch_shapes=[
            pltpu.VMEM((HIST + total, cols, chans), jnp.bfloat16),
            pltpu.VMEM((HIST + total, cols, chans), jnp.bfloat16),
            pltpu.VMEM((3, STEP, cols + 16, chans), jnp.float32),
        ],
        compiler_params=pltpu.CompilerParams(vmem_limit_bytes=VMEM_BYTES),
    )(own, twin, weight, gain, bias)


def far_frames(begin, far, recent, partial, weight, gain, act, sums):
    count, cols, chans = far.shape
    core = lax.axis_index("core")
    row = lax.axis_index("ha") * lax.axis_size("tc") + lax.axis_index("tc")
    row = row * lax.axis_size("core") + core
    rows = lax.axis_size("ha") * lax.axis_size("tc") * lax.axis_size("core")
    clear_sides(sums, cols)
    if recent is None:
        act[pl.ds(0, HIST)] = jnp.zeros((HIST, cols, chans), act.dtype)
    else:
        act[pl.ds(0, HIST)] = activate(recent[pl.ds(recent.shape[0] - HIST, HIST)], gain[...])
    act[pl.ds(HIST, count)] = activate(far[...], gain[...])

    @pl.when(jnp.logical_or(row == 0, row == rows - 1))
    def _():
        act[...] = jnp.zeros(act.shape, act.dtype)

    convolved = convolve((act,), 0, count, weight, (2 * core,), sums)
    return (partial[pl.ds(begin, count)] + convolved).astype(jnp.bfloat16)


def early_kernel(far, partial, weight, gain, out, act, sums):
    out[...] = far_frames(0, far, None, partial, weight, gain, act, sums)


def late_kernel(starts, early_far, far, early, partial, weight, gain, packed,
                act, sums, result, early_sem, sems):
    cut = early.shape[0]
    count, cols, chans = far.shape
    groups = packed.shape[0]
    copy = pltpu.make_async_copy(early, result.at[pl.ds(0, cut)], early_sem)
    copy.start()
    result[pl.ds(cut + count, FMAX)] = jnp.zeros((FMAX, cols, chans), result.dtype)
    result[pl.ds(cut, count)] = far_frames(
        cut, far, early_far, partial, weight, gain, act, sums
    )
    copy.wait()
    copies = [
        pltpu.make_async_copy(
            result.at[pl.ds(jnp.clip(starts[j], 0, cut + count), FMAX)], packed.at[j], sems.at[j]
        )
        for j in range(groups)
    ]
    for copy in copies:
        copy.start()
    for copy in copies:
        copy.wait()


def far_scratch(count, cols, chans):
    return [
        pltpu.VMEM((HIST + count, cols, chans), jnp.bfloat16),
        pltpu.VMEM((3, count, cols + 16, chans), jnp.float32),
    ]


def early_rows(far, partial, weight, gain):
    return pl.pallas_call(
        early_kernel,
        out_shape=jax.ShapeDtypeStruct(far.shape, jnp.bfloat16),
        in_specs=[VMEM_SPEC] * 4,
        out_specs=VMEM_SPEC,
        scratch_shapes=far_scratch(*far.shape),
        compiler_params=pltpu.CompilerParams(vmem_limit_bytes=VMEM_BYTES),
    )(far, partial, weight, gain)


def late_rows(starts, early_far, far, early, partial, weight, gain):
    groups = starts.shape[0]
    total, cols, chans = partial.shape
    return pl.pallas_call(
        late_kernel,
        out_shape=jax.ShapeDtypeStruct((groups, FMAX, cols, chans), jnp.bfloat16),
        in_specs=[SMEM_SPEC] + [VMEM_SPEC] * 6,
        out_specs=HBM_SPEC,
        scratch_shapes=far_scratch(*far.shape)
        + [
            pltpu.VMEM((total + FMAX, cols, chans), jnp.bfloat16),
            pltpu.SemaphoreType.DMA,
            pltpu.SemaphoreType.DMA((groups,)),
        ],
        compiler_params=pltpu.CompilerParams(vmem_limit_bytes=VMEM_BYTES),
    )(starts, early_far, far, early, partial, weight, gain)


def unpack_kernel(total, starts, arrived, out, blank, sems):
    groups = starts.shape[0]
    group = lax.axis_index("tc") * lax.axis_size("core") + lax.axis_index("core")
    after = jnp.where(group + 1 < groups, starts[jnp.minimum(group + 1, groups - 1)], total)
    length = after - starts[group]
    blank[...] = jnp.zeros(blank.shape, blank.dtype)
    for k in range(FMAX):

        @pl.when(k < length)
        def _():
            pltpu.make_async_copy(arrived.at[:, k], out.at[k], sems.at[k]).start()

        @pl.when(k >= length)
        def _():
            pltpu.make_async_copy(blank, out.at[k], sems.at[k]).start()

    for k in range(FMAX):
        pltpu.make_async_copy(blank, out.at[k], sems.at[k]).wait()


def unpack(total, starts, arrived):
    rows, _, cols, chans = arrived.shape
    return pl.pallas_call(
        functools.partial(unpack_kernel, total),
        out_shape=jax.ShapeDtypeStruct((FMAX, rows, cols, chans), arrived.dtype),
        in_specs=[SMEM_SPEC, VMEM_SPEC],
        out_specs=HBM_SPEC,
        scratch_shapes=[
            pltpu.VMEM((rows, cols, chans), arrived.dtype),
            pltpu.SemaphoreType.DMA((FMAX,)),
        ],
    )(starts, arrived)


def on_device(latent, group_start, norm_gain, conv_weight, conv_bias):
    total = latent.shape[0]
    own = latent[:, 0]
    rows = lax.axis_size("ha") * lax.axis_size("tc") * lax.axis_size("core")
    gain = norm_gain.reshape(1, -1)
    bias = conv_bias.reshape(1, -1)
    pairs = [(r, (r + 1) % rows if r % 2 else (r - 1) % rows) for r in range(rows)]
    cut = total * 5 // 8
    early_far = lax.ppermute(own[:cut], ("ha", "tc", "core"), pairs)
    late_far = lax.ppermute(own[cut:], ("ha", "tc", "core"), pairs)
    twin = lax.ppermute(own, "core", [(0, 1), (1, 0)])
    partial = near_rows(own, twin, conv_weight, gain, bias)
    early = early_rows(early_far, partial, conv_weight, gain)
    packed = late_rows(group_start, early_far, late_far, early, partial, conv_weight, gain)
    arrived = lax.all_to_all(packed, ("tc", "core"), split_axis=0, concat_axis=0, tiled=True)
    return unpack(total, group_start, arrived)


def solution(mesh):
    devices = mesh.devices
    fine = Mesh(
        devices.reshape(devices.shape[0], devices.shape[1] // 2, 2), ("ha", "tc", "core")
    )
    placed = (P(None, ("ha", "tc", "core"), None, None), P(), P(), P(), P())
    return jax.shard_map(
        on_device,
        mesh=fine,
        in_specs=placed,
        out_specs=P(("tc", "core"), "ha", None, None),
        check_vma=False,
    )
```

```python
import functools

import jax
import jax.numpy as jnp
from jax import lax
from jax.experimental import pallas as pl
from jax.experimental.pallas import tpu as pltpu
from jax.sharding import Mesh, PartitionSpec as P

FMAX = 4
HIST = 2
STEP = 8
VMEM_BYTES = 30 * 2**20
UNPACK_VMEM_BYTES = 8 * 2**20
SMEM_SPEC = pl.BlockSpec(memory_space=pltpu.SMEM)
VMEM_SPEC = pl.BlockSpec(memory_space=pltpu.VMEM)
HBM_SPEC = pl.BlockSpec(memory_space=pltpu.HBM)


def activate(raw, gain):
    wide = raw.astype(jnp.float32)
    power = jnp.mean(wide * wide, axis=-1, keepdims=True)
    half = wide * lax.rsqrt(power + 1e-06) * (0.5 * gain)
    return (half + half * jnp.tanh(half)).astype(jnp.bfloat16)


def taps_of(weight, row_taps):
    return jnp.concatenate(
        [
            jnp.concatenate([weight[a, b, e] for e in range(3)], axis=1)
            for b in row_taps
            for a in range(3)
        ],
        axis=0,
    )


def convolve(acts, first, count, weight, row_taps, sums):
    cols, chans = acts[0].shape[1:]
    lhs = jnp.concatenate(
        [
            act[pl.ds(first + a, count)].reshape(count * cols, chans)
            for act in acts
            for a in range(3)
        ],
        axis=1,
    )
    part = jnp.dot(lhs, taps_of(weight, row_taps), preferred_element_type=jnp.float32)
    for e in range(3):
        sums[e, pl.ds(0, count), 8 : cols + 8, :] = part[:, e * chans : (e + 1) * chans].reshape(
            count, cols, chans
        )
    return (
        sums[0, pl.ds(0, count), 7 : cols + 7, :]
        + sums[1, pl.ds(0, count), 8 : cols + 8, :]
        + sums[2, pl.ds(0, count), 9 : cols + 9, :]
    )


def clear_sides(sums, cols):
    shape = (sums.shape[1], 1, sums.shape[3])
    sums[0, :, 7:8, :] = jnp.zeros(shape, jnp.float32)
    sums[2, :, cols + 8 : cols + 9, :] = jnp.zeros(shape, jnp.float32)


def near_kernel(own, twin, weight, gain, bias, partial, own_act, twin_act, sums):
    total, cols, _ = own.shape
    core = lax.axis_index("core")
    clear_sides(sums, cols)
    for act in (own_act, twin_act):
        act[pl.ds(0, HIST)] = jnp.zeros((HIST,) + act.shape[1:], act.dtype)

    def prepare(i, carry):
        frames = pl.ds(i * STEP, STEP)
        later = pl.ds(i * STEP + HIST, STEP)
        own_act[later] = activate(own[frames], gain[...])
        twin_act[later] = activate(twin[frames], gain[...])
        return carry

    lax.fori_loop(0, total // STEP, prepare, 0)

    def step(i, carry):
        frames = pl.ds(i * STEP, STEP)
        convolved = convolve(
            (own_act, twin_act), i * STEP, STEP, weight, (1, 2 * (1 - core)), sums
        )
        partial[frames] = own[frames].astype(jnp.float32) + convolved + bias[...]
        return carry

    lax.fori_loop(0, total // STEP, step, 0)


def near_rows(own, twin, weight, gain, bias):
    total, cols, chans = own.shape
    return pl.pallas_call(
        near_kernel,
        out_shape=jax.ShapeDtypeStruct(own.shape, jnp.float32),
        in_specs=[VMEM_SPEC] * 5,
        out_specs=VMEM_SPEC,
        scratch_shapes=[
            pltpu.VMEM((HIST + total, cols, chans), jnp.bfloat16),
            pltpu.VMEM((HIST + total, cols, chans), jnp.bfloat16),
            pltpu.VMEM((3, STEP, cols + 16, chans), jnp.float32),
        ],
        compiler_params=pltpu.CompilerParams(vmem_limit_bytes=VMEM_BYTES),
    )(own, twin, weight, gain, bias)


def far_frames(begin, far, recent, partial, weight, gain, act, sums):
    count, cols, chans = far.shape
    core = lax.axis_index("core")
    row = lax.axis_index("ha") * lax.axis_size("tc") + lax.axis_index("tc")
    row = row * lax.axis_size("core") + core
    rows = lax.axis_size("ha") * lax.axis_size("tc") * lax.axis_size("core")
    clear_sides(sums, cols)
    if recent is None:
        act[pl.ds(0, HIST)] = jnp.zeros((HIST, cols, chans), act.dtype)
    else:
        act[pl.ds(0, HIST)] = activate(recent[pl.ds(recent.shape[0] - HIST, HIST)], gain[...])
    act[pl.ds(HIST, count)] = activate(far[...], gain[...])

    @pl.when(jnp.logical_or(row == 0, row == rows - 1))
    def _():
        act[...] = jnp.zeros(act.shape, act.dtype)

    convolved = convolve((act,), 0, count, weight, (2 * core,), sums)
    return (partial[pl.ds(begin, count)] + convolved).astype(jnp.bfloat16)


def early_kernel(far, partial, weight, gain, out, act, sums):
    out[...] = far_frames(0, far, None, partial, weight, gain, act, sums)


def late_kernel(starts, early_far, far, early, partial, weight, gain, packed,
                act, sums, result, sems):
    cut = early.shape[0]
    count, cols, chans = far.shape
    groups = packed.shape[0]
    ready = [
        pltpu.make_async_copy(
            early.at[pl.ds(jnp.clip(starts[j], 0, cut - FMAX), FMAX)], packed.at[j], sems.at[j]
        )
        for j in range(groups)
    ]
    for j in range(groups):
        pl.when(starts[j] + FMAX <= cut)(ready[j].start)
    result[pl.ds(0, FMAX)] = early[pl.ds(cut - FMAX, FMAX)]
    result[pl.ds(FMAX + count, FMAX)] = jnp.zeros((FMAX, cols, chans), result.dtype)
    result[pl.ds(FMAX, count)] = far_frames(
        cut, far, early_far, partial, weight, gain, act, sums
    )
    for j in range(groups):
        index = jnp.clip(starts[j] - (cut - FMAX), 0, FMAX + count)
        copy = pltpu.make_async_copy(
            result.at[pl.ds(index, FMAX)], packed.at[j], sems.at[j]
        )
        pl.when(starts[j] + FMAX > cut)(copy.start)
    for copy in ready:
        copy.wait()


def far_scratch(count, cols, chans):
    return [
        pltpu.VMEM((HIST + count, cols, chans), jnp.bfloat16),
        pltpu.VMEM((3, count, cols + 16, chans), jnp.float32),
    ]


def early_rows(far, partial, weight, gain):
    return pl.pallas_call(
        early_kernel,
        out_shape=jax.ShapeDtypeStruct(far.shape, jnp.bfloat16),
        in_specs=[VMEM_SPEC] * 4,
        out_specs=VMEM_SPEC,
        scratch_shapes=far_scratch(*far.shape),
        compiler_params=pltpu.CompilerParams(vmem_limit_bytes=VMEM_BYTES),
    )(far, partial, weight, gain)


def late_rows(starts, early_far, far, early, partial, weight, gain):
    groups = starts.shape[0]
    count, cols, chans = far.shape
    return pl.pallas_call(
        late_kernel,
        out_shape=jax.ShapeDtypeStruct((groups, FMAX, cols, chans), jnp.bfloat16),
        in_specs=[SMEM_SPEC] + [VMEM_SPEC] * 6,
        out_specs=HBM_SPEC,
        scratch_shapes=far_scratch(*far.shape)
        + [
            pltpu.VMEM((FMAX + count + FMAX, cols, chans), jnp.bfloat16),
            pltpu.SemaphoreType.DMA((groups,)),
        ],
        compiler_params=pltpu.CompilerParams(vmem_limit_bytes=VMEM_BYTES),
    )(starts, early_far, far, early, partial, weight, gain)


def unpack_kernel(total, starts, arrived, out, blank, sems):
    groups = starts.shape[0]
    group = lax.axis_index("tc") * lax.axis_size("core") + lax.axis_index("core")
    after = jnp.where(group + 1 < groups, starts[jnp.minimum(group + 1, groups - 1)], total)
    length = after - starts[group]
    blank[...] = jnp.zeros(blank.shape, blank.dtype)
    for k in range(FMAX):

        @pl.when(k < length)
        def _():
            pltpu.make_async_copy(arrived.at[:, k], out.at[k], sems.at[k]).start()

        @pl.when(k >= length)
        def _():
            pltpu.make_async_copy(blank, out.at[k], sems.at[k]).start()

    for k in range(FMAX):
        pltpu.make_async_copy(blank, out.at[k], sems.at[k]).wait()


def unpack(total, starts, arrived):
    rows, _, cols, chans = arrived.shape
    return pl.pallas_call(
        functools.partial(unpack_kernel, total),
        out_shape=jax.ShapeDtypeStruct((FMAX, rows, cols, chans), arrived.dtype),
        in_specs=[SMEM_SPEC, VMEM_SPEC],
        out_specs=HBM_SPEC,
        scratch_shapes=[
            pltpu.VMEM((rows, cols, chans), arrived.dtype),
            pltpu.SemaphoreType.DMA((FMAX,)),
        ],
        compiler_params=pltpu.CompilerParams(vmem_limit_bytes=UNPACK_VMEM_BYTES),
    )(starts, arrived)


def on_device(latent, group_start, norm_gain, conv_weight, conv_bias):
    total = latent.shape[0]
    own = latent[:, 0]
    rows = lax.axis_size("ha") * lax.axis_size("tc") * lax.axis_size("core")
    gain = norm_gain.reshape(1, -1)
    bias = conv_bias.reshape(1, -1)
    pairs = [(r, (r + 1) % rows if r % 2 else (r - 1) % rows) for r in range(rows)]
    cut = total * 5 // 8
    front, own = lax.optimization_barrier((own[:cut], own))
    early_far = lax.ppermute(front, ("ha", "tc", "core"), pairs)
    late_far = lax.ppermute(own[cut:], ("ha", "tc", "core"), pairs)
    twin = lax.ppermute(own, "core", [(0, 1), (1, 0)])
    partial = near_rows(own, twin, conv_weight, gain, bias)
    early = early_rows(early_far, partial, conv_weight, gain)
    packed = late_rows(group_start, early_far, late_far, early, partial, conv_weight, gain)
    arrived = lax.all_to_all(packed, ("tc", "core"), split_axis=0, concat_axis=0, tiled=True)
    return unpack(total, group_start, arrived)


def solution(mesh):
    devices = mesh.devices
    fine = Mesh(
        devices.reshape(devices.shape[0], devices.shape[1] // 2, 2), ("ha", "tc", "core")
    )
    placed = (P(None, ("ha", "tc", "core"), None, None), P(), P(), P(), P())
    return jax.shard_map(
        on_device,
        mesh=fine,
        in_specs=placed,
        out_specs=P(("tc", "core"), "ha", None, None),
        check_vma=False,
    )
```

```python
import functools

import jax
import jax.numpy as jnp
from jax import lax
from jax.experimental import pallas as pl
from jax.experimental.pallas import tpu as pltpu
from jax.sharding import Mesh, PartitionSpec as P

FMAX = 4
HIST = 2
STEP = 8
VMEM_BYTES = 30 * 2**20
UNPACK_VMEM_BYTES = 8 * 2**20
SMEM_SPEC = pl.BlockSpec(memory_space=pltpu.SMEM)
VMEM_SPEC = pl.BlockSpec(memory_space=pltpu.VMEM)
HBM_SPEC = pl.BlockSpec(memory_space=pltpu.HBM)


def activate(raw, gain):
    wide = raw.astype(jnp.float32)
    power = jnp.mean(wide * wide, axis=-1, keepdims=True)
    half = wide * lax.rsqrt(power + 1e-06) * (0.5 * gain)
    return (half + half * jnp.tanh(half)).astype(jnp.bfloat16)


def taps_of(weight, row_taps):
    return jnp.concatenate(
        [
            jnp.concatenate([weight[a, b, e] for e in range(3)], axis=1)
            for b in row_taps
            for a in range(3)
        ],
        axis=0,
    )


def convolve(acts, first, count, weight, row_taps, sums):
    cols, chans = acts[0].shape[1:]
    lhs = jnp.concatenate(
        [
            act[pl.ds(first + a, count)].reshape(count * cols, chans)
            for act in acts
            for a in range(3)
        ],
        axis=1,
    )
    part = jnp.dot(lhs, taps_of(weight, row_taps), preferred_element_type=jnp.float32)
    for e in range(3):
        sums[e, pl.ds(0, count), 8 : cols + 8, :] = part[:, e * chans : (e + 1) * chans].reshape(
            count, cols, chans
        )
    return (
        sums[0, pl.ds(0, count), 7 : cols + 7, :]
        + sums[1, pl.ds(0, count), 8 : cols + 8, :]
        + sums[2, pl.ds(0, count), 9 : cols + 9, :]
    )


def clear_sides(sums, cols):
    shape = (sums.shape[1], 1, sums.shape[3])
    sums[0, :, 7:8, :] = jnp.zeros(shape, jnp.float32)
    sums[2, :, cols + 8 : cols + 9, :] = jnp.zeros(shape, jnp.float32)


def near_kernel(own, twin, weight, gain, bias, partial, own_act, twin_act, sums):
    total, cols, _ = own.shape
    core = lax.axis_index("core")
    clear_sides(sums, cols)
    for act in (own_act, twin_act):
        act[pl.ds(0, HIST)] = jnp.zeros((HIST,) + act.shape[1:], act.dtype)

    def prepare(i, carry):
        frames = pl.ds(i * STEP, STEP)
        later = pl.ds(i * STEP + HIST, STEP)
        own_act[later] = activate(own[frames], gain[...])
        twin_act[later] = activate(twin[frames], gain[...])
        return carry

    lax.fori_loop(0, total // STEP, prepare, 0)

    def step(i, carry):
        frames = pl.ds(i * STEP, STEP)
        convolved = convolve(
            (own_act, twin_act), i * STEP, STEP, weight, (1, 2 * (1 - core)), sums
        )
        partial[frames] = own[frames].astype(jnp.float32) + convolved + bias[...]
        return carry

    lax.fori_loop(0, total // STEP, step, 0)


def near_rows(own, twin, weight, gain, bias):
    total, cols, chans = own.shape
    return pl.pallas_call(
        near_kernel,
        out_shape=jax.ShapeDtypeStruct(own.shape, jnp.float32),
        in_specs=[VMEM_SPEC] * 5,
        out_specs=VMEM_SPEC,
        scratch_shapes=[
            pltpu.VMEM((HIST + total, cols, chans), jnp.bfloat16),
            pltpu.VMEM((HIST + total, cols, chans), jnp.bfloat16),
            pltpu.VMEM((3, STEP, cols + 16, chans), jnp.float32),
        ],
        compiler_params=pltpu.CompilerParams(vmem_limit_bytes=VMEM_BYTES),
    )(own, twin, weight, gain, bias)


def far_frames(begin, far, recent, partial, weight, gain, act, sums):
    count, cols, chans = far.shape
    core = lax.axis_index("core")
    row = lax.axis_index("ha") * lax.axis_size("tc") + lax.axis_index("tc")
    row = row * lax.axis_size("core") + core
    rows = lax.axis_size("ha") * lax.axis_size("tc") * lax.axis_size("core")
    clear_sides(sums, cols)
    if recent is None:
        act[pl.ds(0, HIST)] = jnp.zeros((HIST, cols, chans), act.dtype)
    else:
        act[pl.ds(0, HIST)] = activate(recent[pl.ds(recent.shape[0] - HIST, HIST)], gain[...])
    act[pl.ds(HIST, count)] = activate(far[...], gain[...])

    @pl.when(jnp.logical_or(row == 0, row == rows - 1))
    def _():
        act[...] = jnp.zeros(act.shape, act.dtype)

    convolved = convolve((act,), 0, count, weight, (2 * core,), sums)
    return (partial[pl.ds(begin, count)] + convolved).astype(jnp.bfloat16)


def early_kernel(far, partial, weight, gain, out, act, sums):
    out[...] = far_frames(0, far, None, partial, weight, gain, act, sums)


def late_kernel(starts, early_far, far, early, partial, weight, gain, packed, act, sums, result):
    cut = early.shape[0]
    count, cols, chans = far.shape
    result[pl.ds(0, cut)] = early[...]
    result[pl.ds(cut + count, FMAX)] = jnp.zeros((FMAX, cols, chans), result.dtype)
    result[pl.ds(cut, count)] = far_frames(
        cut, far, early_far, partial, weight, gain, act, sums
    )
    for j in range(packed.shape[0]):
        packed[j] = result[pl.ds(jnp.clip(starts[j], 0, cut + count), FMAX)]


def far_scratch(count, cols, chans):
    return [
        pltpu.VMEM((HIST + count, cols, chans), jnp.bfloat16),
        pltpu.VMEM((3, count, cols + 16, chans), jnp.float32),
    ]


def early_rows(far, partial, weight, gain):
    return pl.pallas_call(
        early_kernel,
        out_shape=jax.ShapeDtypeStruct(far.shape, jnp.bfloat16),
        in_specs=[VMEM_SPEC] * 4,
        out_specs=VMEM_SPEC,
        scratch_shapes=far_scratch(*far.shape),
        compiler_params=pltpu.CompilerParams(vmem_limit_bytes=VMEM_BYTES),
    )(far, partial, weight, gain)


def late_rows(starts, early_far, far, early, partial, weight, gain):
    total, cols, chans = partial.shape
    return pl.pallas_call(
        late_kernel,
        out_shape=jax.ShapeDtypeStruct((starts.shape[0], FMAX, cols, chans), jnp.bfloat16),
        in_specs=[SMEM_SPEC] + [VMEM_SPEC] * 6,
        out_specs=VMEM_SPEC,
        scratch_shapes=far_scratch(*far.shape)
        + [pltpu.VMEM((total + FMAX, cols, chans), jnp.bfloat16)],
        compiler_params=pltpu.CompilerParams(vmem_limit_bytes=VMEM_BYTES),
    )(starts, early_far, far, early, partial, weight, gain)


def unpack_kernel(total, starts, arrived, out, blank, sems):
    groups = starts.shape[0]
    group = lax.axis_index("tc") * lax.axis_size("core") + lax.axis_index("core")
    after = jnp.where(group + 1 < groups, starts[jnp.minimum(group + 1, groups - 1)], total)
    length = after - starts[group]
    blank[...] = jnp.zeros(blank.shape, blank.dtype)
    for k in range(FMAX):

        @pl.when(k < length)
        def _():
            pltpu.make_async_copy(arrived.at[:, k], out.at[k], sems.at[k]).start()

        @pl.when(k >= length)
        def _():
            pltpu.make_async_copy(blank, out.at[k], sems.at[k]).start()

    for k in range(FMAX):
        pltpu.make_async_copy(blank, out.at[k], sems.at[k]).wait()


def unpack(total, starts, arrived):
    rows, _, cols, chans = arrived.shape
    return pl.pallas_call(
        functools.partial(unpack_kernel, total),
        out_shape=jax.ShapeDtypeStruct((FMAX, rows, cols, chans), arrived.dtype),
        in_specs=[SMEM_SPEC, VMEM_SPEC],
        out_specs=HBM_SPEC,
        scratch_shapes=[
            pltpu.VMEM((rows, cols, chans), arrived.dtype),
            pltpu.SemaphoreType.DMA((FMAX,)),
        ],
        compiler_params=pltpu.CompilerParams(vmem_limit_bytes=UNPACK_VMEM_BYTES),
    )(starts, arrived)


def on_device(latent, group_start, norm_gain, conv_weight, conv_bias):
    total = latent.shape[0]
    own = latent[:, 0]
    rows = lax.axis_size("ha") * lax.axis_size("tc") * lax.axis_size("core")
    gain = norm_gain.reshape(1, -1)
    bias = conv_bias.reshape(1, -1)
    pairs = [(r, (r + 1) % rows if r % 2 else (r - 1) % rows) for r in range(rows)]
    cut = total * 5 // 8
    front, rest = lax.optimization_barrier((own[:cut], own))
    back, rest = lax.optimization_barrier((rest[cut:], rest))
    early_far = lax.ppermute(front, ("ha", "tc", "core"), pairs)
    late_far = lax.ppermute(back, ("ha", "tc", "core"), pairs)
    twin = lax.ppermute(rest, "core", [(0, 1), (1, 0)])
    partial = near_rows(own, twin, conv_weight, gain, bias)
    early = early_rows(early_far, partial, conv_weight, gain)
    packed = late_rows(group_start, early_far, late_far, early, partial, conv_weight, gain)
    arrived = lax.all_to_all(packed, ("tc", "core"), split_axis=0, concat_axis=0, tiled=True)
    return unpack(total, group_start, arrived)


def solution(mesh):
    devices = mesh.devices
    fine = Mesh(
        devices.reshape(devices.shape[0], devices.shape[1] // 2, 2), ("ha", "tc", "core")
    )
    placed = (P(None, ("ha", "tc", "core"), None, None), P(), P(), P(), P())
    return jax.shard_map(
        on_device,
        mesh=fine,
        in_specs=placed,
        out_specs=P(("tc", "core"), "ha", None, None),
        check_vma=False,
    )
```

```python
import functools

import jax
import jax.numpy as jnp
from jax import lax
from jax.experimental import pallas as pl
from jax.experimental.pallas import tpu as pltpu
from jax.sharding import Mesh, PartitionSpec as P

FMAX = 4
HIST = 2
STEP = 8
VMEM_BYTES = 30 * 2**20
UNPACK_VMEM_BYTES = 8 * 2**20
SMEM_SPEC = pl.BlockSpec(memory_space=pltpu.SMEM)
VMEM_SPEC = pl.BlockSpec(memory_space=pltpu.VMEM)
HBM_SPEC = pl.BlockSpec(memory_space=pltpu.HBM)


def activate(raw, gain):
    wide = raw.astype(jnp.float32)
    power = jnp.mean(wide * wide, axis=-1, keepdims=True)
    half = wide * lax.rsqrt(power + 1e-06) * (0.5 * gain)
    return (half + half * jnp.tanh(half)).astype(jnp.bfloat16)


def taps_of(weight, row_taps):
    return jnp.concatenate(
        [
            jnp.concatenate([weight[a, b, e] for e in range(3)], axis=1)
            for b in row_taps
            for a in range(3)
        ],
        axis=0,
    )


def convolve(acts, first, count, weight, row_taps, sums):
    cols, chans = acts[0].shape[1:]
    lhs = jnp.concatenate(
        [
            act[pl.ds(first + a, count)].reshape(count * cols, chans)
            for act in acts
            for a in range(3)
        ],
        axis=1,
    )
    part = jnp.dot(lhs, taps_of(weight, row_taps), preferred_element_type=jnp.float32)
    for e in range(3):
        sums[e, pl.ds(0, count), 8 : cols + 8, :] = part[:, e * chans : (e + 1) * chans].reshape(
            count, cols, chans
        )
    return (
        sums[0, pl.ds(0, count), 7 : cols + 7, :]
        + sums[1, pl.ds(0, count), 8 : cols + 8, :]
        + sums[2, pl.ds(0, count), 9 : cols + 9, :]
    )


def clear_sides(sums, cols):
    shape = (sums.shape[1], 1, sums.shape[3])
    sums[0, :, 7:8, :] = jnp.zeros(shape, jnp.float32)
    sums[2, :, cols + 8 : cols + 9, :] = jnp.zeros(shape, jnp.float32)


def near_kernel(own, twin, weight, gain, bias, partial, own_act, twin_act, sums):
    total, cols, _ = own.shape
    core = lax.axis_index("core")
    clear_sides(sums, cols)
    for act in (own_act, twin_act):
        act[pl.ds(0, HIST)] = jnp.zeros((HIST,) + act.shape[1:], act.dtype)

    def prepare(i, carry):
        frames = pl.ds(i * STEP, STEP)
        later = pl.ds(i * STEP + HIST, STEP)
        own_act[later] = activate(own[frames], gain[...])
        twin_act[later] = activate(twin[frames], gain[...])
        return carry

    lax.fori_loop(0, total // STEP, prepare, 0)

    def step(i, carry):
        frames = pl.ds(i * STEP, STEP)
        convolved = convolve(
            (own_act, twin_act), i * STEP, STEP, weight, (1, 2 * (1 - core)), sums
        )
        partial[frames] = own[frames].astype(jnp.float32) + convolved + bias[...]
        return carry

    lax.fori_loop(0, total // STEP, step, 0)


def near_rows(own, twin, weight, gain, bias):
    total, cols, chans = own.shape
    return pl.pallas_call(
        near_kernel,
        out_shape=jax.ShapeDtypeStruct(own.shape, jnp.float32),
        in_specs=[VMEM_SPEC] * 5,
        out_specs=VMEM_SPEC,
        scratch_shapes=[
            pltpu.VMEM((HIST + total, cols, chans), jnp.bfloat16),
            pltpu.VMEM((HIST + total, cols, chans), jnp.bfloat16),
            pltpu.VMEM((3, STEP, cols + 16, chans), jnp.float32),
        ],
        compiler_params=pltpu.CompilerParams(vmem_limit_bytes=VMEM_BYTES),
    )(own, twin, weight, gain, bias)


def far_frames(begin, far, recent, partial, weight, gain, act, sums):
    count, cols, chans = far.shape
    core = lax.axis_index("core")
    row = lax.axis_index("ha") * lax.axis_size("tc") + lax.axis_index("tc")
    row = row * lax.axis_size("core") + core
    rows = lax.axis_size("ha") * lax.axis_size("tc") * lax.axis_size("core")
    clear_sides(sums, cols)
    if recent is None:
        act[pl.ds(0, HIST)] = jnp.zeros((HIST, cols, chans), act.dtype)
    else:
        act[pl.ds(0, HIST)] = activate(recent[pl.ds(recent.shape[0] - HIST, HIST)], gain[...])
    act[pl.ds(HIST, count)] = activate(far[...], gain[...])

    @pl.when(jnp.logical_or(row == 0, row == rows - 1))
    def _():
        act[...] = jnp.zeros(act.shape, act.dtype)

    convolved = convolve((act,), 0, count, weight, (2 * core,), sums)
    return (partial[pl.ds(begin, count)] + convolved).astype(jnp.bfloat16)


def early_kernel(far, partial, weight, gain, out, act, sums):
    out[...] = far_frames(0, far, None, partial, weight, gain, act, sums)


def after_of(starts, group, total):
    groups = starts.shape[0]
    return jnp.where(group + 1 < groups, starts[jnp.minimum(group + 1, groups - 1)], total)


def late_kernel(
    fits, starts, early_far, far, early, partial, weight, gain, few, many, act, sums, result
):
    cut = early.shape[0]
    count, cols, chans = far.shape
    result[pl.ds(0, cut)] = early[...]
    result[pl.ds(cut + count, FMAX)] = jnp.zeros((FMAX, cols, chans), result.dtype)
    result[pl.ds(cut, count)] = far_frames(
        cut, far, early_far, partial, weight, gain, act, sums
    )
    total = cut + count

    @pl.when(fits[0] == 0)
    def _():
        for j in range(many.shape[0]):
            many[j] = result[pl.ds(jnp.clip(starts[j], 0, total), FMAX)]

    @pl.when(fits[0] == 1)
    def _():
        slots = few.shape[1]
        for j in range(few.shape[0]):
            first = after_of(starts, j, total) - slots if j % 2 else starts[j]
            few[j] = result[pl.ds(jnp.clip(first, 0, total - slots), slots)]


def far_scratch(count, cols, chans):
    return [
        pltpu.VMEM((HIST + count, cols, chans), jnp.bfloat16),
        pltpu.VMEM((3, count, cols + 16, chans), jnp.float32),
    ]


def early_rows(far, partial, weight, gain):
    return pl.pallas_call(
        early_kernel,
        out_shape=jax.ShapeDtypeStruct(far.shape, jnp.bfloat16),
        in_specs=[VMEM_SPEC] * 4,
        out_specs=VMEM_SPEC,
        scratch_shapes=far_scratch(*far.shape),
        compiler_params=pltpu.CompilerParams(vmem_limit_bytes=VMEM_BYTES),
    )(far, partial, weight, gain)


def late_rows(fits, starts, early_far, far, early, partial, weight, gain):
    total, cols, chans = partial.shape
    return pl.pallas_call(
        late_kernel,
        out_shape=[
            jax.ShapeDtypeStruct((starts.shape[0], slots, cols, chans), jnp.bfloat16)
            for slots in (FMAX - 1, FMAX)
        ],
        in_specs=[SMEM_SPEC] * 2 + [VMEM_SPEC] * 6,
        out_specs=[VMEM_SPEC] * 2,
        scratch_shapes=far_scratch(*far.shape)
        + [pltpu.VMEM((total + FMAX, cols, chans), jnp.bfloat16)],
        compiler_params=pltpu.CompilerParams(vmem_limit_bytes=VMEM_BYTES),
    )(fits, starts, early_far, far, early, partial, weight, gain)


def unpack_kernel(total, starts, arrived, other, out):
    slots = arrived.shape[1]
    core = lax.axis_index("core")
    group = lax.axis_index("tc") * lax.axis_size("core") + core
    start = starts[group]
    after = after_of(starts, group, total)
    length = after - start
    held = start
    if slots < FMAX:
        held = jnp.clip(jnp.where(core == 1, after - slots, start), 0, total - slots)
    for k in range(FMAX):
        slot = start + k - held
        inside = jnp.logical_and(slot >= 0, slot < slots)

        @pl.when(jnp.logical_and(k < length, inside))
        def _():
            out[k] = arrived[:, jnp.clip(slot, 0, slots - 1)]

        @pl.when(jnp.logical_and(k < length, jnp.logical_not(inside)))
        def _():
            out[k] = other[:, 0]

        @pl.when(k >= length)
        def _():
            out[k] = jnp.zeros(out.shape[1:], out.dtype)


def unpack(total, starts, arrived, other):
    rows, _, cols, chans = arrived.shape
    return pl.pallas_call(
        functools.partial(unpack_kernel, total),
        out_shape=jax.ShapeDtypeStruct((FMAX, rows, cols, chans), arrived.dtype),
        in_specs=[SMEM_SPEC, VMEM_SPEC, VMEM_SPEC],
        out_specs=VMEM_SPEC,
        compiler_params=pltpu.CompilerParams(vmem_limit_bytes=UNPACK_VMEM_BYTES),
    )(starts, arrived, other)


def regroup(packed):
    return lax.all_to_all(packed, ("tc", "core"), split_axis=0, concat_axis=0, tiled=True)


def send_few(total, few, many, starts):
    del many
    slots = few.shape[1]
    arrived = regroup(few)
    chip, core = lax.axis_index("tc"), lax.axis_index("core")
    begin = starts[2 * chip]
    held = after_of(starts, 2 * chip + 1, total) - begin
    wanted = jnp.where(core == 0, held - slots - 1, 2 * slots - held)
    sent = lax.dynamic_slice_in_dim(arrived, jnp.clip(wanted, 0, slots - 1), 1, 1)
    other = lax.ppermute(sent, "core", [(0, 1), (1, 0)])
    return unpack(total, starts, arrived, other)


def send_many(total, few, many, starts):
    del few
    arrived = regroup(many)
    return unpack(total, starts, arrived, arrived[:, :1])


def on_device(latent, group_start, norm_gain, conv_weight, conv_bias):
    total = latent.shape[0]
    own = latent[:, 0]
    rows = lax.axis_size("ha") * lax.axis_size("tc") * lax.axis_size("core")
    gain = norm_gain.reshape(1, -1)
    bias = conv_bias.reshape(1, -1)
    pairs = [(r, (r + 1) % rows if r % 2 else (r - 1) % rows) for r in range(rows)]
    cut = total * 11 // 16
    front, own = lax.optimization_barrier((own[:cut], own))
    early_far = lax.ppermute(front, ("ha", "tc", "core"), pairs)
    late_far = lax.ppermute(own[cut:], ("ha", "tc", "core"), pairs)
    twin = lax.ppermute(own, "core", [(0, 1), (1, 0)])
    partial = near_rows(own, twin, conv_weight, gain, bias)
    early = early_rows(early_far, partial, conv_weight, gain)
    bounds = jnp.append(group_start[:: lax.axis_size("core")], total)
    fits = jnp.all(bounds[1:] - bounds[:-1] <= 2 * (FMAX - 1)).astype(jnp.int32).reshape(1)
    few, many = late_rows(
        fits, group_start, early_far, late_far, early, partial, conv_weight, gain
    )
    return lax.switch(
        fits[0],
        [functools.partial(send_many, total), functools.partial(send_few, total)],
        few, many, group_start,
    )


def solution(mesh):
    devices = mesh.devices
    fine = Mesh(
        devices.reshape(devices.shape[0], devices.shape[1] // 2, 2), ("ha", "tc", "core")
    )
    placed = (P(None, ("ha", "tc", "core"), None, None), P(), P(), P(), P())
    return jax.shard_map(
        on_device,
        mesh=fine,
        in_specs=placed,
        out_specs=P(("tc", "core"), "ha", None, None),
        check_vma=False,
    )
```

```python
import functools

import jax
import jax.numpy as jnp
from jax import lax
from jax.experimental import pallas as pl
from jax.experimental.pallas import tpu as pltpu
from jax.sharding import Mesh, PartitionSpec as P

FMAX = 4
HIST = 2
STEP = 8
NEAR_VMEM_BYTES = 14 * 2**20
FAR_VMEM_BYTES = 20 * 2**20
UNPACK_VMEM_BYTES = 8 * 2**20
SMEM_SPEC = pl.BlockSpec(memory_space=pltpu.SMEM)
VMEM_SPEC = pl.BlockSpec(memory_space=pltpu.VMEM)
HBM_SPEC = pl.BlockSpec(memory_space=pltpu.HBM)


def activate(raw, gain):
    wide = raw.astype(jnp.float32)
    power = jnp.mean(wide * wide, axis=-1, keepdims=True)
    half = wide * lax.rsqrt(power + 1e-06) * (0.5 * gain)
    return (half + half * jnp.tanh(half)).astype(jnp.bfloat16)


def taps_of(weight, row_taps):
    return jnp.concatenate(
        [
            jnp.concatenate([weight[a, b, e] for e in range(3)], axis=1)
            for b in row_taps
            for a in range(3)
        ],
        axis=0,
    )


def convolve(acts, first, count, weight, row_taps, sums):
    cols, chans = acts[0].shape[1:]
    lhs = jnp.concatenate(
        [
            act[pl.ds(first + a, count)].reshape(count * cols, chans)
            for act in acts
            for a in range(3)
        ],
        axis=1,
    )
    part = jnp.dot(lhs, taps_of(weight, row_taps), preferred_element_type=jnp.float32)
    for e in range(3):
        sums[e, pl.ds(0, count), 8 : cols + 8, :] = part[:, e * chans : (e + 1) * chans].reshape(
            count, cols, chans
        )
    return (
        sums[0, pl.ds(0, count), 7 : cols + 7, :]
        + sums[1, pl.ds(0, count), 8 : cols + 8, :]
        + sums[2, pl.ds(0, count), 9 : cols + 9, :]
    )


def clear_sides(sums, cols):
    shape = (sums.shape[1], 1, sums.shape[3])
    sums[0, :, 7:8, :] = jnp.zeros(shape, jnp.float32)
    sums[2, :, cols + 8 : cols + 9, :] = jnp.zeros(shape, jnp.float32)


def near_kernel(own, twin, weight, gain, bias, partial, own_act, twin_act, sums):
    total, cols, _ = own.shape
    core = lax.axis_index("core")
    clear_sides(sums, cols)
    for act in (own_act, twin_act):
        act[pl.ds(0, HIST)] = jnp.zeros((HIST,) + act.shape[1:], act.dtype)

    def prepare(i, carry):
        frames = pl.ds(i * STEP, STEP)
        later = pl.ds(i * STEP + HIST, STEP)
        own_act[later] = activate(own[frames], gain[...])
        twin_act[later] = activate(twin[frames], gain[...])
        return carry

    lax.fori_loop(0, total // STEP, prepare, 0)

    def step(i, carry):
        frames = pl.ds(i * STEP, STEP)
        convolved = convolve(
            (own_act, twin_act), i * STEP, STEP, weight, (1, 2 * (1 - core)), sums
        )
        partial[frames] = own[frames].astype(jnp.float32) + convolved + bias[...]
        return carry

    lax.fori_loop(0, total // STEP, step, 0)


def near_rows(own, twin, weight, gain, bias):
    total, cols, chans = own.shape
    return pl.pallas_call(
        near_kernel,
        out_shape=jax.ShapeDtypeStruct(own.shape, jnp.float32),
        in_specs=[VMEM_SPEC] * 5,
        out_specs=VMEM_SPEC,
        scratch_shapes=[
            pltpu.VMEM((HIST + total, cols, chans), jnp.bfloat16),
            pltpu.VMEM((HIST + total, cols, chans), jnp.bfloat16),
            pltpu.VMEM((3, STEP, cols + 16, chans), jnp.float32),
        ],
        compiler_params=pltpu.CompilerParams(vmem_limit_bytes=NEAR_VMEM_BYTES),
    )(own, twin, weight, gain, bias)


def far_frames(begin, far, recent, partial, weight, gain, act, sums):
    count, cols, chans = far.shape
    core = lax.axis_index("core")
    row = lax.axis_index("ha") * lax.axis_size("tc") + lax.axis_index("tc")
    row = row * lax.axis_size("core") + core
    rows = lax.axis_size("ha") * lax.axis_size("tc") * lax.axis_size("core")
    clear_sides(sums, cols)
    if recent is None:
        act[pl.ds(0, HIST)] = jnp.zeros((HIST, cols, chans), act.dtype)
    else:
        act[pl.ds(0, HIST)] = activate(recent[pl.ds(recent.shape[0] - HIST, HIST)], gain[...])
    act[pl.ds(HIST, count)] = activate(far[...], gain[...])

    @pl.when(jnp.logical_or(row == 0, row == rows - 1))
    def _():
        act[...] = jnp.zeros(act.shape, act.dtype)

    convolved = convolve((act,), 0, count, weight, (2 * core,), sums)
    return (partial[pl.ds(begin, count)] + convolved).astype(jnp.bfloat16)


def early_kernel(far, partial, weight, gain, out, act, sums):
    out[...] = far_frames(0, far, None, partial, weight, gain, act, sums)


def after_of(starts, group, total):
    groups = starts.shape[0]
    return jnp.where(group + 1 < groups, starts[jnp.minimum(group + 1, groups - 1)], total)


def late_kernel(
    fits, starts, early_far, far, early, partial, weight, gain, few, many, act, sums, result
):
    cut = early.shape[0]
    count, cols, chans = far.shape
    result[pl.ds(0, cut)] = early[...]
    result[pl.ds(cut + count, FMAX)] = jnp.zeros((FMAX, cols, chans), result.dtype)
    result[pl.ds(cut, count)] = far_frames(
        cut, far, early_far, partial, weight, gain, act, sums
    )
    total = cut + count

    @pl.when(fits[0] == 0)
    def _():
        for j in range(many.shape[0]):
            many[j] = result[pl.ds(jnp.clip(starts[j], 0, total), FMAX)]

    @pl.when(fits[0] == 1)
    def _():
        slots = few.shape[1]
        for j in range(few.shape[0]):
            first = after_of(starts, j, total) - slots if j % 2 else starts[j]
            few[j] = result[pl.ds(jnp.clip(first, 0, total - slots), slots)]


def far_scratch(count, cols, chans):
    return [
        pltpu.VMEM((HIST + count, cols, chans), jnp.bfloat16),
        pltpu.VMEM((3, count, cols + 16, chans), jnp.float32),
    ]


def early_rows(far, partial, weight, gain):
    return pl.pallas_call(
        early_kernel,
        out_shape=jax.ShapeDtypeStruct(far.shape, jnp.bfloat16),
        in_specs=[VMEM_SPEC] * 4,
        out_specs=VMEM_SPEC,
        scratch_shapes=far_scratch(*far.shape),
        compiler_params=pltpu.CompilerParams(vmem_limit_bytes=FAR_VMEM_BYTES),
    )(far, partial, weight, gain)


def late_rows(fits, starts, early_far, far, early, partial, weight, gain):
    total, cols, chans = partial.shape
    return pl.pallas_call(
        late_kernel,
        out_shape=[
            jax.ShapeDtypeStruct((starts.shape[0], slots, cols, chans), jnp.bfloat16)
            for slots in (FMAX - 1, FMAX)
        ],
        in_specs=[SMEM_SPEC] * 2 + [VMEM_SPEC] * 6,
        out_specs=[VMEM_SPEC] * 2,
        scratch_shapes=far_scratch(*far.shape)
        + [pltpu.VMEM((total + FMAX, cols, chans), jnp.bfloat16)],
        compiler_params=pltpu.CompilerParams(vmem_limit_bytes=FAR_VMEM_BYTES),
    )(fits, starts, early_far, far, early, partial, weight, gain)


def unpack_kernel(total, starts, arrived, other, out):
    slots = arrived.shape[1]
    core = lax.axis_index("core")
    group = lax.axis_index("tc") * lax.axis_size("core") + core
    start = starts[group]
    after = after_of(starts, group, total)
    length = after - start
    held = start
    if slots < FMAX:
        held = jnp.clip(jnp.where(core == 1, after - slots, start), 0, total - slots)
    for k in range(FMAX):
        slot = start + k - held
        inside = jnp.logical_and(slot >= 0, slot < slots)

        @pl.when(jnp.logical_and(k < length, inside))
        def _():
            out[k] = arrived[:, jnp.clip(slot, 0, slots - 1)]

        @pl.when(jnp.logical_and(k < length, jnp.logical_not(inside)))
        def _():
            out[k] = other[:, 0]

        @pl.when(k >= length)
        def _():
            out[k] = jnp.zeros(out.shape[1:], out.dtype)


def unpack(total, starts, arrived, other):
    rows, _, cols, chans = arrived.shape
    return pl.pallas_call(
        functools.partial(unpack_kernel, total),
        out_shape=jax.ShapeDtypeStruct((FMAX, rows, cols, chans), arrived.dtype),
        in_specs=[SMEM_SPEC, VMEM_SPEC, VMEM_SPEC],
        out_specs=VMEM_SPEC,
        compiler_params=pltpu.CompilerParams(vmem_limit_bytes=UNPACK_VMEM_BYTES),
    )(starts, arrived, other)


def regroup(packed):
    return lax.all_to_all(packed, ("tc", "core"), split_axis=0, concat_axis=0, tiled=True)


def send_few(total, few, many, starts):
    del many
    slots = few.shape[1]
    arrived = regroup(few)
    chip, core = lax.axis_index("tc"), lax.axis_index("core")
    begin = starts[2 * chip]
    held = after_of(starts, 2 * chip + 1, total) - begin
    wanted = jnp.where(core == 0, held - slots - 1, 2 * slots - held)
    sent = lax.dynamic_slice_in_dim(arrived, jnp.clip(wanted, 0, slots - 1), 1, 1)
    other = lax.ppermute(sent, "core", [(0, 1), (1, 0)])
    return unpack(total, starts, arrived, other)


def send_many(total, few, many, starts):
    del few
    arrived = regroup(many)
    return unpack(total, starts, arrived, arrived[:, :1])


def on_device(latent, group_start, norm_gain, conv_weight, conv_bias):
    total = latent.shape[0]
    own = latent[:, 0]
    rows = lax.axis_size("ha") * lax.axis_size("tc") * lax.axis_size("core")
    gain = norm_gain.reshape(1, -1)
    bias = conv_bias.reshape(1, -1)
    pairs = [(r, (r + 1) % rows if r % 2 else (r - 1) % rows) for r in range(rows)]
    cut = total * 5 // 8
    front, own = lax.optimization_barrier((own[:cut], own))
    early_far = lax.ppermute(front, ("ha", "tc", "core"), pairs)
    late_far = lax.ppermute(own[cut:], ("ha", "tc", "core"), pairs)
    twin = lax.ppermute(own, "core", [(0, 1), (1, 0)])
    partial = near_rows(own, twin, conv_weight, gain, bias)
    early = early_rows(early_far, partial, conv_weight, gain)
    bounds = jnp.append(group_start[:: lax.axis_size("core")], total)
    fits = jnp.all(bounds[1:] - bounds[:-1] <= 2 * (FMAX - 1)).astype(jnp.int32).reshape(1)
    few, many = late_rows(
        fits, group_start, early_far, late_far, early, partial, conv_weight, gain
    )
    return lax.switch(
        fits[0],
        [functools.partial(send_many, total), functools.partial(send_few, total)],
        few, many, group_start,
    )


def solution(mesh):
    devices = mesh.devices
    fine = Mesh(
        devices.reshape(devices.shape[0], devices.shape[1] // 2, 2), ("ha", "tc", "core")
    )
    placed = (P(None, ("ha", "tc", "core"), None, None), P(), P(), P(), P())
    return jax.shard_map(
        on_device,
        mesh=fine,
        in_specs=placed,
        out_specs=P(("tc", "core"), "ha", None, None),
        check_vma=False,
    )
```

```python
import functools

import jax
import jax.numpy as jnp
from jax import lax
from jax.experimental import pallas as pl
from jax.experimental.pallas import tpu as pltpu
from jax.sharding import Mesh, PartitionSpec as P

FMAX = 4
HIST = 2
STEP = 8
NEAR_VMEM_BYTES = 14 * 2**20
FAR_VMEM_BYTES = 20 * 2**20
UNPACK_VMEM_BYTES = 8 * 2**20
SMEM_SPEC = pl.BlockSpec(memory_space=pltpu.SMEM)
VMEM_SPEC = pl.BlockSpec(memory_space=pltpu.VMEM)
HBM_SPEC = pl.BlockSpec(memory_space=pltpu.HBM)


def activate(raw, gain):
    wide = raw.astype(jnp.float32)
    power = jnp.mean(wide * wide, axis=-1, keepdims=True)
    half = wide * lax.rsqrt(power + 1e-06) * (0.5 * gain)
    return (half + half * jnp.tanh(half)).astype(jnp.bfloat16)


def taps_of(weight, row_taps):
    return jnp.concatenate(
        [
            jnp.concatenate([weight[a, b, e] for e in range(3)], axis=1)
            for b in row_taps
            for a in range(3)
        ],
        axis=0,
    )


def convolve(acts, first, count, weight, row_taps, sums):
    cols, chans = acts[0].shape[1:]
    lhs = jnp.concatenate(
        [
            act[pl.ds(first + a, count)].reshape(count * cols, chans)
            for act in acts
            for a in range(3)
        ],
        axis=1,
    )
    part = jnp.dot(lhs, taps_of(weight, row_taps), preferred_element_type=jnp.float32)
    for e in range(3):
        sums[e, pl.ds(0, count), 8 : cols + 8, :] = part[:, e * chans : (e + 1) * chans].reshape(
            count, cols, chans
        )
    return (
        sums[0, pl.ds(0, count), 7 : cols + 7, :]
        + sums[1, pl.ds(0, count), 8 : cols + 8, :]
        + sums[2, pl.ds(0, count), 9 : cols + 9, :]
    )


def clear_sides(sums, cols):
    shape = (sums.shape[1], 1, sums.shape[3])
    sums[0, :, 7:8, :] = jnp.zeros(shape, jnp.float32)
    sums[2, :, cols + 8 : cols + 9, :] = jnp.zeros(shape, jnp.float32)


def near_kernel(
    starts, own, twin, weight, gain, bias, partial, fits, own_act, twin_act, sums
):
    total, cols, _ = own.shape
    core = lax.axis_index("core")
    groups = starts.shape[0]
    most = functools.reduce(
        jnp.maximum,
        [after_of(starts, j + 1, total) - starts[j] for j in range(0, groups, 2)],
    )
    fits[0] = (most <= 2 * (FMAX - 1)).astype(jnp.int32)
    clear_sides(sums, cols)
    for act in (own_act, twin_act):
        act[pl.ds(0, HIST)] = jnp.zeros((HIST,) + act.shape[1:], act.dtype)

    def prepare(i, carry):
        frames = pl.ds(i * STEP, STEP)
        later = pl.ds(i * STEP + HIST, STEP)
        own_act[later] = activate(own[frames], gain[...])
        twin_act[later] = activate(twin[frames], gain[...])
        return carry

    lax.fori_loop(0, total // STEP, prepare, 0)

    def step(i, carry):
        frames = pl.ds(i * STEP, STEP)
        convolved = convolve(
            (own_act, twin_act), i * STEP, STEP, weight, (1, 2 * (1 - core)), sums
        )
        partial[frames] = own[frames].astype(jnp.float32) + convolved + bias[...]
        return carry

    lax.fori_loop(0, total // STEP, step, 0)


def near_rows(starts, own, twin, weight, gain, bias):
    total, cols, chans = own.shape
    return pl.pallas_call(
        near_kernel,
        out_shape=[
            jax.ShapeDtypeStruct(own.shape, jnp.float32),
            jax.ShapeDtypeStruct((1,), jnp.int32),
        ],
        in_specs=[SMEM_SPEC] + [VMEM_SPEC] * 5,
        out_specs=[VMEM_SPEC, SMEM_SPEC],
        scratch_shapes=[
            pltpu.VMEM((HIST + total, cols, chans), jnp.bfloat16),
            pltpu.VMEM((HIST + total, cols, chans), jnp.bfloat16),
            pltpu.VMEM((3, STEP, cols + 16, chans), jnp.float32),
        ],
        compiler_params=pltpu.CompilerParams(vmem_limit_bytes=NEAR_VMEM_BYTES),
    )(starts, own, twin, weight, gain, bias)


def far_frames(begin, far, recent, partial, weight, gain, act, sums):
    count, cols, chans = far.shape
    core = lax.axis_index("core")
    row = lax.axis_index("ha") * lax.axis_size("tc") + lax.axis_index("tc")
    row = row * lax.axis_size("core") + core
    rows = lax.axis_size("ha") * lax.axis_size("tc") * lax.axis_size("core")
    clear_sides(sums, cols)
    if recent is None:
        act[pl.ds(0, HIST)] = jnp.zeros((HIST, cols, chans), act.dtype)
    else:
        act[pl.ds(0, HIST)] = activate(recent[pl.ds(recent.shape[0] - HIST, HIST)], gain[...])
    act[pl.ds(HIST, count)] = activate(far[...], gain[...])

    @pl.when(jnp.logical_or(row == 0, row == rows - 1))
    def _():
        act[...] = jnp.zeros(act.shape, act.dtype)

    convolved = convolve((act,), 0, count, weight, (2 * core,), sums)
    return (partial[pl.ds(begin, count)] + convolved).astype(jnp.bfloat16)


def early_kernel(far, partial, weight, gain, out, act, sums):
    out[...] = far_frames(0, far, None, partial, weight, gain, act, sums)


def after_of(starts, group, total):
    groups = starts.shape[0]
    return jnp.where(group + 1 < groups, starts[jnp.minimum(group + 1, groups - 1)], total)


def late_kernel(
    fits, starts, early_far, far, early, partial, weight, gain, few, many, act, sums, result
):
    cut = early.shape[0]
    count, cols, chans = far.shape
    result[pl.ds(0, cut)] = early[...]
    result[pl.ds(cut + count, FMAX)] = jnp.zeros((FMAX, cols, chans), result.dtype)
    result[pl.ds(cut, count)] = far_frames(
        cut, far, early_far, partial, weight, gain, act, sums
    )
    total = cut + count

    @pl.when(fits[0] == 0)
    def _():
        for j in range(many.shape[0]):
            many[j] = result[pl.ds(jnp.clip(starts[j], 0, total), FMAX)]

    @pl.when(fits[0] == 1)
    def _():
        slots = few.shape[1]
        for j in range(few.shape[0]):
            first = after_of(starts, j, total) - slots if j % 2 else starts[j]
            few[j] = result[pl.ds(jnp.clip(first, 0, total - slots), slots)]


def far_scratch(count, cols, chans):
    return [
        pltpu.VMEM((HIST + count, cols, chans), jnp.bfloat16),
        pltpu.VMEM((3, count, cols + 16, chans), jnp.float32),
    ]


def early_rows(far, partial, weight, gain):
    return pl.pallas_call(
        early_kernel,
        out_shape=jax.ShapeDtypeStruct(far.shape, jnp.bfloat16),
        in_specs=[VMEM_SPEC] * 4,
        out_specs=VMEM_SPEC,
        scratch_shapes=far_scratch(*far.shape),
        compiler_params=pltpu.CompilerParams(vmem_limit_bytes=FAR_VMEM_BYTES),
    )(far, partial, weight, gain)


def late_rows(fits, starts, early_far, far, early, partial, weight, gain):
    total, cols, chans = partial.shape
    return pl.pallas_call(
        late_kernel,
        out_shape=[
            jax.ShapeDtypeStruct((starts.shape[0], slots, cols, chans), jnp.bfloat16)
            for slots in (FMAX - 1, FMAX)
        ],
        in_specs=[SMEM_SPEC] * 2 + [VMEM_SPEC] * 6,
        out_specs=[VMEM_SPEC] * 2,
        scratch_shapes=far_scratch(*far.shape)
        + [pltpu.VMEM((total + FMAX, cols, chans), jnp.bfloat16)],
        compiler_params=pltpu.CompilerParams(vmem_limit_bytes=FAR_VMEM_BYTES),
    )(fits, starts, early_far, far, early, partial, weight, gain)


def unpack_kernel(total, starts, arrived, other, out):
    slots = arrived.shape[1]
    core = lax.axis_index("core")
    group = lax.axis_index("tc") * lax.axis_size("core") + core
    start = starts[group]
    after = after_of(starts, group, total)
    length = after - start
    held = start
    if slots < FMAX:
        held = jnp.clip(jnp.where(core == 1, after - slots, start), 0, total - slots)
    for k in range(FMAX):
        slot = start + k - held
        inside = jnp.logical_and(slot >= 0, slot < slots)

        @pl.when(jnp.logical_and(k < length, inside))
        def _():
            out[k] = arrived[:, jnp.clip(slot, 0, slots - 1)]

        @pl.when(jnp.logical_and(k < length, jnp.logical_not(inside)))
        def _():
            out[k] = other[:, 0]

        @pl.when(k >= length)
        def _():
            out[k] = jnp.zeros(out.shape[1:], out.dtype)


def unpack(total, starts, arrived, other):
    rows, _, cols, chans = arrived.shape
    return pl.pallas_call(
        functools.partial(unpack_kernel, total),
        out_shape=jax.ShapeDtypeStruct((FMAX, rows, cols, chans), arrived.dtype),
        in_specs=[SMEM_SPEC, VMEM_SPEC, VMEM_SPEC],
        out_specs=VMEM_SPEC,
        compiler_params=pltpu.CompilerParams(vmem_limit_bytes=UNPACK_VMEM_BYTES),
    )(starts, arrived, other)


def regroup(packed):
    return lax.all_to_all(packed, ("tc", "core"), split_axis=0, concat_axis=0, tiled=True)


def pick_kernel(total, starts, arrived, sent):
    slots = arrived.shape[1]
    core = lax.axis_index("core")
    group = lax.axis_index("tc") * lax.axis_size("core")
    held = after_of(starts, group + 1, total) - starts[group]
    wanted = jnp.where(core == 0, held - slots - 1, 2 * slots - held)
    sent[:, 0] = arrived[:, jnp.clip(wanted, 0, slots - 1)]


def pick(total, starts, arrived):
    rows, _, cols, chans = arrived.shape
    return pl.pallas_call(
        functools.partial(pick_kernel, total),
        out_shape=jax.ShapeDtypeStruct((rows, 1, cols, chans), arrived.dtype),
        in_specs=[SMEM_SPEC, VMEM_SPEC],
        out_specs=VMEM_SPEC,
        compiler_params=pltpu.CompilerParams(vmem_limit_bytes=UNPACK_VMEM_BYTES),
    )(starts, arrived)


def send_few(total, few, many, starts):
    del many
    arrived = regroup(few)
    other = lax.ppermute(pick(total, starts, arrived), "core", [(0, 1), (1, 0)])
    return unpack(total, starts, arrived, other)


def send_many(total, few, many, starts):
    del few
    arrived = regroup(many)
    return unpack(total, starts, arrived, arrived[:, :1])


def on_device(latent, group_start, norm_gain, conv_weight, conv_bias):
    total = latent.shape[0]
    own = latent[:, 0]
    rows = lax.axis_size("ha") * lax.axis_size("tc") * lax.axis_size("core")
    gain = norm_gain.reshape(1, -1)
    bias = conv_bias.reshape(1, -1)
    pairs = [(r, (r + 1) % rows if r % 2 else (r - 1) % rows) for r in range(rows)]
    cut = total * 5 // 8
    front, own = lax.optimization_barrier((own[:cut], own))
    early_far = lax.ppermute(front, ("ha", "tc", "core"), pairs)
    late_far = lax.ppermute(own[cut:], ("ha", "tc", "core"), pairs)
    twin = lax.ppermute(own, "core", [(0, 1), (1, 0)])
    partial, fits = near_rows(group_start, own, twin, conv_weight, gain, bias)
    early = early_rows(early_far, partial, conv_weight, gain)
    few, many = late_rows(
        fits, group_start, early_far, late_far, early, partial, conv_weight, gain
    )
    return lax.switch(
        fits[0],
        [functools.partial(send_many, total), functools.partial(send_few, total)],
        few, many, group_start,
    )


def solution(mesh):
    devices = mesh.devices
    fine = Mesh(
        devices.reshape(devices.shape[0], devices.shape[1] // 2, 2), ("ha", "tc", "core")
    )
    placed = (P(None, ("ha", "tc", "core"), None, None), P(), P(), P(), P())
    return jax.shard_map(
        on_device,
        mesh=fine,
        in_specs=placed,
        out_specs=P(("tc", "core"), "ha", None, None),
        check_vma=False,
    )
```

```python
import functools

import jax
import jax.numpy as jnp
from jax import lax
from jax.experimental import pallas as pl
from jax.experimental.pallas import tpu as pltpu
from jax.sharding import Mesh, PartitionSpec as P

FMAX = 4
HIST = 2
STEP = 8
NEAR_VMEM_BYTES = 14 * 2**20
FAR_VMEM_BYTES = 20 * 2**20
UNPACK_VMEM_BYTES = 8 * 2**20
SMEM_SPEC = pl.BlockSpec(memory_space=pltpu.SMEM)
VMEM_SPEC = pl.BlockSpec(memory_space=pltpu.VMEM)
HBM_SPEC = pl.BlockSpec(memory_space=pltpu.HBM)


def activate(raw, gain):
    wide = raw.astype(jnp.float32)
    power = jnp.mean(wide * wide, axis=-1, keepdims=True)
    half = wide * lax.rsqrt(power + 1e-06) * (0.5 * gain)
    return (half + half * jnp.tanh(half)).astype(jnp.bfloat16)


def taps_of(weight, row_taps):
    return jnp.concatenate(
        [
            jnp.concatenate([weight[a, b, e] for e in range(3)], axis=1)
            for b in row_taps
            for a in range(3)
        ],
        axis=0,
    )


def convolve(acts, first, count, weight, row_taps, sums):
    cols, chans = acts[0].shape[1:]
    lhs = jnp.concatenate(
        [
            act[pl.ds(first + a, count)].reshape(count * cols, chans)
            for act in acts
            for a in range(3)
        ],
        axis=1,
    )
    part = jnp.dot(lhs, taps_of(weight, row_taps), preferred_element_type=jnp.float32)
    for e in range(3):
        sums[e, pl.ds(0, count), 8 : cols + 8, :] = part[:, e * chans : (e + 1) * chans].reshape(
            count, cols, chans
        )
    return (
        sums[0, pl.ds(0, count), 7 : cols + 7, :]
        + sums[1, pl.ds(0, count), 8 : cols + 8, :]
        + sums[2, pl.ds(0, count), 9 : cols + 9, :]
    )


def clear_sides(sums, cols):
    shape = (sums.shape[1], 1, sums.shape[3])
    sums[0, :, 7:8, :] = jnp.zeros(shape, jnp.float32)
    sums[2, :, cols + 8 : cols + 9, :] = jnp.zeros(shape, jnp.float32)


def near_kernel(
    starts, own, twin, weight, gain, bias, partial, fits, own_act, twin_act, sums
):
    total, cols, _ = own.shape
    core = lax.axis_index("core")
    fits[0] = few_suffice(starts, total).astype(jnp.int32)
    clear_sides(sums, cols)
    for act in (own_act, twin_act):
        act[pl.ds(0, HIST)] = jnp.zeros((HIST,) + act.shape[1:], act.dtype)

    def prepare(i, carry):
        frames = pl.ds(i * STEP, STEP)
        later = pl.ds(i * STEP + HIST, STEP)
        own_act[later] = activate(own[frames], gain[...])
        twin_act[later] = activate(twin[frames], gain[...])
        return carry

    lax.fori_loop(0, total // STEP, prepare, 0)

    def step(i, carry):
        frames = pl.ds(i * STEP, STEP)
        convolved = convolve(
            (own_act, twin_act), i * STEP, STEP, weight, (1, 2 * (1 - core)), sums
        )
        partial[frames] = own[frames].astype(jnp.float32) + convolved + bias[...]
        return carry

    lax.fori_loop(0, total // STEP, step, 0)


def near_rows(starts, own, twin, weight, gain, bias):
    total, cols, chans = own.shape
    return pl.pallas_call(
        near_kernel,
        out_shape=[
            jax.ShapeDtypeStruct(own.shape, jnp.float32),
            jax.ShapeDtypeStruct((1,), jnp.int32),
        ],
        in_specs=[SMEM_SPEC] + [VMEM_SPEC] * 5,
        out_specs=[VMEM_SPEC, SMEM_SPEC],
        scratch_shapes=[
            pltpu.VMEM((HIST + total, cols, chans), jnp.bfloat16),
            pltpu.VMEM((HIST + total, cols, chans), jnp.bfloat16),
            pltpu.VMEM((3, STEP, cols + 16, chans), jnp.float32),
        ],
        compiler_params=pltpu.CompilerParams(vmem_limit_bytes=NEAR_VMEM_BYTES),
    )(starts, own, twin, weight, gain, bias)


def far_frames(begin, far, recent, partial, weight, gain, act, sums):
    count, cols, chans = far.shape
    core = lax.axis_index("core")
    row = lax.axis_index("ha") * lax.axis_size("tc") + lax.axis_index("tc")
    row = row * lax.axis_size("core") + core
    rows = lax.axis_size("ha") * lax.axis_size("tc") * lax.axis_size("core")
    clear_sides(sums, cols)
    if recent is None:
        act[pl.ds(0, HIST)] = jnp.zeros((HIST, cols, chans), act.dtype)
    else:
        act[pl.ds(0, HIST)] = activate(recent[pl.ds(recent.shape[0] - HIST, HIST)], gain[...])
    act[pl.ds(HIST, count)] = activate(far[...], gain[...])

    @pl.when(jnp.logical_or(row == 0, row == rows - 1))
    def _():
        act[...] = jnp.zeros(act.shape, act.dtype)

    convolved = convolve((act,), 0, count, weight, (2 * core,), sums)
    return (partial[pl.ds(begin, count)] + convolved).astype(jnp.bfloat16)


def first_kernel(far, partial, weight, gain, out, act, sums):
    out[...] = far_frames(0, far, None, partial, weight, gain, act, sums)


def second_kernel(recent, far, partial, weight, gain, out, act, sums):
    begin = recent.shape[0]
    out[...] = far_frames(begin, far, recent, partial, weight, gain, act, sums)


def after_of(starts, group, total):
    groups = starts.shape[0]
    return jnp.where(group + 1 < groups, starts[jnp.minimum(group + 1, groups - 1)], total)


def few_suffice(starts, total):
    most = functools.reduce(
        jnp.maximum,
        [after_of(starts, j + 1, total) - starts[j] for j in range(0, starts.shape[0], 2)],
    )
    return most <= 2 * (FMAX - 1)


def late_kernel(
    starts, recent, far, first, second, partial, weight, gain, few, many, act, sums, result
):
    cut = first.shape[0] + second.shape[0]
    count, cols, chans = far.shape
    result[pl.ds(0, first.shape[0])] = first[...]
    result[pl.ds(first.shape[0], second.shape[0])] = second[...]
    result[pl.ds(cut + count, FMAX)] = jnp.zeros((FMAX, cols, chans), result.dtype)
    result[pl.ds(cut, count)] = far_frames(
        cut, far, recent, partial, weight, gain, act, sums
    )
    total = cut + count
    enough = few_suffice(starts, total)

    @pl.when(jnp.logical_not(enough))
    def _():
        for j in range(many.shape[0]):
            many[j] = result[pl.ds(jnp.clip(starts[j], 0, total), FMAX)]

    @pl.when(enough)
    def _():
        slots = few.shape[1]
        for j in range(few.shape[0]):
            first = after_of(starts, j, total) - slots if j % 2 else starts[j]
            few[j] = result[pl.ds(jnp.clip(first, 0, total - slots), slots)]


def far_scratch(count, cols, chans):
    return [
        pltpu.VMEM((HIST + count, cols, chans), jnp.bfloat16),
        pltpu.VMEM((3, count, cols + 16, chans), jnp.float32),
    ]


def earlier_rows(kernel, *args):
    far = args[-4]
    return pl.pallas_call(
        kernel,
        out_shape=jax.ShapeDtypeStruct(far.shape, jnp.bfloat16),
        in_specs=[VMEM_SPEC] * len(args),
        out_specs=VMEM_SPEC,
        scratch_shapes=far_scratch(*far.shape),
        compiler_params=pltpu.CompilerParams(vmem_limit_bytes=FAR_VMEM_BYTES),
    )(*args)


def late_rows(starts, recent, far, first, second, partial, weight, gain):
    total, cols, chans = partial.shape
    return pl.pallas_call(
        late_kernel,
        out_shape=[
            jax.ShapeDtypeStruct((starts.shape[0], slots, cols, chans), jnp.bfloat16)
            for slots in (FMAX - 1, FMAX)
        ],
        in_specs=[SMEM_SPEC] + [VMEM_SPEC] * 7,
        out_specs=[VMEM_SPEC] * 2,
        scratch_shapes=far_scratch(*far.shape)
        + [pltpu.VMEM((total + FMAX, cols, chans), jnp.bfloat16)],
        compiler_params=pltpu.CompilerParams(vmem_limit_bytes=FAR_VMEM_BYTES),
    )(starts, recent, far, first, second, partial, weight, gain)


def unpack_kernel(total, starts, arrived, other, out):
    slots = arrived.shape[1]
    core = lax.axis_index("core")
    group = lax.axis_index("tc") * lax.axis_size("core") + core
    start = starts[group]
    after = after_of(starts, group, total)
    length = after - start
    held = start
    if slots < FMAX:
        held = jnp.clip(jnp.where(core == 1, after - slots, start), 0, total - slots)
    for k in range(FMAX):
        slot = start + k - held
        inside = jnp.logical_and(slot >= 0, slot < slots)

        @pl.when(jnp.logical_and(k < length, inside))
        def _():
            out[k] = arrived[:, jnp.clip(slot, 0, slots - 1)]

        @pl.when(jnp.logical_and(k < length, jnp.logical_not(inside)))
        def _():
            out[k] = other[:, 0]

        @pl.when(k >= length)
        def _():
            out[k] = jnp.zeros(out.shape[1:], out.dtype)


def unpack(total, starts, arrived, other):
    rows, _, cols, chans = arrived.shape
    return pl.pallas_call(
        functools.partial(unpack_kernel, total),
        out_shape=jax.ShapeDtypeStruct((FMAX, rows, cols, chans), arrived.dtype),
        in_specs=[SMEM_SPEC, VMEM_SPEC, VMEM_SPEC],
        out_specs=VMEM_SPEC,
        compiler_params=pltpu.CompilerParams(vmem_limit_bytes=UNPACK_VMEM_BYTES),
    )(starts, arrived, other)


def regroup(packed):
    return lax.all_to_all(packed, ("tc", "core"), split_axis=0, concat_axis=0, tiled=True)


def pick_kernel(total, starts, arrived, sent):
    slots = arrived.shape[1]
    core = lax.axis_index("core")
    group = lax.axis_index("tc") * lax.axis_size("core")
    held = after_of(starts, group + 1, total) - starts[group]
    wanted = jnp.where(core == 0, held - slots - 1, 2 * slots - held)
    sent[:, 0] = arrived[:, jnp.clip(wanted, 0, slots - 1)]


def pick(total, starts, arrived):
    rows, _, cols, chans = arrived.shape
    return pl.pallas_call(
        functools.partial(pick_kernel, total),
        out_shape=jax.ShapeDtypeStruct((rows, 1, cols, chans), arrived.dtype),
        in_specs=[SMEM_SPEC, VMEM_SPEC],
        out_specs=VMEM_SPEC,
        compiler_params=pltpu.CompilerParams(vmem_limit_bytes=UNPACK_VMEM_BYTES),
    )(starts, arrived)


def send_few(total, few, many, starts):
    del many
    arrived = regroup(few)
    other = lax.ppermute(pick(total, starts, arrived), "core", [(0, 1), (1, 0)])
    return unpack(total, starts, arrived, other)


def send_many(total, few, many, starts):
    del few
    arrived = regroup(many)
    return unpack(total, starts, arrived, arrived[:, :1])


def on_device(latent, group_start, norm_gain, conv_weight, conv_bias):
    total = latent.shape[0]
    own = latent[:, 0]
    rows = lax.axis_size("ha") * lax.axis_size("tc") * lax.axis_size("core")
    gain = norm_gain.reshape(1, -1)
    bias = conv_bias.reshape(1, -1)
    pairs = [(r, (r + 1) % rows if r % 2 else (r - 1) % rows) for r in range(rows)]
    cuts = (0, total * 3 // 8, total * 3 // 4, total)
    parts = [own[begin:end] for begin, end in zip(cuts, cuts[1:])]
    parts[0], own = lax.optimization_barrier((parts[0], own))
    parts[1:] = [own[begin:end] for begin, end in zip(cuts[1:], cuts[2:])]
    fars = [lax.ppermute(part, ("ha", "tc", "core"), pairs) for part in parts]
    twin = lax.ppermute(own, "core", [(0, 1), (1, 0)])
    partial, fits = near_rows(group_start, own, twin, conv_weight, gain, bias)
    first = earlier_rows(first_kernel, fars[0], partial, conv_weight, gain)
    second = earlier_rows(second_kernel, fars[0], fars[1], partial, conv_weight, gain)
    few, many = late_rows(
        group_start, fars[1], fars[2], first, second, partial, conv_weight, gain
    )
    return lax.switch(
        fits[0],
        [functools.partial(send_many, total), functools.partial(send_few, total)],
        few, many, group_start,
    )


def solution(mesh):
    devices = mesh.devices
    fine = Mesh(
        devices.reshape(devices.shape[0], devices.shape[1] // 2, 2), ("ha", "tc", "core")
    )
    placed = (P(None, ("ha", "tc", "core"), None, None), P(), P(), P(), P())
    return jax.shard_map(
        on_device,
        mesh=fine,
        in_specs=placed,
        out_specs=P(("tc", "core"), "ha", None, None),
        check_vma=False,
    )
```

```python
import functools

import jax
import jax.numpy as jnp
from jax import lax
from jax.experimental import pallas as pl
from jax.experimental.pallas import tpu as pltpu
from jax.sharding import Mesh, PartitionSpec as P

FMAX = 4
HIST = 2
STEP = 8
NEAR_VMEM_BYTES = 14 * 2**20
FAR_VMEM_BYTES = 20 * 2**20
UNPACK_VMEM_BYTES = 8 * 2**20
SMEM_SPEC = pl.BlockSpec(memory_space=pltpu.SMEM)
VMEM_SPEC = pl.BlockSpec(memory_space=pltpu.VMEM)
HBM_SPEC = pl.BlockSpec(memory_space=pltpu.HBM)


def activate(raw, gain):
    wide = raw.astype(jnp.float32)
    power = jnp.mean(wide * wide, axis=-1, keepdims=True)
    half = wide * lax.rsqrt(power + 1e-06) * (0.5 * gain)
    return (half + half * jnp.tanh(half)).astype(jnp.bfloat16)


def taps_of(weight, row_taps):
    return jnp.concatenate(
        [
            jnp.concatenate([weight[a, b, e] for e in range(3)], axis=1)
            for b in row_taps
            for a in range(3)
        ],
        axis=0,
    )


def convolve(acts, first, count, weight, row_taps, sums):
    cols, chans = acts[0].shape[1:]
    lhs = jnp.concatenate(
        [
            act[pl.ds(first + a, count)].reshape(count * cols, chans)
            for act in acts
            for a in range(3)
        ],
        axis=1,
    )
    part = jnp.dot(lhs, taps_of(weight, row_taps), preferred_element_type=jnp.float32)
    for e in range(3):
        sums[e, pl.ds(0, count), 8 : cols + 8, :] = part[:, e * chans : (e + 1) * chans].reshape(
            count, cols, chans
        )
    return (
        sums[0, pl.ds(0, count), 7 : cols + 7, :]
        + sums[1, pl.ds(0, count), 8 : cols + 8, :]
        + sums[2, pl.ds(0, count), 9 : cols + 9, :]
    )


def clear_sides(sums, cols):
    shape = (sums.shape[1], 1, sums.shape[3])
    sums[0, :, 7:8, :] = jnp.zeros(shape, jnp.float32)
    sums[2, :, cols + 8 : cols + 9, :] = jnp.zeros(shape, jnp.float32)


def near_kernel(
    starts, own, twin, weight, gain, bias, partial, fits, own_act, twin_act, sums
):
    total, cols, _ = own.shape
    core = lax.axis_index("core")
    fits[0] = few_suffice(starts, total).astype(jnp.int32)
    clear_sides(sums, cols)
    for act in (own_act, twin_act):
        act[pl.ds(0, HIST)] = jnp.zeros((HIST,) + act.shape[1:], act.dtype)

    def prepare(i, carry):
        frames = pl.ds(i * STEP, STEP)
        later = pl.ds(i * STEP + HIST, STEP)
        own_act[later] = activate(own[frames], gain[...])
        twin_act[later] = activate(twin[frames], gain[...])
        return carry

    lax.fori_loop(0, total // STEP, prepare, 0)

    def step(i, carry):
        frames = pl.ds(i * STEP, STEP)
        convolved = convolve(
            (own_act, twin_act), i * STEP, STEP, weight, (1, 2 * (1 - core)), sums
        )
        partial[frames] = own[frames].astype(jnp.float32) + convolved + bias[...]
        return carry

    lax.fori_loop(0, total // STEP, step, 0)


def near_rows(starts, own, twin, weight, gain, bias):
    total, cols, chans = own.shape
    return pl.pallas_call(
        near_kernel,
        out_shape=[
            jax.ShapeDtypeStruct(own.shape, jnp.float32),
            jax.ShapeDtypeStruct((1,), jnp.int32),
        ],
        in_specs=[SMEM_SPEC] + [VMEM_SPEC] * 5,
        out_specs=[VMEM_SPEC, SMEM_SPEC],
        scratch_shapes=[
            pltpu.VMEM((HIST + total, cols, chans), jnp.bfloat16),
            pltpu.VMEM((HIST + total, cols, chans), jnp.bfloat16),
            pltpu.VMEM((3, STEP, cols + 16, chans), jnp.float32),
        ],
        compiler_params=pltpu.CompilerParams(vmem_limit_bytes=NEAR_VMEM_BYTES),
    )(starts, own, twin, weight, gain, bias)


def far_frames(begin, far, recent, partial, weight, gain, act, sums):
    count, cols, chans = far.shape
    core = lax.axis_index("core")
    row = lax.axis_index("ha") * lax.axis_size("tc") + lax.axis_index("tc")
    row = row * lax.axis_size("core") + core
    rows = lax.axis_size("ha") * lax.axis_size("tc") * lax.axis_size("core")
    clear_sides(sums, cols)
    if recent is None:
        act[pl.ds(0, HIST)] = jnp.zeros((HIST, cols, chans), act.dtype)
    else:
        act[pl.ds(0, HIST)] = activate(recent[pl.ds(recent.shape[0] - HIST, HIST)], gain[...])
    act[pl.ds(HIST, count)] = activate(far[...], gain[...])

    @pl.when(jnp.logical_or(row == 0, row == rows - 1))
    def _():
        act[...] = jnp.zeros(act.shape, act.dtype)

    convolved = convolve((act,), 0, count, weight, (2 * core,), sums)
    return (partial[pl.ds(begin, count)] + convolved).astype(jnp.bfloat16)


def early_kernel(far, partial, weight, gain, out, act, sums):
    out[...] = far_frames(0, far, None, partial, weight, gain, act, sums)


def after_of(starts, group, total):
    groups = starts.shape[0]
    return jnp.where(group + 1 < groups, starts[jnp.minimum(group + 1, groups - 1)], total)


def few_suffice(starts, total):
    most = functools.reduce(
        jnp.maximum,
        [after_of(starts, j + 1, total) - starts[j] for j in range(0, starts.shape[0], 2)],
    )
    return most <= 2 * (FMAX - 1)


def late_kernel(
    starts, recent, far, early, partial, weight, gain, few, many, act, sums, result
):
    cut = early.shape[0]
    count, cols, chans = far.shape
    result[pl.ds(0, cut)] = early[...]
    result[pl.ds(cut + count, FMAX)] = jnp.zeros((FMAX, cols, chans), result.dtype)
    result[pl.ds(cut, count)] = far_frames(
        cut, far, recent, partial, weight, gain, act, sums
    )
    total = cut + count
    enough = few_suffice(starts, total)

    @pl.when(jnp.logical_not(enough))
    def _():
        for j in range(many.shape[0]):
            many[j] = result[pl.ds(jnp.clip(starts[j], 0, total), FMAX)]

    @pl.when(enough)
    def _():
        slots = few.shape[1]
        for j in range(few.shape[0]):
            first = after_of(starts, j, total) - slots if j % 2 else starts[j]
            few[j] = result[pl.ds(jnp.clip(first, 0, total - slots), slots)]


def far_scratch(count, cols, chans):
    return [
        pltpu.VMEM((HIST + count, cols, chans), jnp.bfloat16),
        pltpu.VMEM((3, count, cols + 16, chans), jnp.float32),
    ]


def early_rows(far, partial, weight, gain):
    return pl.pallas_call(
        early_kernel,
        out_shape=jax.ShapeDtypeStruct(far.shape, jnp.bfloat16),
        in_specs=[VMEM_SPEC] * 4,
        out_specs=VMEM_SPEC,
        scratch_shapes=far_scratch(*far.shape),
        compiler_params=pltpu.CompilerParams(vmem_limit_bytes=FAR_VMEM_BYTES),
    )(far, partial, weight, gain)


def late_rows(starts, recent, far, early, partial, weight, gain):
    total, cols, chans = partial.shape
    return pl.pallas_call(
        late_kernel,
        out_shape=[
            jax.ShapeDtypeStruct((starts.shape[0], slots, cols, chans), jnp.bfloat16)
            for slots in (FMAX - 1, FMAX)
        ],
        in_specs=[SMEM_SPEC] + [VMEM_SPEC] * 6,
        out_specs=[VMEM_SPEC] * 2,
        scratch_shapes=far_scratch(*far.shape)
        + [pltpu.VMEM((total + FMAX, cols, chans), jnp.bfloat16)],
        compiler_params=pltpu.CompilerParams(vmem_limit_bytes=FAR_VMEM_BYTES),
    )(starts, recent, far, early, partial, weight, gain)


def unpack_kernel(total, starts, arrived, other, out):
    slots = arrived.shape[1]
    core = lax.axis_index("core")
    group = lax.axis_index("tc") * lax.axis_size("core") + core
    start = starts[group]
    after = after_of(starts, group, total)
    length = after - start
    held = start
    if slots < FMAX:
        held = jnp.clip(jnp.where(core == 1, after - slots, start), 0, total - slots)
    for k in range(FMAX):
        slot = start + k - held
        inside = jnp.logical_and(slot >= 0, slot < slots)

        @pl.when(jnp.logical_and(k < length, inside))
        def _():
            out[k] = arrived[:, jnp.clip(slot, 0, slots - 1)]

        @pl.when(jnp.logical_and(k < length, jnp.logical_not(inside)))
        def _():
            out[k] = other[:, 0]

        @pl.when(k >= length)
        def _():
            out[k] = jnp.zeros(out.shape[1:], out.dtype)


def unpack(total, starts, arrived, other):
    rows, _, cols, chans = arrived.shape
    return pl.pallas_call(
        functools.partial(unpack_kernel, total),
        out_shape=jax.ShapeDtypeStruct((FMAX, rows, cols, chans), arrived.dtype),
        in_specs=[SMEM_SPEC, VMEM_SPEC, VMEM_SPEC],
        out_specs=VMEM_SPEC,
        compiler_params=pltpu.CompilerParams(vmem_limit_bytes=UNPACK_VMEM_BYTES),
    )(starts, arrived, other)


def regroup(packed):
    return lax.all_to_all(packed, ("tc", "core"), split_axis=0, concat_axis=0, tiled=True)


def pick_kernel(total, starts, arrived, sent):
    slots = arrived.shape[1]
    core = lax.axis_index("core")
    group = lax.axis_index("tc") * lax.axis_size("core")
    held = after_of(starts, group + 1, total) - starts[group]
    wanted = jnp.where(core == 0, held - slots - 1, 2 * slots - held)
    sent[:, 0] = arrived[:, jnp.clip(wanted, 0, slots - 1)]


def pick(total, starts, arrived):
    rows, _, cols, chans = arrived.shape
    return pl.pallas_call(
        functools.partial(pick_kernel, total),
        out_shape=jax.ShapeDtypeStruct((rows, 1, cols, chans), arrived.dtype),
        in_specs=[SMEM_SPEC, VMEM_SPEC],
        out_specs=VMEM_SPEC,
        compiler_params=pltpu.CompilerParams(vmem_limit_bytes=UNPACK_VMEM_BYTES),
    )(starts, arrived)


def send_few(total, few, many, starts):
    del many
    arrived = regroup(few)
    other = lax.ppermute(pick(total, starts, arrived), "core", [(0, 1), (1, 0)])
    return unpack(total, starts, arrived, other)


def send_many(total, few, many, starts):
    del few
    arrived = regroup(many)
    return unpack(total, starts, arrived, arrived[:, :1])


def on_device(latent, group_start, norm_gain, conv_weight, conv_bias):
    total = latent.shape[0]
    own = latent[:, 0]
    rows = lax.axis_size("ha") * lax.axis_size("tc") * lax.axis_size("core")
    gain = norm_gain.reshape(1, -1)
    bias = conv_bias.reshape(1, -1)
    pairs = [(r, (r + 1) % rows if r % 2 else (r - 1) % rows) for r in range(rows)]
    cut = total * 5 // 8
    front, own = lax.optimization_barrier((own[:cut], own))
    early_far = lax.ppermute(front, ("ha", "tc", "core"), pairs)
    late_far = lax.ppermute(own[cut:], ("ha", "tc", "core"), pairs)
    twin = lax.ppermute(own, "core", [(0, 1), (1, 0)])
    partial, fits = near_rows(group_start, own, twin, conv_weight, gain, bias)
    early = early_rows(early_far, partial, conv_weight, gain)
    few, many = late_rows(
        group_start, early_far, late_far, early, partial, conv_weight, gain
    )
    return lax.switch(
        fits[0],
        [functools.partial(send_many, total), functools.partial(send_few, total)],
        few, many, group_start,
    )


def solution(mesh):
    devices = mesh.devices
    fine = Mesh(
        devices.reshape(devices.shape[0], devices.shape[1] // 2, 2), ("ha", "tc", "core")
    )
    placed = (P(None, ("ha", "tc", "core"), None, None), P(), P(), P(), P())
    return jax.shard_map(
        on_device,
        mesh=fine,
        in_specs=placed,
        out_specs=P(("tc", "core"), "ha", None, None),
        check_vma=False,
    )
```

```python
import functools

import jax
import jax.numpy as jnp
from jax import lax
from jax.experimental import pallas as pl
from jax.experimental.pallas import tpu as pltpu
from jax.sharding import Mesh, PartitionSpec as P

FMAX = 4
HIST = 2
STEP = 8
NEAR_VMEM_BYTES = 14 * 2**20
FAR_VMEM_BYTES = 20 * 2**20
UNPACK_VMEM_BYTES = 8 * 2**20
SMEM_SPEC = pl.BlockSpec(memory_space=pltpu.SMEM)
VMEM_SPEC = pl.BlockSpec(memory_space=pltpu.VMEM)
HBM_SPEC = pl.BlockSpec(memory_space=pltpu.HBM)


def activate(raw, gain):
    wide = raw.astype(jnp.float32)
    power = jnp.mean(wide * wide, axis=-1, keepdims=True)
    half = wide * lax.rsqrt(power + 1e-06) * (0.5 * gain)
    return (half + half * jnp.tanh(half)).astype(jnp.bfloat16)


def taps_of(weight, row_taps):
    return jnp.concatenate(
        [
            jnp.concatenate([weight[a, b, e] for e in range(3)], axis=1)
            for b in row_taps
            for a in range(3)
        ],
        axis=0,
    )


def convolve(acts, first, count, weight, row_taps, sums):
    cols, chans = acts[0].shape[1:]
    lhs = jnp.concatenate(
        [
            act[pl.ds(first + a, count)].reshape(count * cols, chans)
            for act in acts
            for a in range(3)
        ],
        axis=1,
    )
    part = jnp.dot(lhs, taps_of(weight, row_taps), preferred_element_type=jnp.float32)
    for e in range(3):
        sums[e, pl.ds(0, count), 8 : cols + 8, :] = part[:, e * chans : (e + 1) * chans].reshape(
            count, cols, chans
        )
    return (
        sums[0, pl.ds(0, count), 7 : cols + 7, :]
        + sums[1, pl.ds(0, count), 8 : cols + 8, :]
        + sums[2, pl.ds(0, count), 9 : cols + 9, :]
    )


def clear_sides(sums, cols):
    shape = (sums.shape[1], 1, sums.shape[3])
    sums[0, :, 7:8, :] = jnp.zeros(shape, jnp.float32)
    sums[2, :, cols + 8 : cols + 9, :] = jnp.zeros(shape, jnp.float32)


def near_kernel(
    starts, own, twin, weight, gain, bias, partial, fits, own_act, twin_act, sums
):
    total, cols, _ = own.shape
    core = lax.axis_index("core")
    fits[0] = few_suffice(starts, total).astype(jnp.int32)
    clear_sides(sums, cols)
    for act in (own_act, twin_act):
        act[pl.ds(0, HIST)] = jnp.zeros((HIST,) + act.shape[1:], act.dtype)

    def prepare(i, carry):
        frames = pl.ds(i * STEP, STEP)
        later = pl.ds(i * STEP + HIST, STEP)
        own_act[later] = activate(own[frames], gain[...])
        twin_act[later] = activate(twin[frames], gain[...])
        return carry

    lax.fori_loop(0, total // STEP, prepare, 0)

    def step(i, carry):
        frames = pl.ds(i * STEP, STEP)
        convolved = convolve(
            (own_act, twin_act), i * STEP, STEP, weight, (1, 2 * (1 - core)), sums
        )
        partial[frames] = own[frames].astype(jnp.float32) + convolved + bias[...]
        return carry

    lax.fori_loop(0, total // STEP, step, 0)


def near_rows(starts, own, twin, weight, gain, bias):
    total, cols, chans = own.shape
    return pl.pallas_call(
        near_kernel,
        out_shape=[
            jax.ShapeDtypeStruct(own.shape, jnp.float32),
            jax.ShapeDtypeStruct((1,), jnp.int32),
        ],
        in_specs=[SMEM_SPEC] + [VMEM_SPEC] * 5,
        out_specs=[VMEM_SPEC, SMEM_SPEC],
        scratch_shapes=[
            pltpu.VMEM((HIST + total, cols, chans), jnp.bfloat16),
            pltpu.VMEM((HIST + total, cols, chans), jnp.bfloat16),
            pltpu.VMEM((3, STEP, cols + 16, chans), jnp.float32),
        ],
        compiler_params=pltpu.CompilerParams(vmem_limit_bytes=NEAR_VMEM_BYTES),
    )(starts, own, twin, weight, gain, bias)


def far_frames(begin, far, recent, partial, weight, gain, act, sums):
    count, cols, chans = far.shape
    core = lax.axis_index("core")
    row = lax.axis_index("ha") * lax.axis_size("tc") + lax.axis_index("tc")
    row = row * lax.axis_size("core") + core
    rows = lax.axis_size("ha") * lax.axis_size("tc") * lax.axis_size("core")
    clear_sides(sums, cols)
    if recent is None:
        act[pl.ds(0, HIST)] = jnp.zeros((HIST, cols, chans), act.dtype)
    else:
        act[pl.ds(0, HIST)] = activate(recent[pl.ds(recent.shape[0] - HIST, HIST)], gain[...])
    act[pl.ds(HIST, count)] = activate(far[...], gain[...])

    @pl.when(jnp.logical_or(row == 0, row == rows - 1))
    def _():
        act[...] = jnp.zeros(act.shape, act.dtype)

    convolved = convolve((act,), 0, count, weight, (2 * core,), sums)
    return (partial[pl.ds(begin, count)] + convolved).astype(jnp.bfloat16)


def early_kernel(far, partial, weight, gain, out, act, sums):
    out[...] = far_frames(0, far, None, partial, weight, gain, act, sums)


def after_of(starts, group, total):
    groups = starts.shape[0]
    return jnp.where(group + 1 < groups, starts[jnp.minimum(group + 1, groups - 1)], total)


def few_suffice(starts, total):
    most = functools.reduce(
        jnp.maximum,
        [after_of(starts, j + 1, total) - starts[j] for j in range(0, starts.shape[0], 2)],
    )
    return most <= 2 * (FMAX - 1)


def late_kernel(
    starts, recent, far, early, partial, weight, gain, few, many, act, sums, result
):
    cut = early.shape[0]
    count, cols, chans = far.shape
    result[pl.ds(0, cut)] = early[...]
    result[pl.ds(cut + count, FMAX)] = jnp.zeros((FMAX, cols, chans), result.dtype)
    result[pl.ds(cut, count)] = far_frames(
        cut, far, recent, partial, weight, gain, act, sums
    )
    total = cut + count
    enough = few_suffice(starts, total)

    @pl.when(jnp.logical_not(enough))
    def _():
        for j in range(many.shape[0]):
            many[j] = result[pl.ds(jnp.clip(starts[j], 0, total), FMAX)]

    @pl.when(enough)
    def _():
        slots = few.shape[1]
        for j in range(few.shape[0]):
            first = after_of(starts, j, total) - slots if j % 2 else starts[j]
            few[j] = result[pl.ds(jnp.clip(first, 0, total - slots), slots)]


def far_scratch(count, cols, chans):
    return [
        pltpu.VMEM((HIST + count, cols, chans), jnp.bfloat16),
        pltpu.VMEM((3, count, cols + 16, chans), jnp.float32),
    ]


def early_rows(far, partial, weight, gain):
    return pl.pallas_call(
        early_kernel,
        out_shape=jax.ShapeDtypeStruct(far.shape, jnp.bfloat16),
        in_specs=[VMEM_SPEC] * 4,
        out_specs=VMEM_SPEC,
        scratch_shapes=far_scratch(*far.shape),
        compiler_params=pltpu.CompilerParams(vmem_limit_bytes=FAR_VMEM_BYTES),
    )(far, partial, weight, gain)


def late_rows(starts, recent, far, early, partial, weight, gain):
    total, cols, chans = partial.shape
    return pl.pallas_call(
        late_kernel,
        out_shape=[
            jax.ShapeDtypeStruct((starts.shape[0], slots, cols, chans), jnp.bfloat16)
            for slots in (FMAX - 1, FMAX)
        ],
        in_specs=[SMEM_SPEC] + [VMEM_SPEC] * 6,
        out_specs=[VMEM_SPEC] * 2,
        scratch_shapes=far_scratch(*far.shape)
        + [pltpu.VMEM((total + FMAX, cols, chans), jnp.bfloat16)],
        compiler_params=pltpu.CompilerParams(vmem_limit_bytes=FAR_VMEM_BYTES),
    )(starts, recent, far, early, partial, weight, gain)


def slots_of(starts, total, slots):
    core = lax.axis_index("core")
    group = lax.axis_index("tc") * lax.axis_size("core") + core
    start = starts[group]
    after = after_of(starts, group, total)
    held = start
    if slots < FMAX:
        held = jnp.clip(jnp.where(core == 1, after - slots, start), 0, total - slots)
    found = []
    for k in range(FMAX):
        slot = start + k - held
        inside = jnp.logical_and(slot >= 0, slot < slots)
        found.append((k < after - start, inside, jnp.clip(slot, 0, slots - 1)))
    return found


def unpack_kernel(total, starts, arrived, out, blank, sems):
    found = slots_of(starts, total, arrived.shape[1])
    blank[...] = jnp.zeros(blank.shape, blank.dtype)
    for k, (used, inside, slot) in enumerate(found):

        @pl.when(jnp.logical_and(used, inside))
        def _():
            pltpu.make_async_copy(arrived.at[:, slot], out.at[k], sems.at[k]).start()

        @pl.when(jnp.logical_not(used))
        def _():
            pltpu.make_async_copy(blank, out.at[k], sems.at[k]).start()

    for k, (used, inside, slot) in enumerate(found):

        @pl.when(jnp.logical_or(inside, jnp.logical_not(used)))
        def _():
            pltpu.make_async_copy(blank, out.at[k], sems.at[k]).wait()


def unpack(total, starts, arrived):
    rows, _, cols, chans = arrived.shape
    return pl.pallas_call(
        functools.partial(unpack_kernel, total),
        out_shape=jax.ShapeDtypeStruct((FMAX, rows, cols, chans), arrived.dtype),
        in_specs=[SMEM_SPEC, VMEM_SPEC],
        out_specs=HBM_SPEC,
        scratch_shapes=[
            pltpu.VMEM((rows, cols, chans), arrived.dtype),
            pltpu.SemaphoreType.DMA((FMAX,)),
        ],
        compiler_params=pltpu.CompilerParams(vmem_limit_bytes=UNPACK_VMEM_BYTES),
    )(starts, arrived)


def patch_kernel(total, starts, other, partial, out, sem):
    del partial
    for k, (used, inside, _) in enumerate(slots_of(starts, total, FMAX - 1)):

        @pl.when(jnp.logical_and(used, jnp.logical_not(inside)))
        def _():
            copy = pltpu.make_async_copy(other.at[:, 0], out.at[k], sem)
            copy.start()
            copy.wait()


def patch(total, starts, other, partial):
    return pl.pallas_call(
        functools.partial(patch_kernel, total),
        out_shape=jax.ShapeDtypeStruct(partial.shape, partial.dtype),
        in_specs=[SMEM_SPEC, VMEM_SPEC, HBM_SPEC],
        out_specs=HBM_SPEC,
        scratch_shapes=[pltpu.SemaphoreType.DMA],
        input_output_aliases={2: 0},
        compiler_params=pltpu.CompilerParams(vmem_limit_bytes=UNPACK_VMEM_BYTES),
    )(starts, other, partial)


def regroup(packed):
    return lax.all_to_all(packed, ("tc", "core"), split_axis=0, concat_axis=0, tiled=True)


def pick_kernel(total, starts, arrived, sent):
    slots = arrived.shape[1]
    core = lax.axis_index("core")
    group = lax.axis_index("tc") * lax.axis_size("core")
    held = after_of(starts, group + 1, total) - starts[group]
    wanted = jnp.where(core == 0, held - slots - 1, 2 * slots - held)
    sent[:, 0] = arrived[:, jnp.clip(wanted, 0, slots - 1)]


def pick(total, starts, arrived):
    rows, _, cols, chans = arrived.shape
    return pl.pallas_call(
        functools.partial(pick_kernel, total),
        out_shape=jax.ShapeDtypeStruct((rows, 1, cols, chans), arrived.dtype),
        in_specs=[SMEM_SPEC, VMEM_SPEC],
        out_specs=VMEM_SPEC,
        compiler_params=pltpu.CompilerParams(vmem_limit_bytes=UNPACK_VMEM_BYTES),
    )(starts, arrived)


def send_few(total, few, many, starts):
    del many
    arrived = regroup(few)
    other = lax.ppermute(pick(total, starts, arrived), "core", [(0, 1), (1, 0)])
    return patch(total, starts, other, unpack(total, starts, arrived))


def send_many(total, few, many, starts):
    del few
    arrived = regroup(many)
    return unpack(total, starts, arrived)


def on_device(latent, group_start, norm_gain, conv_weight, conv_bias):
    total = latent.shape[0]
    own = latent[:, 0]
    rows = lax.axis_size("ha") * lax.axis_size("tc") * lax.axis_size("core")
    gain = norm_gain.reshape(1, -1)
    bias = conv_bias.reshape(1, -1)
    pairs = [(r, (r + 1) % rows if r % 2 else (r - 1) % rows) for r in range(rows)]
    cut = total * 5 // 8
    front, own = lax.optimization_barrier((own[:cut], own))
    early_far = lax.ppermute(front, ("ha", "tc", "core"), pairs)
    late_far = lax.ppermute(own[cut:], ("ha", "tc", "core"), pairs)
    twin = lax.ppermute(own, "core", [(0, 1), (1, 0)])
    partial, fits = near_rows(group_start, own, twin, conv_weight, gain, bias)
    early = early_rows(early_far, partial, conv_weight, gain)
    few, many = late_rows(
        group_start, early_far, late_far, early, partial, conv_weight, gain
    )
    return lax.switch(
        fits[0],
        [functools.partial(send_many, total), functools.partial(send_few, total)],
        few, many, group_start,
    )


def solution(mesh):
    devices = mesh.devices
    fine = Mesh(
        devices.reshape(devices.shape[0], devices.shape[1] // 2, 2), ("ha", "tc", "core")
    )
    placed = (P(None, ("ha", "tc", "core"), None, None), P(), P(), P(), P())
    return jax.shard_map(
        on_device,
        mesh=fine,
        in_specs=placed,
        out_specs=P(("tc", "core"), "ha", None, None),
        check_vma=False,
    )
```

```python
import functools

import jax
import jax.numpy as jnp
from jax import lax
from jax.experimental import pallas as pl
from jax.experimental.pallas import tpu as pltpu
from jax.sharding import Mesh, PartitionSpec as P

FMAX = 4
HIST = 2
STEP = 8
NEAR_VMEM_BYTES = 14 * 2**20
FAR_VMEM_BYTES = 20 * 2**20
UNPACK_VMEM_BYTES = 8 * 2**20
SMEM_SPEC = pl.BlockSpec(memory_space=pltpu.SMEM)
VMEM_SPEC = pl.BlockSpec(memory_space=pltpu.VMEM)
HBM_SPEC = pl.BlockSpec(memory_space=pltpu.HBM)


def activate(raw, gain):
    wide = raw.astype(jnp.float32)
    power = jnp.mean(wide * wide, axis=-1, keepdims=True)
    half = wide * lax.rsqrt(power + 1e-06) * (0.5 * gain)
    return (half + half * jnp.tanh(half)).astype(jnp.bfloat16)


def taps_of(weight, row_taps):
    return jnp.concatenate(
        [
            jnp.concatenate([weight[a, b, e] for e in range(3)], axis=1)
            for b in row_taps
            for a in range(3)
        ],
        axis=0,
    )


def convolve(acts, first, count, weight, row_taps, sums):
    cols, chans = acts[0].shape[1:]
    lhs = jnp.concatenate(
        [
            act[pl.ds(first + a, count)].reshape(count * cols, chans)
            for act in acts
            for a in range(3)
        ],
        axis=1,
    )
    part = jnp.dot(lhs, taps_of(weight, row_taps), preferred_element_type=jnp.float32)
    left, middle, right = (
        part[:, e * chans : (e + 1) * chans].reshape(count, cols, chans) for e in range(3)
    )
    sums[0, pl.ds(0, count), 8 : cols + 8, :] = left
    sums[1, pl.ds(0, count), 8 : cols + 8, :] = right
    return (
        sums[0, pl.ds(0, count), 7 : cols + 7, :]
        + middle
        + sums[1, pl.ds(0, count), 9 : cols + 9, :]
    )


def clear_sides(sums, cols):
    shape = (sums.shape[1], 1, sums.shape[3])
    sums[0, :, 7:8, :] = jnp.zeros(shape, jnp.float32)
    sums[1, :, cols + 8 : cols + 9, :] = jnp.zeros(shape, jnp.float32)


def near_kernel(
    starts, own, twin, weight, gain, bias, partial, fits, own_act, twin_act, sums
):
    total, cols, _ = own.shape
    core = lax.axis_index("core")
    fits[0] = few_suffice(starts, total).astype(jnp.int32)
    clear_sides(sums, cols)
    for act in (own_act, twin_act):
        act[pl.ds(0, HIST)] = jnp.zeros((HIST,) + act.shape[1:], act.dtype)

    def prepare(i, carry):
        frames = pl.ds(i * STEP, STEP)
        later = pl.ds(i * STEP + HIST, STEP)
        own_act[later] = activate(own[frames], gain[...])
        twin_act[later] = activate(twin[frames], gain[...])
        return carry

    lax.fori_loop(0, total // STEP, prepare, 0)

    def step(i, carry):
        frames = pl.ds(i * STEP, STEP)
        convolved = convolve(
            (own_act, twin_act), i * STEP, STEP, weight, (1, 2 * (1 - core)), sums
        )
        partial[frames] = own[frames].astype(jnp.float32) + convolved + bias[...]
        return carry

    lax.fori_loop(0, total // STEP, step, 0)


def near_rows(starts, own, twin, weight, gain, bias):
    total, cols, chans = own.shape
    return pl.pallas_call(
        near_kernel,
        out_shape=[
            jax.ShapeDtypeStruct(own.shape, jnp.float32),
            jax.ShapeDtypeStruct((1,), jnp.int32),
        ],
        in_specs=[SMEM_SPEC] + [VMEM_SPEC] * 5,
        out_specs=[VMEM_SPEC, SMEM_SPEC],
        scratch_shapes=[
            pltpu.VMEM((HIST + total, cols, chans), jnp.bfloat16),
            pltpu.VMEM((HIST + total, cols, chans), jnp.bfloat16),
            pltpu.VMEM((2, STEP, cols + 16, chans), jnp.float32),
        ],
        compiler_params=pltpu.CompilerParams(vmem_limit_bytes=NEAR_VMEM_BYTES),
    )(starts, own, twin, weight, gain, bias)


def far_frames(begin, far, recent, partial, weight, gain, act, sums):
    count, cols, chans = far.shape
    core = lax.axis_index("core")
    row = lax.axis_index("ha") * lax.axis_size("tc") + lax.axis_index("tc")
    row = row * lax.axis_size("core") + core
    rows = lax.axis_size("ha") * lax.axis_size("tc") * lax.axis_size("core")
    clear_sides(sums, cols)
    if recent is None:
        act[pl.ds(0, HIST)] = jnp.zeros((HIST, cols, chans), act.dtype)
    else:
        act[pl.ds(0, HIST)] = activate(recent[pl.ds(recent.shape[0] - HIST, HIST)], gain[...])
    act[pl.ds(HIST, count)] = activate(far[...], gain[...])

    @pl.when(jnp.logical_or(row == 0, row == rows - 1))
    def _():
        act[...] = jnp.zeros(act.shape, act.dtype)

    convolved = convolve((act,), 0, count, weight, (2 * core,), sums)
    return (partial[pl.ds(begin, count)] + convolved).astype(jnp.bfloat16)


def early_kernel(far, partial, weight, gain, out, act, sums):
    out[...] = far_frames(0, far, None, partial, weight, gain, act, sums)


def after_of(starts, group, total):
    groups = starts.shape[0]
    return jnp.where(group + 1 < groups, starts[jnp.minimum(group + 1, groups - 1)], total)


def few_suffice(starts, total):
    most = functools.reduce(
        jnp.maximum,
        [after_of(starts, j + 1, total) - starts[j] for j in range(0, starts.shape[0], 2)],
    )
    return most <= 2 * (FMAX - 1)


def late_kernel(
    starts, recent, far, early, partial, weight, gain, few, many, act, sums, result
):
    cut = early.shape[0]
    count, cols, chans = far.shape
    result[pl.ds(0, cut)] = early[...]
    result[pl.ds(cut + count, FMAX)] = jnp.zeros((FMAX, cols, chans), result.dtype)
    result[pl.ds(cut, count)] = far_frames(
        cut, far, recent, partial, weight, gain, act, sums
    )
    total = cut + count
    enough = few_suffice(starts, total)

    @pl.when(jnp.logical_not(enough))
    def _():
        for j in range(many.shape[0]):
            many[j] = result[pl.ds(jnp.clip(starts[j], 0, total), FMAX)]

    @pl.when(enough)
    def _():
        slots = few.shape[1]
        for j in range(few.shape[0]):
            first = after_of(starts, j, total) - slots if j % 2 else starts[j]
            few[j] = result[pl.ds(jnp.clip(first, 0, total - slots), slots)]


def far_scratch(count, cols, chans):
    return [
        pltpu.VMEM((HIST + count, cols, chans), jnp.bfloat16),
        pltpu.VMEM((2, count, cols + 16, chans), jnp.float32),
    ]


def early_rows(far, partial, weight, gain):
    return pl.pallas_call(
        early_kernel,
        out_shape=jax.ShapeDtypeStruct(far.shape, jnp.bfloat16),
        in_specs=[VMEM_SPEC] * 4,
        out_specs=VMEM_SPEC,
        scratch_shapes=far_scratch(*far.shape),
        compiler_params=pltpu.CompilerParams(vmem_limit_bytes=FAR_VMEM_BYTES),
    )(far, partial, weight, gain)


def late_rows(starts, recent, far, early, partial, weight, gain):
    total, cols, chans = partial.shape
    return pl.pallas_call(
        late_kernel,
        out_shape=[
            jax.ShapeDtypeStruct((starts.shape[0], slots, cols, chans), jnp.bfloat16)
            for slots in (FMAX - 1, FMAX)
        ],
        in_specs=[SMEM_SPEC] + [VMEM_SPEC] * 6,
        out_specs=[VMEM_SPEC] * 2,
        scratch_shapes=far_scratch(*far.shape)
        + [pltpu.VMEM((total + FMAX, cols, chans), jnp.bfloat16)],
        compiler_params=pltpu.CompilerParams(vmem_limit_bytes=FAR_VMEM_BYTES),
    )(starts, recent, far, early, partial, weight, gain)


def slots_of(starts, total, slots):
    core = lax.axis_index("core")
    group = lax.axis_index("tc") * lax.axis_size("core") + core
    start = starts[group]
    after = after_of(starts, group, total)
    held = start
    if slots < FMAX:
        held = jnp.clip(jnp.where(core == 1, after - slots, start), 0, total - slots)
    found = []
    for k in range(FMAX):
        slot = start + k - held
        inside = jnp.logical_and(slot >= 0, slot < slots)
        found.append((k < after - start, inside, jnp.clip(slot, 0, slots - 1)))
    return found


def unpack_kernel(total, starts, arrived, out, blank, sems):
    found = slots_of(starts, total, arrived.shape[1])
    blank[...] = jnp.zeros(blank.shape, blank.dtype)
    for k, (used, inside, slot) in enumerate(found):

        @pl.when(jnp.logical_and(used, inside))
        def _():
            pltpu.make_async_copy(arrived.at[:, slot], out.at[k], sems.at[k]).start()

        @pl.when(jnp.logical_not(used))
        def _():
            pltpu.make_async_copy(blank, out.at[k], sems.at[k]).start()

    for k, (used, inside, slot) in enumerate(found):

        @pl.when(jnp.logical_or(inside, jnp.logical_not(used)))
        def _():
            pltpu.make_async_copy(blank, out.at[k], sems.at[k]).wait()


def unpack(total, starts, arrived):
    rows, _, cols, chans = arrived.shape
    return pl.pallas_call(
        functools.partial(unpack_kernel, total),
        out_shape=jax.ShapeDtypeStruct((FMAX, rows, cols, chans), arrived.dtype),
        in_specs=[SMEM_SPEC, VMEM_SPEC],
        out_specs=HBM_SPEC,
        scratch_shapes=[
            pltpu.VMEM((rows, cols, chans), arrived.dtype),
            pltpu.SemaphoreType.DMA((FMAX,)),
        ],
        compiler_params=pltpu.CompilerParams(vmem_limit_bytes=UNPACK_VMEM_BYTES),
    )(starts, arrived)


def patch_kernel(total, starts, other, partial, out, sem):
    del partial
    for k, (used, inside, _) in enumerate(slots_of(starts, total, FMAX - 1)):

        @pl.when(jnp.logical_and(used, jnp.logical_not(inside)))
        def _():
            copy = pltpu.make_async_copy(other.at[:, 0], out.at[k], sem)
            copy.start()
            copy.wait()


def patch(total, starts, other, partial):
    return pl.pallas_call(
        functools.partial(patch_kernel, total),
        out_shape=jax.ShapeDtypeStruct(partial.shape, partial.dtype),
        in_specs=[SMEM_SPEC, VMEM_SPEC, HBM_SPEC],
        out_specs=HBM_SPEC,
        scratch_shapes=[pltpu.SemaphoreType.DMA],
        input_output_aliases={2: 0},
        compiler_params=pltpu.CompilerParams(vmem_limit_bytes=UNPACK_VMEM_BYTES),
    )(starts, other, partial)


def regroup(packed):
    return lax.all_to_all(packed, ("tc", "core"), split_axis=0, concat_axis=0, tiled=True)


def pick_kernel(total, starts, arrived, sent):
    slots = arrived.shape[1]
    core = lax.axis_index("core")
    group = lax.axis_index("tc") * lax.axis_size("core")
    held = after_of(starts, group + 1, total) - starts[group]
    wanted = jnp.where(core == 0, held - slots - 1, 2 * slots - held)
    sent[:, 0] = arrived[:, jnp.clip(wanted, 0, slots - 1)]


def pick(total, starts, arrived):
    rows, _, cols, chans = arrived.shape
    return pl.pallas_call(
        functools.partial(pick_kernel, total),
        out_shape=jax.ShapeDtypeStruct((rows, 1, cols, chans), arrived.dtype),
        in_specs=[SMEM_SPEC, VMEM_SPEC],
        out_specs=VMEM_SPEC,
        compiler_params=pltpu.CompilerParams(vmem_limit_bytes=UNPACK_VMEM_BYTES),
    )(starts, arrived)


def send_few(total, few, many, starts):
    del many
    arrived = regroup(few)
    other = lax.ppermute(pick(total, starts, arrived), "core", [(0, 1), (1, 0)])
    return patch(total, starts, other, unpack(total, starts, arrived))


def send_many(total, few, many, starts):
    del few
    arrived = regroup(many)
    return unpack(total, starts, arrived)


def on_device(latent, group_start, norm_gain, conv_weight, conv_bias):
    total = latent.shape[0]
    own = latent[:, 0]
    rows = lax.axis_size("ha") * lax.axis_size("tc") * lax.axis_size("core")
    gain = norm_gain.reshape(1, -1)
    bias = conv_bias.reshape(1, -1)
    pairs = [(r, (r + 1) % rows if r % 2 else (r - 1) % rows) for r in range(rows)]
    cut = total * 5 // 8
    front, own = lax.optimization_barrier((own[:cut], own))
    early_far = lax.ppermute(front, ("ha", "tc", "core"), pairs)
    late_far = lax.ppermute(own[cut:], ("ha", "tc", "core"), pairs)
    twin = lax.ppermute(own, "core", [(0, 1), (1, 0)])
    partial, fits = near_rows(group_start, own, twin, conv_weight, gain, bias)
    early = early_rows(early_far, partial, conv_weight, gain)
    few, many = late_rows(
        group_start, early_far, late_far, early, partial, conv_weight, gain
    )
    return lax.switch(
        fits[0],
        [functools.partial(send_many, total), functools.partial(send_few, total)],
        few, many, group_start,
    )


def solution(mesh):
    devices = mesh.devices
    fine = Mesh(
        devices.reshape(devices.shape[0], devices.shape[1] // 2, 2), ("ha", "tc", "core")
    )
    placed = (P(None, ("ha", "tc", "core"), None, None), P(), P(), P(), P())
    return jax.shard_map(
        on_device,
        mesh=fine,
        in_specs=placed,
        out_specs=P(("tc", "core"), "ha", None, None),
        check_vma=False,
    )
```
